32 devices in a mesh: rep: 2 (over y), date: 4 (over x, core), tile: 4 (over z).
Axes of the slice: x: 2, y: 2, z: 4, core: 2. Of those that a mesh axis runs over, the one named last changes fastest.
Arguments:
- tokens: bfloat16 [32, 128, 1280], P(('rep', 'tile'), 'date'), parts along dimension 0, may hold values from -6 to 6
- cotangent: bfloat16 [32, 128, 1280], P(('rep', 'tile'), 'date'), parts along dimension 0, may hold values from -6 to 6
- valid: int32 [32, 128], P(('rep', 'tile')), parts along dimension 0, may hold values from 0 to 1, as said below
- visible: int32 [32], P(('rep', 'tile')), parts along dimension 0, may hold values from 0 to 255
- live: int32 [8], P('rep'), parts along dimension 0, may hold values from 1 to 4, as said below
- pos_table: bfloat16 [256, 1280], replicated, may hold values from -6 to 6
- norm_gain: float32 [1280], replicated, may hold values from 0.5 to 1.5
- norm_bias: float32 [1280], replicated, may hold values from -2 to 2
- w_qkv: bfloat16 [1280, 3840], P('tile'), may hold values from -0.1118034 to 0.1118034
Outputs:
- attended: bfloat16 [32, 128, 1280], P(('rep', 'tile'), 'date'), parts along dimension 0
- grad_tokens: bfloat16 [32, 128, 1280], P(('rep', 'tile'), 'date'), parts along dimension 0
- grad_norm: float32 [4, 1280], P('rep'), parts along dimension 0
The draws below stay inside these ranges and needn't reach their ends.
There are 2 independent parts, one for each index of `rep`. The reference program is written for one: setup_inputs(seed, part) draws one part's arguments, and reference() takes and returns one part's arrays. A program takes and returns all parts, laid end to end along the dimension named above; an argument that names none is the same for every part. Nothing has to cross between parts.
Inputs may be any that keep to these rules, and one draw needn't show every extreme that they name: `valid`: every patch slot has data on at least one date. Whenever a tile owner holds 4 live blocks, the next owner on the tile cycle (index plus one, the last followed by the first) holds at most 2 and the previous owner fewer than 4.
All inputs are finite; a program needn't handle non-finite values.
Results may differ from the reference program's by a relative error of at most 0.04.
Values may be sent and summed in bfloat16 or wider, within the bound.
No kernel may reach another device: no remote copies, remote signals or barrier semaphores. Data moves between devices by JAX's collectives and lax.ppermute only.
A program may use at most 64 MiB of HBM per device.

```python
import jax
import jax.numpy as jnp
from jax import lax

D = 1280
HEAD_DIM = 80
HEADS = 16
DG = 32
POSN = 256
PB = 4
BLOCK_ROWS = 32
CHAN = 1280
PS = 4
PATCHES = 16
DATES = 128
N_TILE = 4


def planted_structure(key):
    key_dir, key_head, key_place, key_power = jax.random.split(key, 4)
    sign_list = jnp.where(jnp.arange(D) < D // 2, 1.0, -1.0).astype(jnp.float32)
    direction = jax.random.permutation(key_dir, sign_list)
    head_pick = jax.random.permutation(key_head, HEADS)[:2]
    plant_count = max(2, POSN // 32)
    places = jax.random.permutation(key_place, POSN)[:plant_count]
    powers = jax.random.uniform(key_power, (plant_count,), minval=1.5, maxval=4.0)
    return (direction, head_pick, places, powers)


def draw_pos_table(key, part):
    direction, head_pick, places, powers = planted_structure(key)
    key = jax.random.fold_in(key, 21)
    noise_part = jnp.clip(0.5 * jax.random.normal(key, (POSN, D)), -2.0, 2.0)
    row_power = jnp.zeros((POSN,), jnp.float32).at[places].set(powers)
    return (noise_part + row_power[:, None] * direction[None, :]).astype(jnp.bfloat16)


def draw_w_qkv(key, part):
    direction, head_pick, places, powers = planted_structure(key)
    key = jax.random.fold_in(key, 22)
    noise_part = jnp.clip(jax.random.normal(key, (D, 3 * CHAN)), -3.5, 3.5)
    head_power = jnp.zeros((HEADS,), jnp.float32).at[head_pick[0]].set(0.18).at[head_pick[1]].set(0.13)
    column = jnp.arange(3 * CHAN, dtype=jnp.int32)
    column_head = column % CHAN // HEAD_DIM
    column_power = jnp.where(column < 2 * CHAN, head_power[column_head], 0.0)
    return ((noise_part + direction[:, None] * column_power[None, :]) * D ** (-0.5)).astype(jnp.bfloat16)


def draw_live(key, part):
    key = jax.random.fold_in(key, 7)
    key_one, key_two, key_three = jax.random.split(key, 3)
    coin_bits = jax.random.randint(key_one, (N_TILE,), 0, 2)
    coin_bits = coin_bits.at[0].set(1).at[1].set(0)
    is_heavy = (coin_bits == 1) & (jnp.roll(coin_bits, -1) == 0)
    receiver = jnp.roll(is_heavy, 1)
    light_counts = jax.random.randint(key_two, (N_TILE,), 1, PB - 1)
    middle = jax.random.randint(key_three, (N_TILE,), 1, PB)
    counts = jnp.where(is_heavy, PB, jnp.where(receiver, light_counts, middle))
    return counts.at[1].set(1).astype(jnp.int32)


def draw_valid(key, part):
    key = jax.random.fold_in(key, 13)
    key_one, key_two = jax.random.split(key, 2)
    coin_bits = jax.random.randint(key_one, (PATCHES, DATES), 0, 10) < 7
    forced = jax.random.randint(key_two, (PATCHES,), 0, DATES)
    chosen = jnp.arange(DATES, dtype=jnp.int32)[None, :] == forced[:, None]
    return (coin_bits | chosen).astype(jnp.int32)


def touch_ends(values, key, low, top_value):
    spot = [jax.random.randint(jax.random.fold_in(key, axis), (), 0, length) for axis, length in enumerate(values.shape)]
    main_axis = values.shape.index(max(values.shape))
    beside = spot[:main_axis] + [(spot[main_axis] + 1) % values.shape[main_axis]] + spot[main_axis + 1:]
    return values.at[tuple(spot)].set(low).at[tuple(beside)].set(top_value)


def level_of(rng, shape, cuts, smallest, high):
    factor_of, own = 1.0, jax.random.fold_in(rng, 6)
    for axis_at, shards_of in cuts:
        heights = jnp.exp(jax.random.uniform(jax.random.fold_in(own, axis_at), (shards_of,), jnp.float32, smallest / len(cuts), high / len(cuts)))
        factor_of = factor_of * jnp.repeat(heights, shape[axis_at] // shards_of).reshape([-1 if axis == axis_at else 1 for axis in range(len(shape))])
    return factor_of


def gaussian(stream_key, shape, scale, bound, cuts=(), kind=jnp.bfloat16):
    level = level_of(stream_key, shape, cuts, -0.22, 0.18) if cuts else 1.0
    values = jax.random.normal(stream_key, shape, jnp.float32) * scale * level
    return jnp.minimum(jnp.maximum(values, -bound), bound).astype(kind)


def setup_inputs(seed: int = 0, part: int = 0) -> dict:
    keys = jax.random.split(jax.random.key(seed), 10)
    part_splits = jax.random.split(jax.random.fold_in(keys[9], part), 10)
    tokens = gaussian(part_splits[0], (PATCHES, DATES, D), 1.0, 6.0, ((0, 4), (1, 4)))
    cotangent = gaussian(part_splits[1], (PATCHES, DATES, CHAN), 1.0, 6.0, ((0, 4), (1, 4)))
    valid = draw_valid(jax.random.fold_in(jax.random.fold_in(keys[9], part), 71), part)
    visible = touch_ends(jax.random.randint(part_splits[3], (PATCHES,), 0, POSN), jax.random.fold_in(part_splits[3], 1), 0, POSN - 1).astype(jnp.int32)
    live = draw_live(jax.random.fold_in(jax.random.fold_in(keys[9], part), 71), part)
    pos_table = draw_pos_table(jax.random.fold_in(keys[9], 71), part)
    norm_gain = jnp.clip(1.0 + 0.1 * jax.random.normal(keys[6], (D,), jnp.float32), 0.5, 1.5)
    norm_bias = gaussian(keys[7], (D,), 0.3, 2.0, (), jnp.float32)
    w_qkv = draw_w_qkv(jax.random.fold_in(keys[9], 71), part)
    return {"tokens": tokens, "cotangent": cotangent, "valid": valid, "visible": visible, "live": live, "pos_table": pos_table, "norm_gain": norm_gain, "norm_bias": norm_bias, "w_qkv": w_qkv}


def owner_layer(tokens, cotangent, valid, visible, live_count, pos_table, norm_gain, norm_bias, w_qkv):
    slot_count, date_count, model_width = tokens.shape
    channels = HEADS * HEAD_DIM
    inv_scale = 1.0 / HEAD_DIM ** 0.5
    position = jnp.take(pos_table, visible, axis=0).astype(jnp.float32)
    embedded = (tokens.astype(jnp.float32) + position[:, None, :]).astype(jnp.bfloat16)
    slot_live = (jnp.arange(slot_count, dtype=jnp.int32) // (BLOCK_ROWS // DG) < live_count).astype(jnp.float32)
    hidden = embedded.astype(jnp.float32)
    centred = hidden - lax.optimization_barrier(jnp.mean(hidden, axis=-1, keepdims=True))
    inv_std = lax.rsqrt(lax.optimization_barrier(jnp.mean(centred * centred, axis=-1, keepdims=True)) + 1e-06)
    unit_rows = centred * inv_std
    normed = (unit_rows * norm_gain + norm_bias).astype(jnp.bfloat16)
    qkv_all = jnp.dot(normed.reshape(-1, model_width), w_qkv, preferred_element_type=jnp.float32).astype(jnp.bfloat16)
    qkv_all = qkv_all.reshape(slot_count, date_count, 3, HEADS, HEAD_DIM).astype(jnp.float32)
    queries = qkv_all[:, :, 0]
    key_rows = qkv_all[:, :, 1]
    values = qkv_all[:, :, 2]
    scores = jnp.einsum('pthe,puhe->phtu', queries, key_rows) * inv_scale
    allowed = (valid > 0)[:, None, None, :]
    scores = jnp.where(allowed, scores, -1e+30)
    top_score = lax.optimization_barrier(jnp.max(scores, axis=-1, keepdims=True))
    exp_scores = jnp.exp(scores - top_score)
    probs_all = exp_scores / lax.optimization_barrier(jnp.sum(exp_scores, axis=-1, keepdims=True))
    probs_low = lax.optimization_barrier(probs_all.astype(jnp.bfloat16)).astype(jnp.float32)
    context = jnp.einsum('phtu,puhe->pthe', probs_low, values)
    live_grid = slot_live[:, None, None, None]
    attended = (context * live_grid).reshape(slot_count, date_count, channels).astype(jnp.bfloat16)
    upstream = cotangent.astype(jnp.float32).reshape(slot_count, date_count, HEADS, HEAD_DIM) * live_grid
    grad_values = jnp.einsum('phtu,pthe->puhe', probs_low, upstream)
    grad_probs = jnp.einsum('pthe,puhe->phtu', upstream, values)
    grad_scores = probs_all * (grad_probs - lax.optimization_barrier(jnp.sum(probs_all * grad_probs, axis=-1, keepdims=True))) * inv_scale
    grad_low = lax.optimization_barrier(grad_scores.astype(jnp.bfloat16)).astype(jnp.float32)
    grad_queries = jnp.einsum('phtu,puhe->pthe', grad_low, key_rows)
    grad_keys = jnp.einsum('phtu,pthe->puhe', grad_low, queries)
    grad_qkv = jnp.stack([grad_queries, grad_keys, grad_values], axis=2)
    grad_qkv = grad_qkv.reshape(slot_count * date_count, 3 * channels).astype(jnp.bfloat16)
    grad_normed = lax.dot_general(grad_qkv, w_qkv, (((1,), (1,)), ((), ())), preferred_element_type=jnp.float32)
    grad_normed = grad_normed.reshape(slot_count, date_count, model_width)
    grad_gain = lax.optimization_barrier(jnp.sum(grad_normed * unit_rows, axis=(0, 1)))
    grad_bias = lax.optimization_barrier(jnp.sum(grad_normed, axis=(0, 1)))
    scaled = grad_normed * norm_gain
    grad_hidden = inv_std * (scaled - lax.optimization_barrier(jnp.mean(scaled, axis=-1, keepdims=True)) - unit_rows * lax.optimization_barrier(jnp.mean(scaled * unit_rows, axis=-1, keepdims=True)))
    return (attended, grad_hidden.astype(jnp.bfloat16), jnp.stack([grad_gain, grad_bias]))

def reference(tokens, cotangent, valid, visible, live, pos_table, norm_gain, norm_bias, w_qkv):

    def per_owner(owner_items):
        return owner_layer(owner_items[0], owner_items[1], owner_items[2], owner_items[3], owner_items[4], pos_table, norm_gain, norm_bias, w_qkv)
    stacked = (tokens.reshape(N_TILE, PS, DATES, D), cotangent.reshape(N_TILE, PS, DATES, CHAN), valid.reshape(N_TILE, PS, DATES), visible.reshape(N_TILE, PS), live)
    attended, grad_all, norm_parts = lax.map(per_owner, stacked)
    return (attended.reshape(PATCHES, DATES, CHAN), grad_all.reshape(PATCHES, DATES, D), lax.optimization_barrier(jnp.sum(norm_parts, axis=0)))
```

```python
import functools

import jax
import jax.numpy as jnp
from jax import lax
from jax.experimental import pallas as pl
from jax.experimental.pallas import tpu as pltpu
from jax.sharding import PartitionSpec as P

HEAD_DIM = 80
HEADS = 16
DG = 32
BLOCK_ROWS = 32
F32 = jnp.float32
BF16 = jnp.bfloat16
VMEM_LIMIT = 48 * 1024 * 1024

VMEM = pl.BlockSpec(memory_space=pltpu.VMEM)
SMEM = pl.BlockSpec(memory_space=pltpu.SMEM)
ANY = pl.BlockSpec(memory_space=pl.ANY)


def dot(a, b):
    return jnp.dot(a, b, preferred_element_type=F32)


def dot_nt(a, b):
    return lax.dot_general(a, b, (((1,), (1,)), ((), ())), preferred_element_type=F32)


def dot_tn(a, b):
    return lax.dot_general(a, b, (((0,), (0,)), ((), ())), preferred_element_type=F32)


def norm_kernel(groups, where_ref, visible_ref, pos_ref, gain_ref, bias_ref, *refs):
    token_refs = refs[:groups]
    normed_ref, unit_ref, own_unit_ref, own_inv_ref = refs[groups:]
    slots, rows, width = token_refs[0].shape
    gain = gain_ref[...]
    bias = bias_ref[...]
    positions = []
    for p in range(slots):
        iota = lax.broadcasted_iota(jnp.int32, (8, pos_ref.shape[0]), 1)
        onehot = (iota == visible_ref[p]).astype(F32).astype(BF16)
        positions.append(dot(onehot, pos_ref[...])[0:1])
    for s in range(groups):
        for p in range(slots):
            embedded = (token_refs[s][p].astype(F32) + positions[p]).astype(BF16).astype(F32)
            centred = embedded - jnp.mean(embedded, axis=-1, keepdims=True)
            inv_std = lax.rsqrt(jnp.mean(centred * centred, axis=-1, keepdims=True) + 1e-06)
            unit = centred * inv_std
            normed_ref[p, where_ref[s]] = (unit * gain + bias).astype(BF16)
            unit_ref[p, where_ref[s]] = unit.astype(BF16)
            if s == 0:
                own_unit_ref[p] = unit
                own_inv_ref[p] = jnp.broadcast_to(inv_std, own_inv_ref.shape[1:])


def attend_kernel(chunks, copies, where_ref, live_ref, normed_ref, unit_ref, up_ref, valid_ref, *refs):
    chunk_refs = refs[:chunks]
    context_ref, grad_ref, sums_ref, weights, qkv_ref, gqkv_ref, sems = refs[chunks:]
    groups, slots, rows, channels = up_ref.shape
    dates = groups * rows
    heads = channels // HEAD_DIM
    inv_scale = 1.0 / HEAD_DIM**0.5
    moves = []
    for c, ref in enumerate(chunk_refs):
        at = pl.multiple_of(where_ref[c], 16)
        moves.append(
            pltpu.make_async_copy(ref, weights.at[pl.ds(at, ref.shape[0]), :], sems.at[c])
        )
    for move in moves:
        move.start()
    for move in moves:
        move.wait()
    qkv_ref[...] = dot(normed_ref[...], weights[...]).astype(BF16)
    for p in range(slots):
        span = slice(p * dates, (p + 1) * dates)
        alive = (live_ref[0] > p // (BLOCK_ROWS // DG)).astype(F32)
        rows_qkv = qkv_ref[span, :]
        upstream = jnp.concatenate([up_ref[g, p] for g in range(groups)], axis=0)
        upstream = upstream * alive.astype(BF16)
        allowed = valid_ref[:, p : p + 1] > 0
        grads = [[], [], []]
        contexts = []
        for h in range(heads):
            q, k, v = (
                rows_qkv[:, i * channels + h * HEAD_DIM : i * channels + (h + 1) * HEAD_DIM]
                for i in range(3)
            )
            up = upstream[:, h * HEAD_DIM : (h + 1) * HEAD_DIM]
            scores = jnp.where(allowed, dot_nt(k, q) * inv_scale, -1e30)
            exps = jnp.exp(scores - jnp.max(scores, axis=0, keepdims=True))
            probs = exps / jnp.sum(exps, axis=0, keepdims=True)
            low = probs.astype(BF16)
            contexts.append(dot_tn(low, v) * alive)
            grads[2].append(dot(low, up))
            gprobs = dot_nt(v, up)
            gscores = probs * (gprobs - jnp.sum(probs * gprobs, axis=0, keepdims=True)) * inv_scale
            glow = gscores.astype(BF16)
            grads[0].append(dot_tn(glow, k))
            grads[1].append(dot(glow, q))
        gqkv_ref[span, :] = jnp.concatenate(grads[0] + grads[1] + grads[2], axis=1).astype(BF16)
        context = jnp.concatenate(contexts, axis=1).astype(BF16)
        for g in range(groups):
            context_ref[g, p] = context[g * rows : (g + 1) * rows]
    gain_sum = None
    for p in range(slots):
        span = slice(p * dates, (p + 1) * dates)
        partial = dot_nt(gqkv_ref[span, :], weights[...])
        for g in range(groups):
            grad_ref[g, p] = partial[g * rows : (g + 1) * rows].astype(BF16)
        gain_part = jnp.sum(partial * unit_ref[span, :].astype(F32), axis=0, keepdims=True)
        bias_part = jnp.sum(partial, axis=0, keepdims=True)
        gain_sum = gain_part if gain_sum is None else gain_sum + gain_part
        bias_sum = bias_part if p == 0 else bias_sum + bias_part
    both = jnp.concatenate([gain_sum, bias_sum], axis=0)
    for c in range(copies):
        sums_ref[c] = both


def finish_kernel(live_ref, grad_ref, unit_ref, inv_ref, gain_ref, context_ref, sums_ref, attended_ref, out_ref, norm_ref):
    groups, slots, rows, width = grad_ref.shape
    gain = gain_ref[...]
    for p in range(slots):
        alive = (live_ref[0] > p // (BLOCK_ROWS // DG)).astype(F32)
        grad = grad_ref[0, p].astype(F32)
        for g in range(1, groups):
            grad = grad + grad_ref[g, p].astype(F32)
        unit = unit_ref[p]
        scaled = grad * gain
        out = inv_ref[p][:, 0:1] * (
            scaled
            - jnp.mean(scaled, axis=-1, keepdims=True)
            - unit * jnp.mean(scaled * unit, axis=-1, keepdims=True)
        )
        out_ref[p] = (out * alive).astype(BF16)
        attended_ref[p] = jnp.concatenate([context_ref[g, p] for g in range(groups)], axis=1)
    norm_ref[...] = jnp.sum(sums_ref[...], axis=0)


def local(tokens, cotangent, valid, visible, live, pos_table, norm_gain, norm_bias, w_qkv):
    slots, rows, width = tokens.shape
    groups = lax.axis_size("date")
    owners = lax.axis_size("tile")
    reps = lax.axis_size("rep")
    group = lax.axis_index("date")
    owner = lax.axis_index("tile")
    rep = lax.axis_index("rep")
    depth, triple = w_qkv.shape
    channels = triple // 3
    part = channels // groups
    dates = rows * groups
    live_here = lax.dynamic_slice_in_dim(live, owner, 1, 0)

    mine = lax.dynamic_slice_in_dim(w_qkv.reshape(depth, 3, channels), group * part, part, 2)
    mine = mine.reshape(depth, 3 * part)
    if owners == 4 and reps == 2 and depth % 32 == 0:
        half_rows = depth // 2
        half = lax.dynamic_slice_in_dim(mine, rep * half_rows, half_rows, 0)
        chunks, places = [mine], [owner * depth]
        for shift in (2, 1, 3):
            got = lax.ppermute(half, "tile", [(i, (i + shift) % owners) for i in range(owners)])
            other = lax.ppermute(got, "rep", [(0, 1), (1, 0)])
            source = (owner - shift) % owners
            chunks += [got, other]
            places += [source * depth + rep * half_rows, source * depth + (1 - rep) * half_rows]
    else:
        chunks, places = [lax.all_gather(mine, "tile", axis=0, tiled=True)], [0]
    places = jnp.stack([jnp.asarray(p, jnp.int32) for p in places])

    gathered = [tokens] + [
        lax.ppermute(tokens, "date", [(i, (i + s) % groups) for i in range(groups)])
        for s in range(1, groups)
    ]
    where = jnp.stack([(group - s) % groups for s in range(groups)]).astype(jnp.int32)
    columns = cotangent.reshape(slots, rows, groups, part).transpose(2, 0, 1, 3)
    upstream = lax.all_to_all(columns, "date", split_axis=0, concat_axis=0, tiled=True)

    params = pltpu.CompilerParams(vmem_limit_bytes=VMEM_LIMIT)
    gain2, bias2 = norm_gain.reshape(1, width), norm_bias.reshape(1, width)
    normed, unit, own_unit, own_inv = pl.pallas_call(
        functools.partial(norm_kernel, groups),
        out_shape=(
            jax.ShapeDtypeStruct((slots, groups, rows, width), BF16),
            jax.ShapeDtypeStruct((slots, groups, rows, width), BF16),
            jax.ShapeDtypeStruct((slots, rows, width), F32),
            jax.ShapeDtypeStruct((slots, rows, 128), F32),
        ),
        in_specs=[SMEM, SMEM] + [VMEM] * (3 + groups),
        out_specs=(VMEM,) * 4,
        compiler_params=params,
        cost_estimate=pl.CostEstimate(flops=10**7, bytes_accessed=6 * 10**6, transcendentals=1000),
        name="norm",
    )(where, visible, pos_table, gain2, bias2, *gathered)

    copies = groups * owners if owners == 4 else 1
    context, grad, sums = pl.pallas_call(
        functools.partial(attend_kernel, len(chunks), copies),
        out_shape=(
            jax.ShapeDtypeStruct((groups, slots, rows, part), BF16),
            jax.ShapeDtypeStruct((groups, slots, rows, width), BF16),
            jax.ShapeDtypeStruct((copies, 2, width), F32),
        ),
        in_specs=[SMEM, SMEM] + [VMEM] * 4 + [ANY] * len(chunks),
        out_specs=(VMEM,) * 3,
        scratch_shapes=[
            pltpu.VMEM((width, 3 * part), BF16),
            pltpu.VMEM((slots * dates, 3 * part), BF16),
            pltpu.VMEM((slots * dates, 3 * part), BF16),
            pltpu.SemaphoreType.DMA((len(chunks),)),
        ],
        compiler_params=params,
        cost_estimate=pl.CostEstimate(flops=3 * 10**9, bytes_accessed=10**7, transcendentals=10**6),
        name="attend",
    )(
        places,
        live_here,
        normed.reshape(slots * dates, width),
        unit.reshape(slots * dates, width),
        upstream,
        valid.T,
        *chunks,
    )

    context_home = lax.all_to_all(context, "date", split_axis=0, concat_axis=0, tiled=True)
    grad_home = lax.all_to_all(grad, "date", split_axis=0, concat_axis=0, tiled=True)
    if copies > 1:
        sums = lax.all_to_all(sums, ("date", "tile"), split_axis=0, concat_axis=0, tiled=True)
    else:
        sums = lax.psum(sums, ("date", "tile"))

    return pl.pallas_call(
        finish_kernel,
        out_shape=(
            jax.ShapeDtypeStruct((slots, rows, channels), BF16),
            jax.ShapeDtypeStruct((slots, rows, width), BF16),
            jax.ShapeDtypeStruct((2, width), F32),
        ),
        in_specs=[SMEM] + [VMEM] * 6,
        out_specs=(VMEM,) * 3,
        compiler_params=params,
        cost_estimate=pl.CostEstimate(flops=10**7, bytes_accessed=4 * 10**6, transcendentals=0),
        name="finish",
    )(live_here, grad_home, own_unit, own_inv, gain2, context_home, sums)


def solution(mesh):
    in_specs = (
        P(("rep", "tile"), "date", None),
        P(("rep", "tile"), "date", None),
        P(("rep", "tile"), None),
        P(("rep", "tile")),
        P("rep"),
        P(),
        P(),
        P(),
        P("tile", None),
    )
    out_specs = (P(("rep", "tile"), "date", None), P(("rep", "tile"), "date", None), P("rep", None))
    return jax.shard_map(local, mesh=mesh, in_specs=in_specs, out_specs=out_specs, check_vma=False)
```

```python
import functools

import jax
import jax.numpy as jnp
from jax import lax
from jax.experimental import pallas as pl
from jax.experimental.pallas import tpu as pltpu
from jax.sharding import PartitionSpec as P

HEAD_DIM = 80
DG = 32
BLOCK_ROWS = 32
F32 = jnp.float32
BF16 = jnp.bfloat16

VMEM = pl.BlockSpec(memory_space=pltpu.VMEM)
SMEM = pl.BlockSpec(memory_space=pltpu.SMEM)
HBM = pl.BlockSpec(memory_space=pltpu.HBM)


def dot(a, b):
    return jnp.dot(a, b, preferred_element_type=F32)


def dot_nt(a, b):
    return lax.dot_general(a, b, (((1,), (1,)), ((), ())), preferred_element_type=F32)


def dot_tn(a, b):
    return lax.dot_general(a, b, (((0,), (0,)), ((), ())), preferred_element_type=F32)


def norm_kernel(visible_ref, pos_ref, gain_ref, bias_ref, *refs):
    groups = len(refs) - 4
    token_refs = refs[:groups]
    normed_ref, unit_ref, own_unit_ref, own_inv_ref = refs[groups:]
    slots, rows, width = token_refs[0].shape
    gain = gain_ref[...]
    bias = bias_ref[...]
    for p in range(slots):
        iota = lax.broadcasted_iota(jnp.int32, (8, pos_ref.shape[0]), 1)
        onehot = (iota == visible_ref[p]).astype(F32).astype(BF16)
        position = dot(onehot, pos_ref[...])[0:1]
        for s in range(groups):
            embedded = (token_refs[s][p].astype(F32) + position).astype(BF16).astype(F32)
            centred = embedded - jnp.mean(embedded, axis=-1, keepdims=True)
            inv_std = lax.rsqrt(jnp.mean(centred * centred, axis=-1, keepdims=True) + 1e-06)
            unit = centred * inv_std
            normed_ref[p, s] = (unit * gain + bias).astype(BF16)
            unit_ref[p, s] = unit.astype(BF16)
            if s == 0:
                own_unit_ref[p] = unit
                own_inv_ref[p] = jnp.broadcast_to(inv_std, own_inv_ref.shape[1:])


def attend_kernel(
    places, copies, where_ref, live_ref, normed_ref, unit_ref, up_ref, valid_ref, gathered, *refs
):
    groups, slots, rows, channels = up_ref.shape
    context_refs, grad_refs = refs[:groups], refs[groups : 2 * groups]
    sums_ref, weights, qkv_ref, gqkv_ref, sems = refs[2 * groups :]
    dates = groups * rows
    heads = channels // HEAD_DIM
    inv_scale = 1.0 / HEAD_DIM**0.5
    height = gathered.shape[0] // len(places)
    moves = [
        pltpu.make_async_copy(
            gathered.at[pl.ds(c * height, height)], weights.at[pl.ds(place, height)], sems.at[c]
        )
        for c, place in enumerate(places)
    ]
    for move in moves:
        move.start()
    for move in moves:
        move.wait()
    qkv_ref[...] = dot(normed_ref[...], weights[...]).astype(BF16)
    valid_rows = jnp.concatenate(
        [valid_ref[pl.ds(pl.multiple_of(where_ref[s] * rows, rows), rows), :] for s in range(groups)],
        axis=0,
    )
    for p in range(slots):
        span = slice(p * dates, (p + 1) * dates)
        alive = (live_ref[0] > p // (BLOCK_ROWS // DG)).astype(F32)
        rows_qkv = qkv_ref[span, :]
        upstream = jnp.concatenate([up_ref[where_ref[s], p] for s in range(groups)], axis=0)
        upstream = upstream * alive.astype(BF16)
        allowed = valid_rows[:, p : p + 1] > 0
        grads = [[], [], []]
        contexts = []
        for h in range(heads):
            q, k, v = (
                rows_qkv[:, i * channels + h * HEAD_DIM : i * channels + (h + 1) * HEAD_DIM]
                for i in range(3)
            )
            up = upstream[:, h * HEAD_DIM : (h + 1) * HEAD_DIM]
            scores = jnp.where(allowed, dot_nt(k, q) * inv_scale, -1e30)
            exps = jnp.exp(scores - jnp.max(scores, axis=0, keepdims=True))
            probs = exps / jnp.sum(exps, axis=0, keepdims=True)
            low = probs.astype(BF16)
            contexts.append(dot_tn(low, v) * alive)
            grads[2].append(dot(low, up))
            gprobs = dot_nt(v, up)
            gscores = probs * (gprobs - jnp.sum(probs * gprobs, axis=0, keepdims=True)) * inv_scale
            glow = gscores.astype(BF16)
            grads[0].append(dot_tn(glow, k))
            grads[1].append(dot(glow, q))
        gqkv_ref[span, :] = jnp.concatenate(grads[0] + grads[1] + grads[2], axis=1).astype(BF16)
        context = jnp.concatenate(contexts, axis=1).astype(BF16)
        for s in range(groups):
            context_refs[s][p] = context[s * rows : (s + 1) * rows]
    gain_sum = None
    for p in range(slots):
        span = slice(p * dates, (p + 1) * dates)
        partial = dot_nt(gqkv_ref[span, :], weights[...])
        for s in range(groups):
            grad_refs[s][p] = partial[s * rows : (s + 1) * rows].astype(BF16)
        gain_part = jnp.sum(partial * unit_ref[span, :].astype(F32), axis=0, keepdims=True)
        bias_part = jnp.sum(partial, axis=0, keepdims=True)
        gain_sum = gain_part if gain_sum is None else gain_sum + gain_part
        bias_sum = bias_part if p == 0 else bias_sum + bias_part
    both = jnp.concatenate([gain_sum, bias_sum], axis=0)
    for c in range(copies):
        sums_ref[c] = both


def finish_kernel(where_ref, live_ref, unit_ref, inv_ref, gain_ref, sums_ref, *refs):
    groups = (len(refs) - 4) // 2
    context_refs, grad_refs = refs[:groups], refs[groups : 2 * groups]
    attended_ref, out_ref, norm_ref, held = refs[2 * groups :]
    slots, rows, width = unit_ref.shape
    gain = gain_ref[...]
    for s in range(groups):
        held[where_ref[s]] = context_refs[s][...]
    for p in range(slots):
        alive = (live_ref[0] > p // (BLOCK_ROWS // DG)).astype(F32)
        grad = grad_refs[0][p].astype(F32)
        for s in range(1, groups):
            grad = grad + grad_refs[s][p].astype(F32)
        unit = unit_ref[p]
        scaled = grad * gain
        out = inv_ref[p][:, 0:1] * (
            scaled
            - jnp.mean(scaled, axis=-1, keepdims=True)
            - unit * jnp.mean(scaled * unit, axis=-1, keepdims=True)
        )
        out_ref[p] = (out * alive).astype(BF16)
        attended_ref[p] = jnp.concatenate([held[g, p] for g in range(groups)], axis=1)
    norm_ref[...] = jnp.sum(sums_ref[...], axis=0)


def shifted(array, axis, shift):
    size = lax.axis_size(axis)
    return lax.ppermute(array, axis, [(i, (i + shift) % size) for i in range(size)])


def params(megabytes):
    return pltpu.CompilerParams(vmem_limit_bytes=megabytes * 1024 * 1024)


def local(tokens, cotangent, valid, visible, live, pos_table, norm_gain, norm_bias, w_qkv):
    slots, rows, width = tokens.shape
    groups = lax.axis_size("date")
    owners = lax.axis_size("tile")
    reps = lax.axis_size("rep")
    group = lax.axis_index("date")
    owner = lax.axis_index("tile")
    rep = lax.axis_index("rep")
    depth, triple = w_qkv.shape
    channels = triple // 3
    part = channels // groups
    dates = rows * groups
    live_here = lax.dynamic_slice_in_dim(live, owner, 1, 0)

    share = depth // reps
    spread = share % 16 == 0
    first, height = (rep * share, share) if spread else (0, depth)
    mine = jnp.concatenate(
        [
            lax.dynamic_slice(w_qkv, (first, i * channels + group * part), (height, part))
            for i in range(3)
        ],
        axis=1,
    )
    if spread:
        weights = lax.all_gather(mine, ("rep", "tile"), axis=0, tiled=True)
        places = [k * depth + r * share for r in range(reps) for k in range(owners)]
    else:
        weights = lax.all_gather(mine, "tile", axis=0, tiled=True)
        places = [0]

    gathered = [tokens] + [shifted(tokens, "date", s) for s in range(1, groups)]
    columns = cotangent.reshape(slots, rows, groups, part).transpose(2, 0, 1, 3)
    upstream = lax.all_to_all(columns, "date", split_axis=0, concat_axis=0, tiled=True)
    where = jnp.stack([(group - s) % groups for s in range(groups)]).astype(jnp.int32)
    whence = jnp.stack([(group + s) % groups for s in range(groups)]).astype(jnp.int32)

    gain2, bias2 = norm_gain.reshape(1, width), norm_bias.reshape(1, width)
    normed, unit, own_unit, own_inv = pl.pallas_call(
        norm_kernel,
        out_shape=(
            jax.ShapeDtypeStruct((slots, groups, rows, width), BF16),
            jax.ShapeDtypeStruct((slots, groups, rows, width), BF16),
            jax.ShapeDtypeStruct((slots, rows, width), F32),
            jax.ShapeDtypeStruct((slots, rows, 128), F32),
        ),
        in_specs=[SMEM] + [VMEM] * (3 + groups),
        out_specs=(VMEM,) * 4,
        compiler_params=params(16),
        cost_estimate=pl.CostEstimate(flops=10**7, bytes_accessed=6 * 10**6, transcendentals=1000),
        name="norm",
    )(visible, pos_table, gain2, bias2, *gathered)

    copies = groups * owners if owners == 4 else 1
    results = pl.pallas_call(
        functools.partial(attend_kernel, places, copies),
        out_shape=(jax.ShapeDtypeStruct((slots, rows, part), BF16),) * groups
        + (jax.ShapeDtypeStruct((slots, rows, width), BF16),) * groups
        + (jax.ShapeDtypeStruct((copies, 2, width), F32),),
        in_specs=[SMEM, SMEM] + [VMEM] * 4 + [HBM],
        out_specs=(VMEM,) * (2 * groups + 1),
        scratch_shapes=[
            pltpu.VMEM((width, 3 * part), BF16),
            pltpu.VMEM((slots * dates, 3 * part), BF16),
            pltpu.VMEM((slots * dates, 3 * part), BF16),
            pltpu.SemaphoreType.DMA((len(places),)),
        ],
        compiler_params=params(24),
        cost_estimate=pl.CostEstimate(flops=3 * 10**9, bytes_accessed=10**7, transcendentals=10**6),
        name="attend",
    )(
        where,
        live_here,
        normed.reshape(slots * dates, width),
        unit.reshape(slots * dates, width),
        upstream,
        valid.T,
        weights,
    )
    contexts, grads, sums = results[:groups], results[groups : 2 * groups], results[-1]

    grad_home = [grads[0]] + [shifted(grads[s], "date", -s) for s in range(1, groups)]
    context_home = [contexts[0]] + [shifted(contexts[s], "date", -s) for s in range(1, groups)]
    if copies > 1:
        sums = lax.all_to_all(sums, ("date", "tile"), split_axis=0, concat_axis=0, tiled=True)
    else:
        sums = lax.psum(sums, ("date", "tile"))

    return pl.pallas_call(
        finish_kernel,
        out_shape=(
            jax.ShapeDtypeStruct((slots, rows, channels), BF16),
            jax.ShapeDtypeStruct((slots, rows, width), BF16),
            jax.ShapeDtypeStruct((2, width), F32),
        ),
        in_specs=[SMEM, SMEM] + [VMEM] * (4 + 2 * groups),
        out_specs=(VMEM,) * 3,
        scratch_shapes=[pltpu.VMEM((groups, slots, rows, part), BF16)],
        compiler_params=params(16),
        cost_estimate=pl.CostEstimate(flops=10**7, bytes_accessed=4 * 10**6, transcendentals=0),
        name="finish",
    )(whence, live_here, own_unit, own_inv, gain2, sums, *context_home, *grad_home)


def solution(mesh):
    in_specs = (
        P(("rep", "tile"), "date", None),
        P(("rep", "tile"), "date", None),
        P(("rep", "tile"), None),
        P(("rep", "tile")),
        P("rep"),
        P(),
        P(),
        P(),
        P("tile", None),
    )
    out_specs = (P(("rep", "tile"), "date", None), P(("rep", "tile"), "date", None), P("rep", None))
    return jax.shard_map(local, mesh=mesh, in_specs=in_specs, out_specs=out_specs, check_vma=False)
```

```python
import functools

import jax
import jax.numpy as jnp
from jax import lax
from jax.experimental import pallas as pl
from jax.experimental.pallas import tpu as pltpu
from jax.sharding import PartitionSpec as P

HEAD_DIM = 80
DG = 32
BLOCK_ROWS = 32
F32 = jnp.float32
BF16 = jnp.bfloat16

VMEM = pl.BlockSpec(memory_space=pltpu.VMEM)
SMEM = pl.BlockSpec(memory_space=pltpu.SMEM)
HBM = pl.BlockSpec(memory_space=pltpu.HBM)


def dot(a, b):
    return jnp.dot(a, b, preferred_element_type=F32)


def dot_nt(a, b):
    return lax.dot_general(a, b, (((1,), (1,)), ((), ())), preferred_element_type=F32)


def dot_tn(a, b):
    return lax.dot_general(a, b, (((0,), (0,)), ((), ())), preferred_element_type=F32)


def run_all(moves):
    for move in moves:
        move.start()
    for move in moves:
        move.wait()


def pick_kernel(part, spot_ref, w_ref, out_ref, windows, sems):
    height = out_ref.shape[0]
    channels = w_ref.shape[1] // 3
    first = pl.multiple_of(spot_ref[0], 16)
    group = spot_ref[1]
    odd = lax.rem(group, 2)
    wide = windows.shape[2]
    start = (group // 2) * (2 * part) + odd * (2 * part - wide)
    run_all(
        [
            pltpu.make_async_copy(
                w_ref.at[
                    pl.ds(first, height), pl.ds(pl.multiple_of(i * channels + start, 128), wide)
                ],
                windows.at[i],
                sems.at[i],
            )
            for i in range(3)
        ]
    )
    pieces = []
    for i in range(3):
        window = windows[i]
        pieces.append(jnp.where(odd == 1, window[:, wide - part :], window[:, :part]))
    out_ref[...] = jnp.concatenate(pieces, axis=1)


def norm_kernel(visible_ref, pos_ref, gain_ref, bias_ref, *refs):
    groups = len(refs) - 7
    token_refs = refs[:groups]
    normed_out, unit_out, own_unit_ref, own_inv_ref, normed_ref, unit_ref, sems = refs[groups:]
    slots, rows, width = token_refs[0].shape
    gain = gain_ref[...]
    bias = bias_ref[...]
    moves = []
    for p in range(slots):
        iota = lax.broadcasted_iota(jnp.int32, (8, pos_ref.shape[0]), 1)
        onehot = (iota == visible_ref[p]).astype(F32).astype(BF16)
        position = dot(onehot, pos_ref[...])[0:1]
        for s in range(groups):
            embedded = (token_refs[s][p].astype(F32) + position).astype(BF16).astype(F32)
            centred = embedded - jnp.mean(embedded, axis=-1, keepdims=True)
            inv_std = lax.rsqrt(jnp.mean(centred * centred, axis=-1, keepdims=True) + 1e-06)
            unit = centred * inv_std
            normed_ref[p, s] = (unit * gain + bias).astype(BF16)
            unit_ref[p, s] = unit.astype(BF16)
            if s == 0:
                own_unit_ref[p] = unit
                own_inv_ref[p] = jnp.broadcast_to(inv_std, own_inv_ref.shape[1:])
        for i, (here, out) in enumerate(((normed_ref, normed_out), (unit_ref, unit_out))):
            moves.append(pltpu.make_async_copy(here.at[p], out.at[p], sems.at[2 * p + i]))
            moves[-1].start()
    for move in moves:
        move.wait()


def weight_moves(places_ref, chunk_refs, weights, sems):
    return [
        pltpu.make_async_copy(
            ref,
            weights.at[pl.ds(pl.multiple_of(places_ref[c], 16), ref.shape[0]), :],
            sems.at[c],
        )
        for c, ref in enumerate(chunk_refs)
    ]


def attend_kernel(chunks, where_ref, live_ref, places_ref, normed_hbm, up_ref, valid_ref, *refs):
    groups, slots, rows, channels = up_ref.shape
    chunk_refs = refs[:chunks]
    context_outs = refs[chunks : chunks + groups]
    gqkv_out, weights, normed, qkv_ref, gqkv_ref, context_ref, sems, out_sems = refs[chunks + groups :]
    dates = groups * rows
    heads = channels // HEAD_DIM
    inv_scale = 1.0 / HEAD_DIM**0.5
    run_all(
        weight_moves(places_ref, chunk_refs, weights, sems)
        + [pltpu.make_async_copy(normed_hbm, normed, sems.at[chunks])]
    )
    qkv_ref[...] = dot(normed[...], weights[...]).astype(BF16)
    valid_rows = jnp.concatenate(
        [valid_ref[pl.ds(pl.multiple_of(where_ref[s] * rows, rows), rows), :] for s in range(groups)],
        axis=0,
    )
    moves = []
    for p in range(slots):
        span = slice(p * dates, (p + 1) * dates)
        alive = (live_ref[0] > p // (BLOCK_ROWS // DG)).astype(F32)
        rows_qkv = qkv_ref[span, :]
        upstream = jnp.concatenate([up_ref[where_ref[s], p] for s in range(groups)], axis=0)
        upstream = upstream * alive.astype(BF16)
        allowed = valid_rows[:, p : p + 1] > 0
        grads = [[], [], []]
        contexts = []
        for h in range(heads):
            q, k, v = (
                rows_qkv[:, i * channels + h * HEAD_DIM : i * channels + (h + 1) * HEAD_DIM]
                for i in range(3)
            )
            up = upstream[:, h * HEAD_DIM : (h + 1) * HEAD_DIM]
            scores = jnp.where(allowed, dot_nt(k, q) * inv_scale, -1e30)
            exps = jnp.exp(scores - jnp.max(scores, axis=0, keepdims=True))
            probs = exps * (1.0 / jnp.sum(exps, axis=0, keepdims=True))
            low = probs.astype(BF16)
            contexts.append(dot_tn(low, v) * alive)
            grads[2].append(dot(low, up))
            gprobs = dot_nt(v, up)
            gscores = probs * (gprobs - jnp.sum(probs * gprobs, axis=0, keepdims=True)) * inv_scale
            glow = gscores.astype(BF16)
            grads[0].append(dot_tn(glow, k))
            grads[1].append(dot(glow, q))
        gqkv_ref[span, :] = jnp.concatenate(grads[0] + grads[1] + grads[2], axis=1).astype(BF16)
        context_ref[span, :] = jnp.concatenate(contexts, axis=1).astype(BF16)
        first = len(moves)
        moves.append(pltpu.make_async_copy(gqkv_ref.at[span], gqkv_out.at[span], out_sems.at[first]))
        for s in range(groups):
            piece = context_ref.at[pl.ds(p * dates + s * rows, rows)]
            moves.append(
                pltpu.make_async_copy(piece, context_outs[s].at[p], out_sems.at[first + 1 + s])
            )
        for move in moves[first:]:
            move.start()
    for move in moves:
        move.wait()


def back_kernel(chunks, copies, places_ref, gqkv_hbm, unit_hbm, *refs):
    chunk_refs = refs[:chunks]
    stay_out, cross_out, sums_ref, weights, gqkv, unit, stay, cross, sems, out_sems = refs[chunks:]
    halves, slots, rows, width = stay.shape
    groups = 2 * halves
    dates = groups * rows
    unit_move = pltpu.make_async_copy(unit_hbm, unit, sems.at[chunks + 1])
    unit_move.start()
    run_all(
        weight_moves(places_ref, chunk_refs, weights, sems)
        + [pltpu.make_async_copy(gqkv_hbm, gqkv, sems.at[chunks])]
    )
    unit_move.wait()
    step = 256
    moves = []
    for n in range(width // step):
        lanes = slice(n * step, (n + 1) * step)
        partial = dot_nt(gqkv[...], weights[lanes, :])
        low = partial.astype(BF16)
        for p in range(slots):
            for s in range(groups):
                at = p * dates + s * rows
                (cross if s % 2 else stay)[s // 2, p, :, lanes] = low[at : at + rows]
        sums_ref[0, 0:1, lanes] = jnp.sum(partial * unit[:, lanes].astype(F32), axis=0, keepdims=True)
        sums_ref[0, 1:2, lanes] = jnp.sum(partial, axis=0, keepdims=True)
        for i, (here, out) in enumerate(((cross, cross_out), (stay, stay_out))):
            spot = pl.ds(n * step, step)
            moves.append(
                pltpu.make_async_copy(
                    here.at[:, :, :, spot], out.at[:, :, :, spot], out_sems.at[2 * n + i]
                )
            )
            moves[-1].start()
    for c in range(1, copies):
        sums_ref[c] = sums_ref[0]
    for move in moves:
        move.wait()


def finish_kernel(where_ref, live_ref, unit_ref, inv_ref, gain_ref, sums_ref, stay_ref, near_ref, far_ref, *refs):
    groups = len(refs) - 4
    context_refs = refs[:groups]
    attended_ref, out_ref, norm_ref, held = refs[groups:]
    slots, rows, width = unit_ref.shape
    gain = gain_ref[...]
    for s in range(groups):
        held[where_ref[s]] = context_refs[s][...]
    for p in range(slots):
        alive = (live_ref[0] > p // (BLOCK_ROWS // DG)).astype(F32)
        grad = stay_ref[p].astype(F32) + near_ref[p].astype(F32) + far_ref[p].astype(F32)
        unit = unit_ref[p]
        scaled = grad * gain
        out = inv_ref[p][:, 0:1] * (
            scaled
            - jnp.mean(scaled, axis=-1, keepdims=True)
            - unit * jnp.mean(scaled * unit, axis=-1, keepdims=True)
        )
        out_ref[p] = (out * alive).astype(BF16)
        attended_ref[p] = jnp.concatenate([held[g, p] for g in range(groups)], axis=1)
    norm_ref[...] = jnp.sum(sums_ref[...], axis=0)


def swapped(array, axis, bits):
    return lax.ppermute(array, axis, [(i, i ^ bits) for i in range(lax.axis_size(axis))])


def params(megabytes):
    return pltpu.CompilerParams(vmem_limit_bytes=megabytes * 1024 * 1024)


def pick(w_qkv, first, height, group, part):
    wide = -(-part // 128) * 128
    spot = jnp.stack([jnp.asarray(first, jnp.int32), group.astype(jnp.int32)])
    return pl.pallas_call(
        functools.partial(pick_kernel, part),
        out_shape=jax.ShapeDtypeStruct((height, 3 * part), BF16),
        in_specs=[SMEM, HBM],
        out_specs=VMEM,
        scratch_shapes=[pltpu.VMEM((3, height, wide), BF16), pltpu.SemaphoreType.DMA((3,))],
        compiler_params=params(4),
        cost_estimate=pl.CostEstimate(flops=10**5, bytes_accessed=10**6, transcendentals=0),
        name="pick",
    )(spot, w_qkv)


def gather_weights(w_qkv, group, part):
    owners = lax.axis_size("tile")
    owner = lax.axis_index("tile")
    rep = lax.axis_index("rep")
    depth, triple = w_qkv.shape
    share = depth // 2
    if owners != 4 or lax.axis_size("rep") != 2 or share % 16:
        mine = jnp.concatenate(
            [
                lax.dynamic_slice_in_dim(w_qkv, i * (triple // 3) + group * part, part, 1)
                for i in range(3)
            ],
            axis=1,
        )
        return [lax.all_gather(mine, "tile", axis=0, tiled=True)], [0]
    ring = [0, 1, 3, 2]
    held = pick(w_qkv, rep * share, share, group, part)
    rest = pick(w_qkv, (1 - rep) * share, share, group, part)
    pieces = [held, rest]
    places = [owner * depth + rep * share, owner * depth + (1 - rep) * share]
    spot = owner ^ (owner >> 1)
    for step in range(1, owners):
        held = lax.ppermute(held, "tile", [(ring[i], ring[(i + 1) % owners]) for i in range(owners)])
        back = (spot - step) % owners
        source = back ^ (back >> 1)
        pieces += [held, swapped(held, "rep", 1)]
        places += [source * depth + rep * share, source * depth + (1 - rep) * share]
    return pieces, places


def local(tokens, cotangent, valid, visible, live, pos_table, norm_gain, norm_bias, w_qkv):
    slots, rows, width = tokens.shape
    groups = lax.axis_size("date")
    owners = lax.axis_size("tile")
    group = lax.axis_index("date")
    owner = lax.axis_index("tile")
    channels = w_qkv.shape[1] // 3
    part = channels // groups
    dates = rows * groups
    live_here = lax.dynamic_slice_in_dim(live, owner, 1, 0)
    where = jnp.stack([group ^ s for s in range(groups)]).astype(jnp.int32)

    pieces, places = gather_weights(w_qkv, group, part)
    places = jnp.stack([jnp.asarray(p, jnp.int32) for p in places])
    chunks = len(pieces)

    across = swapped(tokens, "date", 2)
    gathered = [tokens, swapped(tokens, "date", 1), across, swapped(across, "date", 1)]
    columns = cotangent.reshape(slots, rows, groups, part).transpose(2, 0, 1, 3)
    upstream = lax.all_to_all(columns, "date", split_axis=0, concat_axis=0, tiled=True)

    gain2, bias2 = norm_gain.reshape(1, width), norm_bias.reshape(1, width)
    normed, unit, own_unit, own_inv = pl.pallas_call(
        norm_kernel,
        out_shape=(
            jax.ShapeDtypeStruct((slots, groups, rows, width), BF16),
            jax.ShapeDtypeStruct((slots, groups, rows, width), BF16),
            jax.ShapeDtypeStruct((slots, rows, width), F32),
            jax.ShapeDtypeStruct((slots, rows, 128), F32),
        ),
        in_specs=[SMEM] + [VMEM] * (3 + groups),
        out_specs=(HBM, HBM, VMEM, VMEM),
        scratch_shapes=[
            pltpu.VMEM((slots, groups, rows, width), BF16),
            pltpu.VMEM((slots, groups, rows, width), BF16),
            pltpu.SemaphoreType.DMA((2 * slots,)),
        ],
        compiler_params=params(12),
        cost_estimate=pl.CostEstimate(flops=10**7, bytes_accessed=6 * 10**6, transcendentals=1000),
        name="norm",
    )(visible, pos_table, gain2, bias2, *gathered)

    results = pl.pallas_call(
        functools.partial(attend_kernel, chunks),
        out_shape=(jax.ShapeDtypeStruct((slots, rows, part), BF16),) * groups
        + (jax.ShapeDtypeStruct((slots * dates, 3 * part), BF16),),
        in_specs=[SMEM, SMEM, SMEM, HBM, VMEM, VMEM] + [HBM] * chunks,
        out_specs=(HBM,) * (groups + 1),
        scratch_shapes=[
            pltpu.VMEM((width, 3 * part), BF16),
            pltpu.VMEM((slots * dates, width), BF16),
            pltpu.VMEM((slots * dates, 3 * part), BF16),
            pltpu.VMEM((slots * dates, 3 * part), BF16),
            pltpu.VMEM((slots * dates, part), BF16),
            pltpu.SemaphoreType.DMA((chunks + 1,)),
            pltpu.SemaphoreType.DMA((slots * (groups + 1),)),
        ],
        compiler_params=params(20),
        cost_estimate=pl.CostEstimate(flops=3 * 10**9, bytes_accessed=10**7, transcendentals=10**6),
        name="attend",
    )(where, live_here, places, normed.reshape(slots * dates, width), upstream, valid.T, *pieces)
    contexts, gqkv = results[:groups], results[-1]

    copies = groups * owners if owners == 4 else 1
    half = (groups // 2, slots, rows, width)
    stay, cross, sums = pl.pallas_call(
        functools.partial(back_kernel, chunks, copies),
        out_shape=(
            jax.ShapeDtypeStruct(half, BF16),
            jax.ShapeDtypeStruct(half, BF16),
            jax.ShapeDtypeStruct((copies, 2, width), F32),
        ),
        in_specs=[SMEM, HBM, HBM] + [HBM] * chunks,
        out_specs=(HBM, HBM, VMEM),
        scratch_shapes=[
            pltpu.VMEM((width, 3 * part), BF16),
            pltpu.VMEM((slots * dates, 3 * part), BF16),
            pltpu.VMEM((slots * dates, width), BF16),
            pltpu.VMEM(half, BF16),
            pltpu.VMEM(half, BF16),
            pltpu.SemaphoreType.DMA((chunks + 2,)),
            pltpu.SemaphoreType.DMA((2 * (width // 256),)),
        ],
        compiler_params=params(20),
        cost_estimate=pl.CostEstimate(flops=2 * 10**9, bytes_accessed=10**7, transcendentals=0),
        name="back",
    )(places, gqkv, unit.reshape(slots * dates, width), *pieces)

    context_home = [contexts[0]] + [swapped(contexts[s], "date", s) for s in range(1, groups)]
    near = swapped(cross, "date", 1)
    chip_sum = (stay[1].astype(F32) + near[1].astype(F32)).astype(BF16)
    far = swapped(chip_sum, "date", 2)
    if copies > 1:
        sums = lax.all_to_all(sums, ("date", "tile"), split_axis=0, concat_axis=0, tiled=True)
    else:
        sums = lax.psum(sums, ("date", "tile"))

    return pl.pallas_call(
        finish_kernel,
        out_shape=(
            jax.ShapeDtypeStruct((slots, rows, channels), BF16),
            jax.ShapeDtypeStruct((slots, rows, width), BF16),
            jax.ShapeDtypeStruct((2, width), F32),
        ),
        in_specs=[SMEM, SMEM] + [VMEM] * (7 + groups),
        out_specs=(VMEM,) * 3,
        scratch_shapes=[pltpu.VMEM((groups, slots, rows, part), BF16)],
        compiler_params=params(12),
        cost_estimate=pl.CostEstimate(flops=10**7, bytes_accessed=4 * 10**6, transcendentals=0),
        name="finish",
    )(where, live_here, own_unit, own_inv, gain2, sums, stay[0], near[0], far, *context_home)


def solution(mesh):
    in_specs = (
        P(("rep", "tile"), "date", None),
        P(("rep", "tile"), "date", None),
        P(("rep", "tile"), None),
        P(("rep", "tile")),
        P("rep"),
        P(),
        P(),
        P(),
        P("tile", None),
    )
    out_specs = (P(("rep", "tile"), "date", None), P(("rep", "tile"), "date", None), P("rep", None))
    return jax.shard_map(local, mesh=mesh, in_specs=in_specs, out_specs=out_specs, check_vma=False)
```

```python
import functools

import jax
import jax.numpy as jnp
from jax import lax
from jax.experimental import pallas as pl
from jax.experimental.pallas import tpu as pltpu
from jax.sharding import PartitionSpec as P

HEAD_DIM = 80
DG = 32
BLOCK_ROWS = 32
F32 = jnp.float32
BF16 = jnp.bfloat16

VMEM = pl.BlockSpec(memory_space=pltpu.VMEM)
SMEM = pl.BlockSpec(memory_space=pltpu.SMEM)
HBM = pl.BlockSpec(memory_space=pltpu.HBM)


def dot(a, b):
    return jnp.dot(a, b, preferred_element_type=F32)


def dot_nt(a, b):
    return lax.dot_general(a, b, (((1,), (1,)), ((), ())), preferred_element_type=F32)


def dot_tn(a, b):
    return lax.dot_general(a, b, (((0,), (0,)), ((), ())), preferred_element_type=F32)


def window_of(group, part):
    wide = -(-part // 128) * 128
    odd = lax.rem(group, 2)
    start = (group // 2) * (2 * part) + odd * (2 * part - wide)
    return start, wide, odd == 1


def pick_kernel(part, other, ids_ref, w_ref, out_ref, windows, sems):
    height = out_ref.shape[0]
    channels = w_ref.shape[1] // 3
    half = 1 - ids_ref[0] if other else ids_ref[0]
    first = pl.multiple_of(half * height, 16)
    start, wide, odd = window_of(ids_ref[1], part)
    moves = [
        pltpu.make_async_copy(
            w_ref.at[pl.ds(first, height), pl.ds(pl.multiple_of(i * channels + start, 128), wide)],
            windows.at[i],
            sems.at[i],
        )
        for i in range(3)
    ]
    for move in moves:
        move.start()
    for move in moves:
        move.wait()
    pieces = []
    for i in range(3):
        window = windows[i]
        pieces.append(jnp.where(odd, window[:, wide - part :], window[:, :part]))
    out_ref[...] = jnp.concatenate(pieces, axis=1)


def columns_kernel(ids_ref, cotangent_ref, *out_refs):
    part = out_refs[0].shape[2]
    for s, out_ref in enumerate(out_refs):
        start, wide, odd = window_of(ids_ref[1] ^ s, part)
        window = cotangent_ref[:, :, pl.ds(pl.multiple_of(start, 128), wide)]
        out_ref[...] = jnp.where(odd, window[:, :, wide - part :], window[:, :, :part])


def norm_kernel(visible_ref, pos_ref, gain_ref, bias_ref, *refs):
    groups = len(refs) - 4
    token_refs = refs[:groups]
    normed_ref, unit_ref, own_unit_ref, own_inv_ref = refs[groups:]
    slots, rows, width = token_refs[0].shape
    gain = gain_ref[...]
    bias = bias_ref[...]
    for p in range(slots):
        iota = lax.broadcasted_iota(jnp.int32, (8, pos_ref.shape[0]), 1)
        onehot = (iota == visible_ref[p]).astype(F32).astype(BF16)
        position = dot(onehot, pos_ref[...])[0:1]
        for s in range(groups):
            embedded = (token_refs[s][p].astype(F32) + position).astype(BF16).astype(F32)
            centred = embedded - jnp.mean(embedded, axis=-1, keepdims=True)
            inv_std = lax.rsqrt(jnp.mean(centred * centred, axis=-1, keepdims=True) + 1e-06)
            unit = centred * inv_std
            at = (p * groups + s) * rows
            normed_ref[at : at + rows] = (unit * gain + bias).astype(BF16)
            unit_ref[at : at + rows] = unit.astype(BF16)
            if s == 0:
                own_unit_ref[p] = unit
                own_inv_ref[p] = jnp.broadcast_to(inv_std, own_inv_ref.shape[1:])


def piece_rows(ids_ref, count, depth):
    if count == 1:
        return [0]
    rep, owner = ids_ref[0], ids_ref[2]
    owners = count // 2
    share = depth // 2
    spot = owner ^ (owner >> 1)
    firsts = []
    for step in range(owners):
        back = lax.rem(spot + owners - step, owners)
        source = back ^ (back >> 1)
        firsts.append(pl.multiple_of(source * depth + rep * share, 16))
        firsts.append(pl.multiple_of(source * depth + (1 - rep) * share, 16))
    return firsts


def attend_kernel(count, depth, ids_ref, live_ref, normed_ref, valid_ref, *refs):
    groups = (len(refs) - count - 3) // 2
    up_refs, piece_refs = refs[:groups], refs[groups : groups + count]
    context_refs = refs[groups + count : 2 * groups + count]
    gqkv_ref, weights, qkv_ref = refs[2 * groups + count :]
    slots, rows, channels = up_refs[0].shape
    dates = groups * rows
    heads = channels // HEAD_DIM
    inv_scale = 1.0 / HEAD_DIM**0.5
    for first, ref in zip(piece_rows(ids_ref, count, depth), piece_refs):
        weights[pl.ds(first, ref.shape[0]), :] = ref[...]
    qkv_ref[...] = dot(normed_ref[...], weights[...]).astype(BF16)
    valid_rows = jnp.concatenate(
        [
            valid_ref[pl.ds(pl.multiple_of((ids_ref[1] ^ s) * rows, rows), rows), :]
            for s in range(groups)
        ],
        axis=0,
    )
    for p in range(slots):
        span = slice(p * dates, (p + 1) * dates)
        alive = (live_ref[ids_ref[2]] > p // (BLOCK_ROWS // DG)).astype(F32)
        rows_qkv = qkv_ref[span, :]
        upstream = jnp.concatenate([ref[p] for ref in up_refs], axis=0) * alive.astype(BF16)
        allowed = valid_rows[:, p : p + 1] > 0
        grads = [[], [], []]
        contexts = []
        for h in range(heads):
            q, k, v = (
                rows_qkv[:, i * channels + h * HEAD_DIM : i * channels + (h + 1) * HEAD_DIM]
                for i in range(3)
            )
            up = upstream[:, h * HEAD_DIM : (h + 1) * HEAD_DIM]
            scores = jnp.where(allowed, dot_nt(k, q) * inv_scale, -1e30)
            exps = jnp.exp(scores - jnp.max(scores, axis=0, keepdims=True))
            probs = exps * (1.0 / jnp.sum(exps, axis=0, keepdims=True))
            low = probs.astype(BF16)
            contexts.append(dot_tn(low, v) * alive)
            grads[2].append(dot(low, up))
            gprobs = dot_nt(v, up)
            gscores = probs * (gprobs - jnp.sum(probs * gprobs, axis=0, keepdims=True)) * inv_scale
            glow = gscores.astype(BF16)
            grads[0].append(dot_tn(glow, k))
            grads[1].append(dot(glow, q))
        gqkv_ref[span, :] = jnp.concatenate(grads[0] + grads[1] + grads[2], axis=1).astype(BF16)
        context = jnp.concatenate(contexts, axis=1).astype(BF16)
        for s in range(groups):
            context_refs[s][p] = context[s * rows : (s + 1) * rows]


def back_kernel(gqkv_ref, unit_ref, weights, stay_ref, pass_ref, cross_ref, sums_ref):
    slots, rows, width = stay_ref.shape
    groups = 4
    dates = groups * rows
    step = 256
    for n in range(width // step):
        lanes = slice(n * step, (n + 1) * step)
        partial = dot_nt(gqkv_ref[...], weights[lanes, :])
        low = partial.astype(BF16)
        for p in range(slots):
            for s, out in enumerate((stay_ref, cross_ref.at[0], pass_ref, cross_ref.at[1])):
                at = p * dates + s * rows
                out[p, :, lanes] = low[at : at + rows]
        sums_ref[0:1, lanes] = jnp.sum(partial * unit_ref[:, lanes].astype(F32), axis=0, keepdims=True)
        sums_ref[1:2, lanes] = jnp.sum(partial, axis=0, keepdims=True)


def merge_kernel(pass_ref, near_ref, *refs):
    out_ref, total_ref = refs[-2:]
    out_ref[...] = (pass_ref[...].astype(F32) + near_ref[1].astype(F32)).astype(BF16)
    total = refs[0][...]
    for ref in refs[1:-2]:
        total = total + ref[...]
    total_ref[...] = total


def home_kernel(ids_ref, stay_ref, near_ref, *refs):
    groups = len(refs) - 3
    context_refs = refs[:groups]
    grad_ref, attended_ref, held = refs[groups:]
    grad_ref[...] = stay_ref[...].astype(F32) + near_ref[0].astype(F32)
    for s in range(groups):
        held[ids_ref[1] ^ s] = context_refs[s][...]
    for p in range(attended_ref.shape[0]):
        attended_ref[p] = jnp.concatenate([held[g, p] for g in range(groups)], axis=1)


def finish_kernel(ids_ref, live_ref, unit_ref, inv_ref, gain_ref, grad_ref, far_ref, *refs):
    out_ref, norm_ref = refs[-2:]
    slots = unit_ref.shape[0]
    gain = gain_ref[...]
    for p in range(slots):
        alive = (live_ref[ids_ref[2]] > p // (BLOCK_ROWS // DG)).astype(F32)
        unit = unit_ref[p]
        scaled = (grad_ref[p] + far_ref[p].astype(F32)) * gain
        out = inv_ref[p][:, 0:1] * (
            scaled
            - jnp.mean(scaled, axis=-1, keepdims=True)
            - unit * jnp.mean(scaled * unit, axis=-1, keepdims=True)
        )
        out_ref[p] = (out * alive).astype(BF16)
    total = refs[0][...]
    for ref in refs[1:-2]:
        total = total + ref[...]
    norm_ref[...] = total


def swapped(array, axis, bits):
    return lax.ppermute(array, axis, [(i, i ^ bits) for i in range(lax.axis_size(axis))])


def after(array, *others):
    return lax.optimization_barrier((array, *others))[0]


def near(array):
    return pltpu.with_memory_space_constraint(array, pltpu.VMEM)


def call(kernel, name, out_shape, in_specs, args, megabytes, flops=10**6, size=10**6, scratch=()):
    return pl.pallas_call(
        kernel,
        out_shape=out_shape,
        in_specs=in_specs,
        out_specs=jax.tree.map(lambda _: VMEM, out_shape),
        scratch_shapes=list(scratch),
        compiler_params=pltpu.CompilerParams(vmem_limit_bytes=megabytes * 1024 * 1024),
        cost_estimate=pl.CostEstimate(flops=flops, bytes_accessed=size, transcendentals=0),
        name=name,
    )(*args)


def pick(w_qkv, ids, share, part, other):
    wide = -(-part // 128) * 128
    return call(
        functools.partial(pick_kernel, part, other),
        "pick",
        pltpu.VMEM((share, 3 * part), BF16),
        [SMEM, HBM],
        (ids, pltpu.with_memory_space_constraint(w_qkv, pltpu.HBM)),
        4,
        scratch=(pltpu.VMEM((3, share, wide), BF16), pltpu.SemaphoreType.DMA((3,))),
    )


def local(tokens, cotangent, valid, visible, live, pos_table, norm_gain, norm_bias, w_qkv):
    slots, rows, width = tokens.shape
    groups = lax.axis_size("date")
    owners = lax.axis_size("tile")
    depth, triple = w_qkv.shape
    channels = triple // 3
    part = channels // groups
    dates = rows * groups
    ids = jnp.stack([lax.axis_index(name) for name in ("rep", "date", "tile")]).astype(jnp.int32)
    gain2, bias2 = norm_gain.reshape(1, width), norm_bias.reshape(1, width)
    valid_t = valid.T

    chain = owners == 4 and lax.axis_size("rep") == 2 and depth % 32 == 0
    ring = [(0, 1), (1, 3), (3, 2), (2, 0)]
    share = depth // 2
    if chain:
        held = pick(w_qkv, ids, share, part, False)
        first = lax.ppermute(held, "tile", ring)
        rest = pick(w_qkv, ids, share, part, True)
    across = swapped(tokens, "date", 2)
    beside = swapped(tokens, "date", 1)
    ups = call(
        columns_kernel,
        "columns",
        (jax.ShapeDtypeStruct((slots, rows, part), BF16),) * groups,
        [SMEM, VMEM],
        (ids, cotangent),
        4,
    )
    ups = [ups[0]] + [swapped(ups[s], "date", s) for s in range(1, groups)]
    beyond = swapped(across, "date", 1)
    if chain:
        first = after(first, across, *ups[1:])
        second = lax.ppermute(first, "tile", ring)
        first_other = swapped(first, "rep", 1)
        second = after(second, beside, beyond, first_other)
        third = lax.ppermute(second, "tile", ring)
        second_other = swapped(second, "rep", 1)
    gathered = [tokens, beside, across, beyond]

    normed, unit, own_unit, own_inv = call(
        norm_kernel,
        "norm",
        (
            pltpu.VMEM((slots * dates, width), BF16),
            pltpu.VMEM((slots * dates, width), BF16),
            pltpu.VMEM((slots, rows, width), F32),
            pltpu.VMEM((slots, rows, 128), F32),
        ),
        [SMEM] + [VMEM] * (3 + groups),
        (visible, pos_table, gain2, bias2, *gathered),
        12,
        flops=10**7,
        size=6 * 10**6,
    )
    if chain:
        third = after(third, normed, second_other)
        third_other = swapped(third, "rep", 1)
        pieces = [held, rest, first, first_other, second, second_other, third, third_other]
    else:
        group = lax.axis_index("date")
        mine = [
            lax.dynamic_slice_in_dim(w_qkv, i * channels + group * part, part, 1) for i in range(3)
        ]
        pieces = [lax.all_gather(jnp.concatenate(mine, axis=1), "tile", axis=0, tiled=True)]
    pieces = [near(piece) for piece in pieces]

    results = call(
        functools.partial(attend_kernel, len(pieces), depth),
        "attend",
        (pltpu.VMEM((slots, rows, part), BF16),) * groups
        + (pltpu.VMEM((slots * dates, 3 * part), BF16), pltpu.VMEM((width, 3 * part), BF16)),
        [SMEM] * 2 + [VMEM] * (2 + groups + len(pieces)),
        (ids, live, near(normed), valid_t, *ups, *pieces),
        20,
        flops=3 * 10**9,
        size=10**7,
        scratch=(pltpu.VMEM((slots * dates, 3 * part), BF16),),
    )
    contexts, gqkv, weights = results[:groups], results[groups], results[groups + 1]
    contexts = [contexts[0]] + [swapped(contexts[s], "date", s) for s in range(1, groups)]

    block = pltpu.VMEM((slots, rows, width), BF16)
    stay, passing, cross, sums = call(
        back_kernel,
        "back",
        (block, block, pltpu.VMEM((2, slots, rows, width), BF16), pltpu.VMEM((2, width), F32)),
        [VMEM] * 3,
        (near(gqkv), near(unit), near(weights)),
        12,
        flops=4 * 10**9,
        size=10**7,
    )

    close = swapped(cross, "date", 1)
    close = after(close, *contexts[1:])
    if owners == 4:
        tiles = [sums] + [swapped(sums, "tile", s) for s in range(1, owners)]
    else:
        tiles = [lax.psum(sums, ("date", "tile"))]
    chip, total = call(
        merge_kernel,
        "merge",
        (block, pltpu.VMEM((2, width), F32)),
        [VMEM] * (2 + len(tiles)),
        (passing, close, *tiles),
        6,
    )
    far = swapped(chip, "date", 2)
    totals = [total] + [swapped(total, "date", s) for s in range(1, groups)] if owners == 4 else [total]
    home, attended = call(
        home_kernel,
        "home",
        (pltpu.VMEM((slots, rows, width), F32), jax.ShapeDtypeStruct((slots, rows, channels), BF16)),
        [SMEM] + [VMEM] * (2 + groups),
        (ids, stay, close, *contexts),
        6,
        scratch=(pltpu.VMEM((groups, slots, rows, part), BF16),),
    )
    grad_tokens, grad_norm = call(
        finish_kernel,
        "finish",
        (
            jax.ShapeDtypeStruct((slots, rows, width), BF16),
            jax.ShapeDtypeStruct((2, width), F32),
        ),
        [SMEM] * 2 + [VMEM] * (5 + len(totals)),
        (ids, live, near(own_unit), near(own_inv), gain2, near(home), far, *totals),
        6,
    )
    return attended, grad_tokens, grad_norm


def solution(mesh):
    in_specs = (
        P(("rep", "tile"), "date", None),
        P(("rep", "tile"), "date", None),
        P(("rep", "tile"), None),
        P(("rep", "tile")),
        P("rep"),
        P(),
        P(),
        P(),
        P("tile", None),
    )
    out_specs = (P(("rep", "tile"), "date", None), P(("rep", "tile"), "date", None), P("rep", None))
    return jax.shard_map(local, mesh=mesh, in_specs=in_specs, out_specs=out_specs, check_vma=False)
```

```python
import functools

import jax
import jax.numpy as jnp
from jax import lax
from jax.experimental import pallas as pl
from jax.experimental.pallas import tpu as pltpu
from jax.sharding import PartitionSpec as P

HEAD_DIM = 80
DG = 32
BLOCK_ROWS = 32
F32 = jnp.float32
BF16 = jnp.bfloat16

VMEM = pl.BlockSpec(memory_space=pltpu.VMEM)
SMEM = pl.BlockSpec(memory_space=pltpu.SMEM)
HBM = pl.BlockSpec(memory_space=pltpu.HBM)


def dot(a, b):
    return jnp.dot(a, b, preferred_element_type=F32)


def dot_nt(a, b):
    return lax.dot_general(a, b, (((1,), (1,)), ((), ())), preferred_element_type=F32)


def dot_tn(a, b):
    return lax.dot_general(a, b, (((0,), (0,)), ((), ())), preferred_element_type=F32)


def window_of(group, part):
    wide = -(-part // 128) * 128
    odd = lax.rem(group, 2)
    start = (group // 2) * (2 * part) + odd * (2 * part - wide)
    return start, wide, odd == 1


def pick_kernel(part, other, ids_ref, w_ref, out_ref, windows, sems):
    height = out_ref.shape[0]
    channels = w_ref.shape[1] // 3
    half = 1 - ids_ref[0] if other else ids_ref[0]
    first = pl.multiple_of(half * height, 16)
    start, wide, odd = window_of(ids_ref[1], part)
    moves = [
        pltpu.make_async_copy(
            w_ref.at[pl.ds(first, height), pl.ds(pl.multiple_of(i * channels + start, 128), wide)],
            windows.at[i],
            sems.at[i],
        )
        for i in range(3)
    ]
    for move in moves:
        move.start()
    for move in moves:
        move.wait()
    pieces = []
    for i in range(3):
        window = windows[i]
        pieces.append(jnp.where(odd, window[:, wide - part :], window[:, :part]))
    out_ref[...] = jnp.concatenate(pieces, axis=1)


def columns_kernel(part, ids_ref, cotangent_ref, out_ref):
    theirs = (1 - ids_ref[1] // 2) * (2 * part)
    out_ref[...] = cotangent_ref[:, :, pl.ds(pl.multiple_of(theirs, 128), 2 * part)]


def part_kernel(part, ids_ref, cotangent_ref, columns_ref, up_ref, out_ref):
    ours = pl.multiple_of(ids_ref[1] // 2 * (2 * part), 128)
    odd = lax.rem(ids_ref[1], 2) == 1
    for i, block in enumerate((cotangent_ref[:, :, pl.ds(ours, 2 * part)], columns_ref[...])):
        low, high = block[:, :, :part], block[:, :, part:]
        up_ref[i] = jnp.where(odd, high, low)
        out_ref[i] = jnp.where(odd, low, high)


def norm_kernel(visible_ref, pos_ref, gain_ref, bias_ref, *refs):
    token_refs = refs[:-4]
    normed_ref, unit_ref, own_unit_ref, own_inv_ref = refs[-4:]
    slots, rows, width = token_refs[0].shape
    gain = gain_ref[...]
    bias = bias_ref[...]
    for p in range(slots):
        iota = lax.broadcasted_iota(jnp.int32, (8, pos_ref.shape[0]), 1)
        onehot = (iota == visible_ref[p]).astype(F32).astype(BF16)
        position = dot(onehot, pos_ref[...])[0:1]
        for s, tokens_ref in enumerate(token_refs):
            embedded = (tokens_ref[p].astype(F32) + position).astype(BF16).astype(F32)
            centred = embedded - jnp.mean(embedded, axis=-1, keepdims=True)
            inv_std = lax.rsqrt(jnp.mean(centred * centred, axis=-1, keepdims=True) + 1e-06)
            unit = centred * inv_std
            at = (p * len(token_refs) + s) * rows
            normed_ref[at : at + rows] = (unit * gain + bias).astype(BF16)
            unit_ref[at : at + rows] = unit.astype(BF16)
            if s == 0:
                own_unit_ref[p] = unit
                own_inv_ref[p] = jnp.broadcast_to(inv_std, own_inv_ref.shape[1:])


def piece_rows(ids_ref, count, depth):
    if count == 1:
        return [0]
    rep, owner = ids_ref[0], ids_ref[2]
    owners = count // 2
    share = depth // 2
    spot = owner ^ (owner >> 1)
    firsts = []
    for step in range(owners):
        back = lax.rem(spot + owners - step, owners)
        source = back ^ (back >> 1)
        firsts.append(pl.multiple_of(source * depth + rep * share, 16))
        firsts.append(pl.multiple_of(source * depth + (1 - rep) * share, 16))
    return firsts


def attend_kernel(count, depth, ids_ref, live_ref, normed_ref, valid_ref, up_ref, beside_ref, *refs):
    piece_refs = refs[:count]
    own_ref, close_ref, across_ref, gqkv_ref, weights, qkv_ref = refs[-6:]
    _, slots, rows, channels = up_ref.shape
    dates = valid_ref.shape[1]
    heads = channels // HEAD_DIM
    inv_scale = 1.0 / HEAD_DIM**0.5
    for first, ref in zip(piece_rows(ids_ref, count, depth), piece_refs):
        weights[pl.ds(first, ref.shape[0]), :] = ref[...]
    qkv_ref[...] = dot(normed_ref[...], weights[...]).astype(BF16)
    row = lax.broadcasted_iota(jnp.int32, (dates, dates), 0)
    column = lax.broadcasted_iota(jnp.int32, (dates, dates), 1)
    same_date = column == (row ^ (ids_ref[1] * rows))
    for p in range(slots):
        span = slice(p * dates, (p + 1) * dates)
        alive = (live_ref[ids_ref[2]] > p // (BLOCK_ROWS // DG)).astype(F32)
        rows_qkv = qkv_ref[span, :]
        upstream = [up_ref[0, p], beside_ref[0, p], up_ref[1, p], beside_ref[1, p]]
        upstream = jnp.concatenate(upstream, axis=0) * alive.astype(BF16)
        valid = valid_ref[p : p + 1, :].astype(F32)
        allowed = jnp.sum(jnp.where(same_date, valid, 0.0), axis=1, keepdims=True) > 0
        grads = [[], [], []]
        contexts = []
        for h in range(heads):
            q, k, v = (
                rows_qkv[:, i * channels + h * HEAD_DIM : i * channels + (h + 1) * HEAD_DIM]
                for i in range(3)
            )
            up = upstream[:, h * HEAD_DIM : (h + 1) * HEAD_DIM]
            scores = jnp.where(allowed, dot_nt(k, q) * inv_scale, -1e30)
            exps = jnp.exp(scores - jnp.max(scores, axis=0, keepdims=True))
            probs = exps * (1.0 / jnp.sum(exps, axis=0, keepdims=True))
            low = probs.astype(BF16)
            contexts.append(dot_tn(low, v) * alive)
            grads[2].append(dot(low, up))
            gprobs = dot_nt(v, up)
            gscores = probs * (gprobs - jnp.sum(probs * gprobs, axis=0, keepdims=True)) * inv_scale
            glow = gscores.astype(BF16)
            grads[0].append(dot_tn(glow, k))
            grads[1].append(dot(glow, q))
        gqkv_ref[span, :] = jnp.concatenate(grads[0] + grads[1] + grads[2], axis=1).astype(BF16)
        context = jnp.concatenate(contexts, axis=1).astype(BF16)
        for s, out in enumerate((own_ref, close_ref, across_ref.at[0], across_ref.at[1])):
            out[p] = context[s * rows : (s + 1) * rows]


def back_kernel(gqkv_ref, unit_ref, weights, stay_ref, pass_ref, cross_ref, sums_ref):
    slots, rows, width = stay_ref.shape
    dates = gqkv_ref.shape[0] // slots
    tail = 2 * slots * rows
    step = 256
    for n in range(width // step):
        lanes = slice(n * step, (n + 1) * step)
        partial = dot_nt(gqkv_ref[...], weights[lanes, :])
        low = partial.astype(BF16)
        for p in range(slots):
            for s in range(dates // rows):
                block = low[p * dates + s * rows : p * dates + (s + 1) * rows]
                if s % 2:
                    at = (s // 2 * slots + p) * rows
                    cross_ref[at : at + rows, lanes] = block
                else:
                    (pass_ref if s else stay_ref)[p, :, lanes] = block
        gain_sum = jnp.sum(partial * unit_ref[:, lanes].astype(F32), axis=0, keepdims=True)
        sums = jnp.concatenate([gain_sum, jnp.sum(partial, axis=0, keepdims=True)], axis=0)
        sums_ref[:, lanes] = sums
        high = sums.astype(BF16)
        rest = (sums - high.astype(F32)).astype(BF16)
        fill = jnp.zeros((cross_ref.shape[0] - tail - 4, step), BF16)
        cross_ref[tail:, lanes] = jnp.concatenate([high, rest, fill], axis=0)


def merge_kernel(pass_ref, close_ref, sums_ref, out_ref, total_ref):
    slots, rows, width = out_ref.shape
    for p in range(slots):
        at = (slots + p) * rows
        out_ref[p] = (pass_ref[p].astype(F32) + close_ref[at : at + rows].astype(F32)).astype(BF16)
    sums = close_ref[2 * slots * rows :].astype(F32)
    total_ref[...] = sums_ref[...] + sums[0:2] + sums[2:4]


def both_kernel(close_ref, far_ref, both_ref):
    both_ref[0] = close_ref[...]
    both_ref[1] = far_ref[1]


def add_kernel(*refs):
    total = refs[0][...]
    for ref in refs[1:-1]:
        total = total + ref[...]
    refs[-1][...] = total


def home_kernel(ids_ref, stay_ref, close_ref, own_ref, beside_ref, across_ref, grad_ref, attended_ref, held):
    slots, rows, width = grad_ref.shape
    group = ids_ref[1]
    held[group] = own_ref[...]
    held[group ^ 1] = beside_ref[0]
    held[group ^ 2] = across_ref[0]
    held[group ^ 3] = beside_ref[1]
    for p in range(slots):
        close = close_ref[p * rows : (p + 1) * rows].astype(F32)
        grad_ref[p] = stay_ref[p].astype(F32) + close
        attended_ref[p] = jnp.concatenate([held[g, p] for g in range(held.shape[0])], axis=1)


def finish_kernel(ids_ref, live_ref, unit_ref, inv_ref, gain_ref, grad_ref, far_ref, *refs):
    out_ref, norm_ref = refs[-2:]
    slots = unit_ref.shape[0]
    gain = gain_ref[...]
    for p in range(slots):
        alive = (live_ref[ids_ref[2]] > p // (BLOCK_ROWS // DG)).astype(F32)
        unit = unit_ref[p]
        scaled = (grad_ref[p] + far_ref[p].astype(F32)) * gain
        out = inv_ref[p][:, 0:1] * (
            scaled
            - jnp.mean(scaled, axis=-1, keepdims=True)
            - unit * jnp.mean(scaled * unit, axis=-1, keepdims=True)
        )
        out_ref[p] = (out * alive).astype(BF16)
    total = refs[0][...]
    for ref in refs[1:-2]:
        total = total + ref[...]
    norm_ref[...] = total


def swapped(array, axis, bits):
    return lax.ppermute(array, axis, [(i, i ^ bits) for i in range(lax.axis_size(axis))])


def after(array, *others):
    return lax.optimization_barrier((array, *others))[0]


def near(array):
    return pltpu.with_memory_space_constraint(array, pltpu.VMEM)


def call(kernel, name, out_shape, in_specs, args, megabytes, scratch=()):
    return pl.pallas_call(
        kernel,
        out_shape=out_shape,
        in_specs=in_specs,
        out_specs=jax.tree.map(lambda _: VMEM, out_shape),
        scratch_shapes=list(scratch),
        compiler_params=pltpu.CompilerParams(vmem_limit_bytes=megabytes * 1024 * 1024),
        cost_estimate=pl.CostEstimate(flops=1000, bytes_accessed=1000, transcendentals=0),
        name=name,
    )(*args)


def pick(w_qkv, ids, share, part, other):
    wide = -(-part // 128) * 128
    return call(
        functools.partial(pick_kernel, part, other),
        "pick",
        pltpu.VMEM((share, 3 * part), BF16),
        [SMEM, HBM],
        (ids, pltpu.with_memory_space_constraint(w_qkv, pltpu.HBM)),
        4,
        scratch=(pltpu.VMEM((3, share, wide), BF16), pltpu.SemaphoreType.DMA((3,))),
    )


def local(tokens, cotangent, valid, visible, live, pos_table, norm_gain, norm_bias, w_qkv):
    slots, rows, width = tokens.shape
    groups = lax.axis_size("date")
    owners = lax.axis_size("tile")
    depth, triple = w_qkv.shape
    channels = triple // 3
    part = channels // groups
    dates = rows * groups
    ids = jnp.stack([lax.axis_index(name) for name in ("rep", "date", "tile")]).astype(jnp.int32)
    gain2, bias2 = norm_gain.reshape(1, width), norm_bias.reshape(1, width)

    chain = owners == 4 and lax.axis_size("rep") == 2 and depth % 32 == 0
    ring = [(0, 1), (1, 3), (3, 2), (2, 0)]
    share = depth // 2

    held = pick(w_qkv, ids, share, part, False) if chain else ids
    sooner = after(tokens, held)
    across = swapped(sooner, "date", 2)
    beside = swapped(sooner, "date", 1)
    if chain:
        first = lax.ppermute(held, "tile", ring)
        first = after(first, across, beside)
        second = lax.ppermute(first, "tile", ring)
        first_other = swapped(first, "rep", 1)
        rest = pick(w_qkv, after(ids, first), share, part, True)
    else:
        first = ids
    across = after(across, first)
    beyond = swapped(across, "date", 1)
    pair = pltpu.VMEM((2, slots, rows, part), BF16)
    columns = call(
        functools.partial(columns_kernel, part),
        "columns",
        pltpu.VMEM((slots, rows, 2 * part), BF16),
        [SMEM, VMEM],
        (after(ids, first), cotangent),
        4,
    )
    columns = swapped(columns, "date", 2)
    if chain:
        second = after(second, first_other, beyond, columns, rest)
        third = lax.ppermute(second, "tile", ring)
        second_other = swapped(second, "rep", 1)
        columns = after(columns, second)
    ups, ups_beside = call(
        functools.partial(part_kernel, part),
        "part",
        (pair, pair),
        [SMEM, VMEM, VMEM],
        (ids, cotangent, near(columns)),
        4,
    )
    ups_beside = swapped(ups_beside, "date", 1)

    normed, unit, own_unit, own_inv = call(
        norm_kernel,
        "norm",
        (
            pltpu.VMEM((slots * dates, width), BF16),
            pltpu.VMEM((slots * dates, width), BF16),
            pltpu.VMEM((slots, rows, width), F32),
            pltpu.VMEM((slots, rows, 128), F32),
        ),
        [SMEM] + [VMEM] * (3 + groups),
        (visible, pos_table, gain2, bias2, tokens, near(beside), near(across), near(beyond)),
        12,
    )
    if chain:
        third = after(third, second_other, ups_beside, normed)
        third_other = swapped(third, "rep", 1)
        pieces = [held, rest, first, first_other, second, second_other, third, third_other]
    else:
        group = lax.axis_index("date")
        mine = [
            lax.dynamic_slice_in_dim(w_qkv, i * channels + group * part, part, 1) for i in range(3)
        ]
        pieces = [lax.all_gather(jnp.concatenate(mine, axis=1), "tile", axis=0, tiled=True)]
    pieces = [near(piece) for piece in pieces]

    piece = pltpu.VMEM((slots, rows, part), BF16)
    context, close_context, far_context, gqkv, weights = call(
        functools.partial(attend_kernel, len(pieces), depth),
        "attend",
        (
            piece,
            piece,
            pair,
            pltpu.VMEM((slots * dates, 3 * part), BF16),
            pltpu.VMEM((width, 3 * part), BF16),
        ),
        [SMEM] * 2 + [VMEM] * (4 + len(pieces)),
        (ids, live, near(normed), valid, near(ups), near(ups_beside), *pieces),
        20,
        scratch=(pltpu.VMEM((slots * dates, 3 * part), BF16),),
    )
    far_context = swapped(far_context, "date", 2)

    block = pltpu.VMEM((slots, rows, width), BF16)
    pairs = pltpu.VMEM((2, width), F32)
    stay, passing, cross, sums = call(
        back_kernel,
        "back",
        (block, block, pltpu.VMEM((2 * slots * rows + 16, width), BF16), pairs),
        [VMEM] * 3,
        (near(gqkv), near(unit), near(weights)),
        12,
    )

    close = swapped(cross, "date", 1)
    chip, total = call(
        merge_kernel,
        "merge",
        (block, pairs),
        [VMEM] * 3,
        (near(passing), near(close), near(sums)),
        6,
    )
    far_context = after(far_context, chip)
    both = call(both_kernel, "both", pair, [VMEM] * 2, (near(close_context), near(far_context)), 2)
    far = swapped(chip, "date", 2)
    if owners == 4:
        total = call(
            add_kernel,
            "add",
            pairs,
            [VMEM] * owners,
            [near(total)] + [near(swapped(total, "tile", s)) for s in range(1, owners)],
            2,
        )
    else:
        total = lax.psum(total, "tile")
    far_total = swapped(total, "date", 2)
    both = swapped(both, "date", 1)
    home, attended = call(
        home_kernel,
        "home",
        (pltpu.VMEM((slots, rows, width), F32), jax.ShapeDtypeStruct((slots, rows, channels), BF16)),
        [SMEM] + [VMEM] * 5,
        (ids, near(stay), near(close), near(context), near(both), near(far_context)),
        6,
        scratch=(pltpu.VMEM((groups, slots, rows, part), BF16),),
    )
    grad_tokens, grad_norm = call(
        finish_kernel,
        "finish",
        (
            jax.ShapeDtypeStruct((slots, rows, width), BF16),
            jax.ShapeDtypeStruct((2, width), F32),
        ),
        [SMEM] * 2 + [VMEM] * 7,
        (ids, live, near(own_unit), near(own_inv), gain2, near(home), near(far), total, far_total),
        6,
    )
    return attended, grad_tokens, grad_norm


def solution(mesh):
    in_specs = (
        P(("rep", "tile"), "date", None),
        P(("rep", "tile"), "date", None),
        P(("rep", "tile"), None),
        P(("rep", "tile")),
        P("rep"),
        P(),
        P(),
        P(),
        P("tile", None),
    )
    out_specs = (P(("rep", "tile"), "date", None), P(("rep", "tile"), "date", None), P("rep", None))
    return jax.shard_map(local, mesh=mesh, in_specs=in_specs, out_specs=out_specs, check_vma=False)
```

```python
import functools

import jax
import jax.numpy as jnp
from jax import lax
from jax.experimental import pallas as pl
from jax.experimental.pallas import tpu as pltpu
from jax.sharding import PartitionSpec as P

HEAD_DIM = 80
DG = 32
BLOCK_ROWS = 32
F32 = jnp.float32
BF16 = jnp.bfloat16

VMEM = pl.BlockSpec(memory_space=pltpu.VMEM)
SMEM = pl.BlockSpec(memory_space=pltpu.SMEM)
HBM = pl.BlockSpec(memory_space=pltpu.HBM)


def dot(a, b):
    return jnp.dot(a, b, preferred_element_type=F32)


def dot_nt(a, b):
    return lax.dot_general(a, b, (((1,), (1,)), ((), ())), preferred_element_type=F32)


def dot_tn(a, b):
    return lax.dot_general(a, b, (((0,), (0,)), ((), ())), preferred_element_type=F32)


def window_of(group, part):
    wide = -(-part // 128) * 128
    odd = lax.rem(group, 2)
    start = (group // 2) * (2 * part) + odd * (2 * part - wide)
    return start, wide, odd == 1


def pick_kernel(part, other, ids_ref, w_ref, out_ref, windows, sems):
    height = out_ref.shape[0]
    channels = w_ref.shape[1] // 3
    half = 1 - ids_ref[0] if other else ids_ref[0]
    first = pl.multiple_of(half * height, 16)
    start, wide, odd = window_of(ids_ref[1], part)
    moves = [
        pltpu.make_async_copy(
            w_ref.at[pl.ds(first, height), pl.ds(pl.multiple_of(i * channels + start, 128), wide)],
            windows.at[i],
            sems.at[i],
        )
        for i in range(3)
    ]
    for move in moves:
        move.start()
    for move in moves:
        move.wait()
    pieces = []
    for i in range(3):
        window = windows[i]
        pieces.append(jnp.where(odd, window[:, wide - part :], window[:, :part]))
    out_ref[...] = jnp.concatenate(pieces, axis=1)


def columns_kernel(part, ids_ref, cotangent_ref, out_ref):
    theirs = (1 - ids_ref[1] // 2) * (2 * part)
    out_ref[...] = cotangent_ref[:, :, pl.ds(pl.multiple_of(theirs, 128), 2 * part)]


def part_kernel(part, ids_ref, cotangent_ref, columns_ref, up_ref, out_ref):
    ours = pl.multiple_of(ids_ref[1] // 2 * (2 * part), 128)
    odd = lax.rem(ids_ref[1], 2) == 1
    for i, block in enumerate((cotangent_ref[:, :, pl.ds(ours, 2 * part)], columns_ref[...])):
        low, high = block[:, :, :part], block[:, :, part:]
        up_ref[i] = jnp.where(odd, high, low)
        out_ref[i] = jnp.where(odd, low, high)


def norm_kernel(visible_ref, pos_ref, gain_ref, bias_ref, *refs):
    token_refs = refs[:-4]
    normed_ref, unit_ref, own_unit_ref, own_inv_ref = refs[-4:]
    slots, rows, width = token_refs[0].shape
    gain = gain_ref[...]
    bias = bias_ref[...]
    for p in range(slots):
        iota = lax.broadcasted_iota(jnp.int32, (8, pos_ref.shape[0]), 1)
        onehot = (iota == visible_ref[p]).astype(F32).astype(BF16)
        position = dot(onehot, pos_ref[...])[0:1]
        for s, tokens_ref in enumerate(token_refs):
            embedded = (tokens_ref[p].astype(F32) + position).astype(BF16).astype(F32)
            centred = embedded - jnp.mean(embedded, axis=-1, keepdims=True)
            inv_std = lax.rsqrt(jnp.mean(centred * centred, axis=-1, keepdims=True) + 1e-06)
            unit = centred * inv_std
            at = (p * len(token_refs) + s) * rows
            normed_ref[at : at + rows] = (unit * gain + bias).astype(BF16)
            unit_ref[at : at + rows] = unit.astype(BF16)
            if s == 0:
                own_unit_ref[p] = unit
                own_inv_ref[p] = jnp.broadcast_to(inv_std, own_inv_ref.shape[1:])


def piece_rows(ids_ref, count, depth):
    if count == 1:
        return [0]
    rep, owner = ids_ref[0], ids_ref[2]
    owners = count // 2
    share = depth // 2
    spot = owner ^ (owner >> 1)
    firsts = []
    for step in (0, 1, 3, 2):
        back = lax.rem(spot + owners - step, owners)
        source = back ^ (back >> 1)
        firsts.append(pl.multiple_of(source * depth + rep * share, 16))
        firsts.append(pl.multiple_of(source * depth + (1 - rep) * share, 16))
    return firsts


def attend_kernel(count, depth, ids_ref, live_ref, normed_ref, valid_ref, up_ref, beside_ref, *refs):
    piece_refs = refs[:count]
    own_ref, close_ref, across_ref, gqkv_ref, weights, qkv_ref = refs[-6:]
    _, slots, rows, channels = up_ref.shape
    dates = valid_ref.shape[1]
    heads = channels // HEAD_DIM
    inv_scale = 1.0 / HEAD_DIM**0.5
    for first, ref in zip(piece_rows(ids_ref, count, depth), piece_refs):
        weights[pl.ds(first, ref.shape[0]), :] = ref[...]
    qkv_ref[...] = dot(normed_ref[...], weights[...]).astype(BF16)
    row = lax.broadcasted_iota(jnp.int32, (dates, dates), 0)
    column = lax.broadcasted_iota(jnp.int32, (dates, dates), 1)
    same_date = column == (row ^ (ids_ref[1] * rows))
    for p in range(slots):
        span = slice(p * dates, (p + 1) * dates)
        alive = (live_ref[ids_ref[2]] > p // (BLOCK_ROWS // DG)).astype(F32)
        rows_qkv = qkv_ref[span, :]
        upstream = [up_ref[0, p], beside_ref[0, p], up_ref[1, p], beside_ref[1, p]]
        upstream = jnp.concatenate(upstream, axis=0) * alive.astype(BF16)
        valid = valid_ref[p : p + 1, :].astype(F32)
        allowed = jnp.sum(jnp.where(same_date, valid, 0.0), axis=1, keepdims=True) > 0
        grads = [[], [], []]
        contexts = []
        for h in range(heads):
            q, k, v = (
                rows_qkv[:, i * channels + h * HEAD_DIM : i * channels + (h + 1) * HEAD_DIM]
                for i in range(3)
            )
            up = upstream[:, h * HEAD_DIM : (h + 1) * HEAD_DIM]
            scores = jnp.where(allowed, dot_nt(k, q) * inv_scale, -1e30)
            exps = jnp.exp(scores - jnp.max(scores, axis=0, keepdims=True))
            probs = exps * (1.0 / jnp.sum(exps, axis=0, keepdims=True))
            low = probs.astype(BF16)
            contexts.append(dot_tn(low, v) * alive)
            grads[2].append(dot(low, up))
            gprobs = dot_nt(v, up)
            gscores = probs * (gprobs - jnp.sum(probs * gprobs, axis=0, keepdims=True)) * inv_scale
            glow = gscores.astype(BF16)
            grads[0].append(dot_tn(glow, k))
            grads[1].append(dot(glow, q))
        gqkv_ref[span, :] = jnp.concatenate(grads[0] + grads[1] + grads[2], axis=1).astype(BF16)
        context = jnp.concatenate(contexts, axis=1).astype(BF16)
        for s, out in enumerate((own_ref, close_ref, across_ref.at[0], across_ref.at[1])):
            out[p] = context[s * rows : (s + 1) * rows]


def back_kernel(gqkv_ref, unit_ref, weights, stay_ref, pass_ref, cross_ref, sums_ref):
    slots, rows, width = stay_ref.shape
    dates = gqkv_ref.shape[0] // slots
    tail = 2 * slots * rows
    step = 256
    for n in range(width // step):
        lanes = slice(n * step, (n + 1) * step)
        partial = dot_nt(gqkv_ref[...], weights[lanes, :])
        low = partial.astype(BF16)
        for p in range(slots):
            for s in range(dates // rows):
                block = low[p * dates + s * rows : p * dates + (s + 1) * rows]
                if s % 2:
                    at = (s // 2 * slots + p) * rows
                    cross_ref[at : at + rows, lanes] = block
                else:
                    (pass_ref if s else stay_ref)[p, :, lanes] = block
        gain_sum = jnp.sum(partial * unit_ref[:, lanes].astype(F32), axis=0, keepdims=True)
        sums = jnp.concatenate([gain_sum, jnp.sum(partial, axis=0, keepdims=True)], axis=0)
        sums_ref[:, lanes] = sums
        high = sums.astype(BF16)
        rest = (sums - high.astype(F32)).astype(BF16)
        fill = jnp.zeros((cross_ref.shape[0] - tail - 4, step), BF16)
        cross_ref[tail:, lanes] = jnp.concatenate([high, rest, fill], axis=0)


def merge_kernel(pass_ref, close_ref, sums_ref, out_ref, total_ref):
    slots, rows, width = out_ref.shape
    for p in range(slots):
        at = (slots + p) * rows
        out_ref[p] = (pass_ref[p].astype(F32) + close_ref[at : at + rows].astype(F32)).astype(BF16)
    sums = close_ref[2 * slots * rows :].astype(F32)
    total_ref[...] = sums_ref[...] + sums[0:2] + sums[2:4]


def both_kernel(close_ref, far_ref, both_ref):
    both_ref[0] = close_ref[...]
    both_ref[1] = far_ref[1]


def add_kernel(*refs):
    total = refs[0][...]
    for ref in refs[1:-1]:
        total = total + ref[...]
    refs[-1][...] = total


def home_kernel(ids_ref, stay_ref, close_ref, own_ref, beside_ref, across_ref, grad_ref, attended_ref, held):
    slots, rows, width = grad_ref.shape
    group = ids_ref[1]
    held[group] = own_ref[...]
    held[group ^ 1] = beside_ref[0]
    held[group ^ 2] = across_ref[0]
    held[group ^ 3] = beside_ref[1]
    for p in range(slots):
        close = close_ref[p * rows : (p + 1) * rows].astype(F32)
        grad_ref[p] = stay_ref[p].astype(F32) + close
        attended_ref[p] = jnp.concatenate([held[g, p] for g in range(held.shape[0])], axis=1)


def finish_kernel(ids_ref, live_ref, unit_ref, inv_ref, gain_ref, grad_ref, far_ref, *refs):
    out_ref, norm_ref = refs[-2:]
    slots = unit_ref.shape[0]
    gain = gain_ref[...]
    for p in range(slots):
        alive = (live_ref[ids_ref[2]] > p // (BLOCK_ROWS // DG)).astype(F32)
        unit = unit_ref[p]
        scaled = (grad_ref[p] + far_ref[p].astype(F32)) * gain
        out = inv_ref[p][:, 0:1] * (
            scaled
            - jnp.mean(scaled, axis=-1, keepdims=True)
            - unit * jnp.mean(scaled * unit, axis=-1, keepdims=True)
        )
        out_ref[p] = (out * alive).astype(BF16)
    total = refs[0][...]
    for ref in refs[1:-2]:
        total = total + ref[...]
    norm_ref[...] = total


def swapped(array, axis, bits):
    return lax.ppermute(array, axis, [(i, i ^ bits) for i in range(lax.axis_size(axis))])


def after(array, *others):
    return lax.optimization_barrier((array, *others))[0]


def near(array):
    return pltpu.with_memory_space_constraint(array, pltpu.VMEM)


def call(kernel, name, out_shape, in_specs, args, megabytes, scratch=(), microseconds=0.01):
    return pl.pallas_call(
        kernel,
        out_shape=out_shape,
        in_specs=in_specs,
        out_specs=jax.tree.map(lambda _: VMEM, out_shape),
        scratch_shapes=list(scratch),
        compiler_params=pltpu.CompilerParams(vmem_limit_bytes=megabytes * 1024 * 1024),
        cost_estimate=pl.CostEstimate(
            flops=int(microseconds * 10**9), bytes_accessed=1000, transcendentals=0
        ),
        name=name,
    )(*args)


def pick(w_qkv, ids, share, part, other):
    wide = -(-part // 128) * 128
    return call(
        functools.partial(pick_kernel, part, other),
        "pick",
        pltpu.VMEM((share, 3 * part), BF16),
        [SMEM, HBM],
        (ids, pltpu.with_memory_space_constraint(w_qkv, pltpu.HBM)),
        4,
        scratch=(pltpu.VMEM((3, share, wide), BF16), pltpu.SemaphoreType.DMA((3,))),
    )


def local(tokens, cotangent, valid, visible, live, pos_table, norm_gain, norm_bias, w_qkv):
    slots, rows, width = tokens.shape
    groups = lax.axis_size("date")
    owners = lax.axis_size("tile")
    depth, triple = w_qkv.shape
    channels = triple // 3
    part = channels // groups
    dates = rows * groups
    ids = jnp.stack([lax.axis_index(name) for name in ("rep", "date", "tile")]).astype(jnp.int32)
    gain2, bias2 = norm_gain.reshape(1, width), norm_bias.reshape(1, width)

    chain = owners == 4 and lax.axis_size("rep") == 2 and depth % 32 == 0
    ring = [(0, 1), (1, 3), (3, 2), (2, 0)]
    share = depth // 2

    held = pick(w_qkv, ids, share, part, False) if chain else ids
    sooner = after(tokens, held)
    across = swapped(sooner, "date", 2)
    beside = swapped(sooner, "date", 1)
    if chain:
        first = lax.ppermute(held, "tile", ring)
        third = lax.ppermute(held, "tile", [(b, a) for a, b in ring])
        first = after(first, across, beside)
        second = lax.ppermute(first, "tile", ring)
        first_other = swapped(first, "rep", 1)
        third_other = swapped(third, "rep", 1)
        rest = pick(w_qkv, after(ids, first), share, part, True)
    else:
        first = ids
    across = after(across, first)
    beyond = swapped(across, "date", 1)
    pair = pltpu.VMEM((2, slots, rows, part), BF16)
    columns = call(
        functools.partial(columns_kernel, part),
        "columns",
        pltpu.VMEM((slots, rows, 2 * part), BF16),
        [SMEM, VMEM],
        (after(ids, first), cotangent),
        4,
    )
    columns = swapped(columns, "date", 2)
    if chain:
        second = after(second, first_other, beyond, columns, rest)
        second_other = swapped(second, "rep", 1)
        columns = after(columns, second)
    ups, ups_beside = call(
        functools.partial(part_kernel, part),
        "part",
        (pair, pair),
        [SMEM, VMEM, VMEM],
        (ids, cotangent, near(columns)),
        4,
    )
    ups_beside = swapped(ups_beside, "date", 1)
    if chain:
        beyond = after(beyond, third_other)

    normed, unit, own_unit, own_inv = call(
        norm_kernel,
        "norm",
        (
            pltpu.VMEM((slots * dates, width), BF16),
            pltpu.VMEM((slots * dates, width), BF16),
            pltpu.VMEM((slots, rows, width), F32),
            pltpu.VMEM((slots, rows, 128), F32),
        ),
        [SMEM] + [VMEM] * (3 + groups),
        (visible, pos_table, gain2, bias2, tokens, near(beside), near(across), near(beyond)),
        12,
        microseconds=2,
    )
    if chain:
        pieces = [held, rest, first, first_other, third, third_other, second, second_other]
    else:
        group = lax.axis_index("date")
        mine = [
            lax.dynamic_slice_in_dim(w_qkv, i * channels + group * part, part, 1) for i in range(3)
        ]
        pieces = [lax.all_gather(jnp.concatenate(mine, axis=1), "tile", axis=0, tiled=True)]
    pieces = [near(piece) for piece in pieces]

    piece = pltpu.VMEM((slots, rows, part), BF16)
    context, close_context, far_context, gqkv, weights = call(
        functools.partial(attend_kernel, len(pieces), depth),
        "attend",
        (
            piece,
            piece,
            pair,
            pltpu.VMEM((slots * dates, 3 * part), BF16),
            pltpu.VMEM((width, 3 * part), BF16),
        ),
        [SMEM] * 2 + [VMEM] * (4 + len(pieces)),
        (ids, live, near(normed), valid, near(ups), near(ups_beside), *pieces),
        20,
        scratch=(pltpu.VMEM((slots * dates, 3 * part), BF16),),
    )
    far_context = swapped(far_context, "date", 2)

    block = pltpu.VMEM((slots, rows, width), BF16)
    pairs = pltpu.VMEM((2, width), F32)
    stay, passing, cross, sums = call(
        back_kernel,
        "back",
        (block, block, pltpu.VMEM((2 * slots * rows + 16, width), BF16), pairs),
        [VMEM] * 3,
        (near(gqkv), near(unit), near(weights)),
        12,
    )

    close = swapped(cross, "date", 1)
    both = call(
        both_kernel,
        "both",
        pair,
        [VMEM] * 2,
        (near(close_context), near(far_context)),
        2,
        microseconds=10,
    )
    close = after(close, both)
    chip, total = call(
        merge_kernel,
        "merge",
        (block, pairs),
        [VMEM] * 3,
        (near(passing), near(close), near(sums)),
        6,
    )
    far = swapped(chip, "date", 2)
    if owners == 4:
        total = call(
            add_kernel,
            "add",
            pairs,
            [VMEM] * owners,
            [near(total)] + [near(swapped(total, "tile", s)) for s in range(1, owners)],
            2,
        )
    else:
        total = lax.psum(total, "tile")
    far_total = swapped(total, "date", 2)
    both = swapped(both, "date", 1)
    home, attended = call(
        home_kernel,
        "home",
        (pltpu.VMEM((slots, rows, width), F32), jax.ShapeDtypeStruct((slots, rows, channels), BF16)),
        [SMEM] + [VMEM] * 5,
        (ids, near(stay), near(close), near(context), near(both), near(far_context)),
        6,
        scratch=(pltpu.VMEM((groups, slots, rows, part), BF16),),
    )
    grad_tokens, grad_norm = call(
        finish_kernel,
        "finish",
        (
            jax.ShapeDtypeStruct((slots, rows, width), BF16),
            jax.ShapeDtypeStruct((2, width), F32),
        ),
        [SMEM] * 2 + [VMEM] * 7,
        (ids, live, near(own_unit), near(own_inv), gain2, near(home), near(far), total, far_total),
        6,
    )
    return attended, grad_tokens, grad_norm


def solution(mesh):
    in_specs = (
        P(("rep", "tile"), "date", None),
        P(("rep", "tile"), "date", None),
        P(("rep", "tile"), None),
        P(("rep", "tile")),
        P("rep"),
        P(),
        P(),
        P(),
        P("tile", None),
    )
    out_specs = (P(("rep", "tile"), "date", None), P(("rep", "tile"), "date", None), P("rep", None))
    return jax.shard_map(local, mesh=mesh, in_specs=in_specs, out_specs=out_specs, check_vma=False)
```

```python
import functools

import jax
import jax.numpy as jnp
from jax import lax
from jax.experimental import pallas as pl
from jax.experimental.pallas import tpu as pltpu
from jax.sharding import PartitionSpec as P

HEAD_DIM = 80
DG = 32
BLOCK_ROWS = 32
F32 = jnp.float32
BF16 = jnp.bfloat16

VMEM = pl.BlockSpec(memory_space=pltpu.VMEM)
SMEM = pl.BlockSpec(memory_space=pltpu.SMEM)
HBM = pl.BlockSpec(memory_space=pltpu.HBM)


def dot(a, b):
    return jnp.dot(a, b, preferred_element_type=F32)


def dot_nt(a, b):
    return lax.dot_general(a, b, (((1,), (1,)), ((), ())), preferred_element_type=F32)


def dot_tn(a, b):
    return lax.dot_general(a, b, (((0,), (0,)), ((), ())), preferred_element_type=F32)


def window_of(group, part):
    wide = -(-part // 128) * 128
    odd = lax.rem(group, 2)
    start = (group // 2) * (2 * part) + odd * (2 * part - wide)
    return start, wide, odd == 1


def pick_kernel(part, other, ids_ref, w_ref, out_ref, windows, sems):
    height = out_ref.shape[0]
    channels = w_ref.shape[1] // 3
    half = 1 - ids_ref[0] if other else ids_ref[0]
    first = pl.multiple_of(half * height, 16)
    start, wide, odd = window_of(ids_ref[1], part)
    moves = [
        pltpu.make_async_copy(
            w_ref.at[pl.ds(first, height), pl.ds(pl.multiple_of(i * channels + start, 128), wide)],
            windows.at[i],
            sems.at[i],
        )
        for i in range(3)
    ]
    for move in moves:
        move.start()
    for move in moves:
        move.wait()
    pieces = []
    for i in range(3):
        window = windows[i]
        pieces.append(jnp.where(odd, window[:, wide - part :], window[:, :part]))
    out_ref[...] = jnp.concatenate(pieces, axis=1)


def columns_kernel(part, ids_ref, cotangent_ref, out_ref):
    theirs = (1 - ids_ref[1] // 2) * (2 * part)
    out_ref[...] = cotangent_ref[:, :, pl.ds(pl.multiple_of(theirs, 128), 2 * part)]


def part_kernel(part, ids_ref, cotangent_ref, columns_ref, up_ref, out_ref):
    ours = pl.multiple_of(ids_ref[1] // 2 * (2 * part), 128)
    odd = lax.rem(ids_ref[1], 2) == 1
    for i, block in enumerate((cotangent_ref[:, :, pl.ds(ours, 2 * part)], columns_ref[...])):
        low, high = block[:, :, :part], block[:, :, part:]
        up_ref[i] = jnp.where(odd, high, low)
        out_ref[i] = jnp.where(odd, low, high)


def norm_kernel(visible_ref, pos_ref, gain_ref, bias_ref, *refs):
    token_refs = refs[:-4]
    normed_ref, unit_ref, own_unit_ref, own_inv_ref = refs[-4:]
    slots, rows, width = token_refs[0].shape
    gain = gain_ref[...]
    bias = bias_ref[...]
    for p in range(slots):
        iota = lax.broadcasted_iota(jnp.int32, (8, pos_ref.shape[0]), 1)
        onehot = (iota == visible_ref[p]).astype(F32).astype(BF16)
        position = dot(onehot, pos_ref[...])[0:1]
        for s, tokens_ref in enumerate(token_refs):
            embedded = (tokens_ref[p].astype(F32) + position).astype(BF16).astype(F32)
            centred = embedded - jnp.mean(embedded, axis=-1, keepdims=True)
            inv_std = lax.rsqrt(jnp.mean(centred * centred, axis=-1, keepdims=True) + 1e-06)
            unit = centred * inv_std
            at = (p * len(token_refs) + s) * rows
            normed_ref[at : at + rows] = (unit * gain + bias).astype(BF16)
            unit_ref[at : at + rows] = unit.astype(BF16)
            if s == 0:
                own_unit_ref[p] = unit
                own_inv_ref[p] = jnp.broadcast_to(inv_std, own_inv_ref.shape[1:])


def piece_rows(ids_ref, count, depth):
    if count == 1:
        return [0]
    rep, owner = ids_ref[0], ids_ref[2]
    owners = count // 2
    share = depth // 2
    spot = owner ^ (owner >> 1)
    firsts = []
    for step in range(owners):
        back = lax.rem(spot + owners - step, owners)
        source = back ^ (back >> 1)
        firsts.append(pl.multiple_of(source * depth + rep * share, 16))
        firsts.append(pl.multiple_of(source * depth + (1 - rep) * share, 16))
    return firsts


def attend_kernel(count, depth, ids_ref, live_ref, normed_ref, valid_ref, up_ref, beside_ref, *refs):
    piece_refs = refs[:count]
    own_ref, close_ref, across_ref, gqkv_ref, weights, qkv_ref = refs[-6:]
    _, slots, rows, channels = up_ref.shape
    dates = valid_ref.shape[1]
    heads = channels // HEAD_DIM
    inv_scale = 1.0 / HEAD_DIM**0.5
    for first, ref in zip(piece_rows(ids_ref, count, depth), piece_refs):
        weights[pl.ds(first, ref.shape[0]), :] = ref[...]
    qkv_ref[...] = dot(normed_ref[...], weights[...]).astype(BF16)
    row = lax.broadcasted_iota(jnp.int32, (dates, dates), 0)
    column = lax.broadcasted_iota(jnp.int32, (dates, dates), 1)
    same_date = column == (row ^ (ids_ref[1] * rows))
    for p in range(slots):
        span = slice(p * dates, (p + 1) * dates)
        alive = (live_ref[ids_ref[2]] > p // (BLOCK_ROWS // DG)).astype(F32)
        rows_qkv = qkv_ref[span, :]
        upstream = [up_ref[0, p], beside_ref[0, p], up_ref[1, p], beside_ref[1, p]]
        upstream = jnp.concatenate(upstream, axis=0) * alive.astype(BF16)
        valid = valid_ref[p : p + 1, :].astype(F32)
        allowed = jnp.sum(jnp.where(same_date, valid, 0.0), axis=1, keepdims=True) > 0
        grads = [[], [], []]
        contexts = []
        for h in range(heads):
            q, k, v = (
                rows_qkv[:, i * channels + h * HEAD_DIM : i * channels + (h + 1) * HEAD_DIM]
                for i in range(3)
            )
            up = upstream[:, h * HEAD_DIM : (h + 1) * HEAD_DIM]
            scores = jnp.where(allowed, dot_nt(k, q) * inv_scale, -1e30)
            exps = jnp.exp(scores - jnp.max(scores, axis=0, keepdims=True))
            probs = exps * (1.0 / jnp.sum(exps, axis=0, keepdims=True))
            low = probs.astype(BF16)
            contexts.append(dot_tn(low, v) * alive)
            grads[2].append(dot(low, up))
            gprobs = dot_nt(v, up)
            gscores = probs * (gprobs - jnp.sum(probs * gprobs, axis=0, keepdims=True)) * inv_scale
            glow = gscores.astype(BF16)
            grads[0].append(dot_tn(glow, k))
            grads[1].append(dot(glow, q))
        gqkv_ref[span, :] = jnp.concatenate(grads[0] + grads[1] + grads[2], axis=1).astype(BF16)
        context = jnp.concatenate(contexts, axis=1).astype(BF16)
        for s, out in enumerate((own_ref, close_ref, across_ref.at[0], across_ref.at[1])):
            out[p] = context[s * rows : (s + 1) * rows]


def back_kernel(gqkv_ref, unit_ref, weights, stay_ref, pass_ref, cross_ref, sums_ref):
    slots, rows, width = stay_ref.shape
    dates = gqkv_ref.shape[0] // slots
    tail = 2 * slots * rows
    step = 256
    for n in range(width // step):
        lanes = slice(n * step, (n + 1) * step)
        partial = dot_nt(gqkv_ref[...], weights[lanes, :])
        low = partial.astype(BF16)
        for p in range(slots):
            for s in range(dates // rows):
                block = low[p * dates + s * rows : p * dates + (s + 1) * rows]
                if s % 2:
                    at = (s // 2 * slots + p) * rows
                    cross_ref[at : at + rows, lanes] = block
                else:
                    (pass_ref if s else stay_ref)[p, :, lanes] = block
        gain_sum = jnp.sum(partial * unit_ref[:, lanes].astype(F32), axis=0, keepdims=True)
        sums = jnp.concatenate([gain_sum, jnp.sum(partial, axis=0, keepdims=True)], axis=0)
        sums_ref[:, lanes] = sums
        high = sums.astype(BF16)
        rest = (sums - high.astype(F32)).astype(BF16)
        fill = jnp.zeros((cross_ref.shape[0] - tail - 4, step), BF16)
        cross_ref[tail:, lanes] = jnp.concatenate([high, rest, fill], axis=0)


def merge_kernel(pass_ref, close_ref, sums_ref, out_ref, total_ref):
    slots, rows, width = out_ref.shape
    for p in range(slots):
        at = (slots + p) * rows
        out_ref[p] = (pass_ref[p].astype(F32) + close_ref[at : at + rows].astype(F32)).astype(BF16)
    sums = close_ref[2 * slots * rows :].astype(F32)
    total_ref[...] = sums_ref[...] + sums[0:2] + sums[2:4]


def both_kernel(close_ref, far_ref, both_ref):
    both_ref[0] = close_ref[...]
    both_ref[1] = far_ref[1]


def add_kernel(*refs):
    total = refs[0][...]
    for ref in refs[1:-1]:
        total = total + ref[...]
    refs[-1][...] = total


def home_kernel(ids_ref, stay_ref, close_ref, own_ref, beside_ref, across_ref, grad_ref, attended_ref, held):
    slots, rows, width = grad_ref.shape
    group = ids_ref[1]
    held[group] = own_ref[...]
    held[group ^ 1] = beside_ref[0]
    held[group ^ 2] = across_ref[0]
    held[group ^ 3] = beside_ref[1]
    for p in range(slots):
        close = close_ref[p * rows : (p + 1) * rows].astype(F32)
        grad_ref[p] = stay_ref[p].astype(F32) + close
        attended_ref[p] = jnp.concatenate([held[g, p] for g in range(held.shape[0])], axis=1)


def finish_kernel(ids_ref, live_ref, unit_ref, inv_ref, gain_ref, grad_ref, far_ref, *refs):
    out_ref, norm_ref = refs[-2:]
    slots = unit_ref.shape[0]
    gain = gain_ref[...]
    for p in range(slots):
        alive = (live_ref[ids_ref[2]] > p // (BLOCK_ROWS // DG)).astype(F32)
        unit = unit_ref[p]
        scaled = (grad_ref[p] + far_ref[p].astype(F32)) * gain
        out = inv_ref[p][:, 0:1] * (
            scaled
            - jnp.mean(scaled, axis=-1, keepdims=True)
            - unit * jnp.mean(scaled * unit, axis=-1, keepdims=True)
        )
        out_ref[p] = (out * alive).astype(BF16)
    total = refs[0][...]
    for ref in refs[1:-2]:
        total = total + ref[...]
    norm_ref[...] = total


def swapped(array, axis, bits):
    return lax.ppermute(array, axis, [(i, i ^ bits) for i in range(lax.axis_size(axis))])


def after(array, *others):
    return lax.optimization_barrier((array, *others))[0]


def near(array):
    return pltpu.with_memory_space_constraint(array, pltpu.VMEM)


def call(kernel, name, out_shape, in_specs, args, megabytes, scratch=(), microseconds=0.01):
    return pl.pallas_call(
        kernel,
        out_shape=out_shape,
        in_specs=in_specs,
        out_specs=jax.tree.map(lambda _: VMEM, out_shape),
        scratch_shapes=list(scratch),
        compiler_params=pltpu.CompilerParams(vmem_limit_bytes=megabytes * 1024 * 1024),
        cost_estimate=pl.CostEstimate(
            flops=int(microseconds * 10**9), bytes_accessed=1000, transcendentals=0
        ),
        name=name,
    )(*args)


def pick(w_qkv, ids, share, part, other):
    wide = -(-part // 128) * 128
    return call(
        functools.partial(pick_kernel, part, other),
        "pick",
        pltpu.VMEM((share, 3 * part), BF16),
        [SMEM, HBM],
        (ids, pltpu.with_memory_space_constraint(w_qkv, pltpu.HBM)),
        4,
        scratch=(pltpu.VMEM((3, share, wide), BF16), pltpu.SemaphoreType.DMA((3,))),
    )


def local(tokens, cotangent, valid, visible, live, pos_table, norm_gain, norm_bias, w_qkv):
    slots, rows, width = tokens.shape
    groups = lax.axis_size("date")
    owners = lax.axis_size("tile")
    depth, triple = w_qkv.shape
    channels = triple // 3
    part = channels // groups
    dates = rows * groups
    ids = jnp.stack([lax.axis_index(name) for name in ("rep", "date", "tile")]).astype(jnp.int32)
    gain2, bias2 = norm_gain.reshape(1, width), norm_bias.reshape(1, width)

    chain = owners == 4 and lax.axis_size("rep") == 2 and depth % 32 == 0
    ring = [(0, 1), (1, 3), (3, 2), (2, 0)]
    share = depth // 2

    if chain:
        held = pick(w_qkv, ids, share, part, False)
        first = lax.ppermute(held, "tile", ring)
        second = lax.ppermute(first, "tile", ring)
        first_other = swapped(first, "rep", 1)
        rest = pick(w_qkv, after(ids, first), share, part, True)
        second = after(second, first_other, rest)
        third = lax.ppermute(second, "tile", ring)
        second_other = swapped(second, "rep", 1)
        third = after(third, second_other)
        third_other = swapped(third, "rep", 1)
    else:
        first = second = ids

    sooner = after(tokens, first)
    across = swapped(sooner, "date", 2)
    beside = swapped(sooner, "date", 1)
    beyond = swapped(after(across, second), "date", 1)
    pair = pltpu.VMEM((2, slots, rows, part), BF16)
    columns = call(
        functools.partial(columns_kernel, part),
        "columns",
        pltpu.VMEM((slots, rows, 2 * part), BF16),
        [SMEM, VMEM],
        (after(ids, first), cotangent),
        4,
    )
    columns = swapped(columns, "date", 2)
    ups, ups_beside = call(
        functools.partial(part_kernel, part),
        "part",
        (pair, pair),
        [SMEM, VMEM, VMEM],
        (ids, cotangent, near(columns)),
        4,
        microseconds=2,
    )
    ups_beside = swapped(ups_beside, "date", 1)

    normed, unit, own_unit, own_inv = call(
        norm_kernel,
        "norm",
        (
            pltpu.VMEM((slots * dates, width), BF16),
            pltpu.VMEM((slots * dates, width), BF16),
            pltpu.VMEM((slots, rows, width), F32),
            pltpu.VMEM((slots, rows, 128), F32),
        ),
        [SMEM] + [VMEM] * (3 + groups),
        (visible, pos_table, gain2, bias2, tokens, near(beside), near(across), near(beyond)),
        12,
        microseconds=2,
    )
    if chain:
        pieces = [held, rest, first, first_other, second, second_other, third, third_other]
    else:
        group = lax.axis_index("date")
        mine = [
            lax.dynamic_slice_in_dim(w_qkv, i * channels + group * part, part, 1) for i in range(3)
        ]
        pieces = [lax.all_gather(jnp.concatenate(mine, axis=1), "tile", axis=0, tiled=True)]
    pieces = [near(piece) for piece in pieces]

    piece = pltpu.VMEM((slots, rows, part), BF16)
    context, close_context, far_context, gqkv, weights = call(
        functools.partial(attend_kernel, len(pieces), depth),
        "attend",
        (
            piece,
            piece,
            pair,
            pltpu.VMEM((slots * dates, 3 * part), BF16),
            pltpu.VMEM((width, 3 * part), BF16),
        ),
        [SMEM] * 2 + [VMEM] * (4 + len(pieces)),
        (ids, live, near(normed), valid, near(ups), near(ups_beside), *pieces),
        20,
        scratch=(pltpu.VMEM((slots * dates, 3 * part), BF16),),
    )
    far_context = swapped(far_context, "date", 2)

    block = pltpu.VMEM((slots, rows, width), BF16)
    pairs = pltpu.VMEM((2, width), F32)
    stay, passing, cross, sums = call(
        back_kernel,
        "back",
        (block, block, pltpu.VMEM((2 * slots * rows + 16, width), BF16), pairs),
        [VMEM] * 3,
        (near(gqkv), near(unit), near(weights)),
        12,
    )

    close = swapped(cross, "date", 1)
    both = call(
        both_kernel,
        "both",
        pair,
        [VMEM] * 2,
        (near(close_context), near(far_context)),
        2,
        microseconds=10,
    )
    close = after(close, both)
    chip, total = call(
        merge_kernel,
        "merge",
        (block, pairs),
        [VMEM] * 3,
        (near(passing), near(close), near(sums)),
        6,
    )
    far = swapped(chip, "date", 2)
    if owners == 4:
        total = call(
            add_kernel,
            "add",
            pairs,
            [VMEM] * owners,
            [near(total)] + [near(swapped(total, "tile", s)) for s in range(1, owners)],
            2,
        )
    else:
        total = lax.psum(total, "tile")
    far_total = swapped(total, "date", 2)
    both = swapped(both, "date", 1)
    home, attended = call(
        home_kernel,
        "home",
        (pltpu.VMEM((slots, rows, width), F32), jax.ShapeDtypeStruct((slots, rows, channels), BF16)),
        [SMEM] + [VMEM] * 5,
        (ids, near(stay), near(close), near(context), near(both), near(far_context)),
        6,
        scratch=(pltpu.VMEM((groups, slots, rows, part), BF16),),
    )
    grad_tokens, grad_norm = call(
        finish_kernel,
        "finish",
        (
            jax.ShapeDtypeStruct((slots, rows, width), BF16),
            jax.ShapeDtypeStruct((2, width), F32),
        ),
        [SMEM] * 2 + [VMEM] * 7,
        (ids, live, near(own_unit), near(own_inv), gain2, near(home), near(far), total, far_total),
        6,
    )
    return attended, grad_tokens, grad_norm


def solution(mesh):
    in_specs = (
        P(("rep", "tile"), "date", None),
        P(("rep", "tile"), "date", None),
        P(("rep", "tile"), None),
        P(("rep", "tile")),
        P("rep"),
        P(),
        P(),
        P(),
        P("tile", None),
    )
    out_specs = (P(("rep", "tile"), "date", None), P(("rep", "tile"), "date", None), P("rep", None))
    return jax.shard_map(local, mesh=mesh, in_specs=in_specs, out_specs=out_specs, check_vma=False)
```

```python
import functools

import jax
import jax.numpy as jnp
from jax import lax
from jax.experimental import pallas as pl
from jax.experimental.pallas import tpu as pltpu
from jax.sharding import PartitionSpec as P

HEAD_DIM = 80
DG = 32
BLOCK_ROWS = 32
F32 = jnp.float32
BF16 = jnp.bfloat16

VMEM = pl.BlockSpec(memory_space=pltpu.VMEM)
SMEM = pl.BlockSpec(memory_space=pltpu.SMEM)
HBM = pl.BlockSpec(memory_space=pltpu.HBM)


def dot(a, b):
    return jnp.dot(a, b, preferred_element_type=F32)


def dot_nt(a, b):
    return lax.dot_general(a, b, (((1,), (1,)), ((), ())), preferred_element_type=F32)


def dot_tn(a, b):
    return lax.dot_general(a, b, (((0,), (0,)), ((), ())), preferred_element_type=F32)


def window_of(group, part):
    wide = -(-part // 128) * 128
    odd = lax.rem(group, 2)
    start = (group // 2) * (2 * part) + odd * (2 * part - wide)
    return start, wide, odd == 1


def pick_kernel(part, other, ids_ref, w_ref, *refs):
    out_refs, windows, sems = refs[:-2], refs[-2], refs[-1]
    height = windows.shape[1]
    channels = w_ref.shape[1] // 3
    half = 1 - ids_ref[0] if other else ids_ref[0]
    first = pl.multiple_of(half * height, 16)
    start, wide, odd = window_of(ids_ref[1], part)
    moves = [
        pltpu.make_async_copy(
            w_ref.at[pl.ds(first, height), pl.ds(pl.multiple_of(i * channels + start, 128), wide)],
            windows.at[i],
            sems.at[i],
        )
        for i in range(3)
    ]
    for move in moves:
        move.start()
    for move in moves:
        move.wait()
    pieces = []
    for i in range(3):
        window = windows[i]
        pieces.append(jnp.where(odd, window[:, wide - part :], window[:, :part]))
    picked = jnp.concatenate(pieces, axis=1)
    at = 0
    for out_ref in out_refs:
        out_ref[...] = picked[at : at + out_ref.shape[0]]
        at += out_ref.shape[0]


def chip_pair(ids_ref, part):
    pair = ids_ref[1] // 2
    return pl.multiple_of(pair * (2 * part), 128), pl.multiple_of((1 - pair) * (2 * part), 128)


def pack_across_kernel(part, ids_ref, tokens_ref, cotangent_ref, out_ref):
    width = tokens_ref.shape[2]
    theirs = chip_pair(ids_ref, part)[1]
    out_ref[:, :, :width] = tokens_ref[...]
    out_ref[:, :, width:] = cotangent_ref[:, :, pl.ds(theirs, 2 * part)]


def pack_beside_kernel(part, ids_ref, tokens_ref, cotangent_ref, across_ref, out_ref, up_ref):
    width = tokens_ref.shape[2]
    ours = chip_pair(ids_ref, part)[0]
    odd = lax.rem(ids_ref[1], 2) == 1
    out_ref[:, :, :width] = tokens_ref[...]
    out_ref[:, :, width : 2 * width] = across_ref[:, :, :width]
    theirs = []
    for i, block in enumerate((cotangent_ref[:, :, pl.ds(ours, 2 * part)], across_ref[:, :, width:])):
        low, high = block[:, :, :part], block[:, :, part:]
        up_ref[i] = jnp.where(odd, high, low)
        theirs.append(jnp.where(odd, low, high))
    out_ref[:, :, 2 * width :] = jnp.concatenate(theirs, axis=2)


def norm_kernel(visible_ref, pos_ref, gain_ref, bias_ref, tokens_ref, across_ref, beside_ref, *refs):
    normed_ref, unit_ref, own_unit_ref, own_inv_ref = refs
    slots, rows, width = tokens_ref.shape
    gain = gain_ref[...]
    bias = bias_ref[...]
    for p in range(slots):
        iota = lax.broadcasted_iota(jnp.int32, (8, pos_ref.shape[0]), 1)
        onehot = (iota == visible_ref[p]).astype(F32).astype(BF16)
        position = dot(onehot, pos_ref[...])[0:1]
        groups = (
            tokens_ref[p],
            beside_ref[p, :, :width],
            across_ref[p, :, :width],
            beside_ref[p, :, width : 2 * width],
        )
        for s, tokens in enumerate(groups):
            embedded = (tokens.astype(F32) + position).astype(BF16).astype(F32)
            centred = embedded - jnp.mean(embedded, axis=-1, keepdims=True)
            inv_std = lax.rsqrt(jnp.mean(centred * centred, axis=-1, keepdims=True) + 1e-06)
            unit = centred * inv_std
            at = (p * len(groups) + s) * rows
            normed_ref[at : at + rows] = (unit * gain + bias).astype(BF16)
            unit_ref[at : at + rows] = unit.astype(BF16)
            if s == 0:
                own_unit_ref[p] = unit
                own_inv_ref[p] = jnp.broadcast_to(inv_std, own_inv_ref.shape[1:])


def put_pieces(ids_ref, depth, offset, piece_refs, weights):
    owners = len(piece_refs) // 2 + 1
    rep, owner = ids_ref[0], ids_ref[2]
    share = depth // 2
    spot = owner ^ (owner >> 1)
    for i, ref in enumerate(piece_refs):
        back = lax.rem(spot + owners - (i // 2 + 1), owners)
        half = 1 - rep if i % 2 else rep
        first = (back ^ (back >> 1)) * depth + half * share + offset
        weights[pl.ds(pl.multiple_of(first, 16), ref.shape[0]), :] = ref[...]


def place_kernel(depth, ids_ref, low_ref, high_ref, rest_ref, *refs):
    weights = refs[-1]
    rep, own = ids_ref[0], ids_ref[2] * depth
    share = depth // 2
    low = pl.multiple_of(own + rep * share, 16)
    weights[pl.ds(low, low_ref.shape[0]), :] = low_ref[...]
    high = pl.multiple_of(own + rep * share + low_ref.shape[0], 16)
    weights[pl.ds(high, high_ref.shape[0]), :] = high_ref[...]
    rest = pl.multiple_of(own + (1 - rep) * share, 16)
    weights[pl.ds(rest, rest_ref.shape[0]), :] = rest_ref[...]
    put_pieces(ids_ref, depth, 0, refs[:-1], weights)


def attend_kernel(
    count, depth, ids_ref, live_ref, _, normed_ref, valid_ref, up_ref, beside_ref, *refs
):
    piece_refs = refs[:count]
    own_ref, close_ref, across_ref, gqkv_ref, weights, qkv_ref = refs[count:]
    _, slots, rows, channels = up_ref.shape
    dates = valid_ref.shape[1]
    heads = channels // HEAD_DIM
    inv_scale = 1.0 / HEAD_DIM**0.5
    if count:
        put_pieces(ids_ref, depth, depth // 4, piece_refs, weights)
    qkv_ref[...] = dot(normed_ref[...], weights[...]).astype(BF16)
    row = lax.broadcasted_iota(jnp.int32, (dates, dates), 0)
    column = lax.broadcasted_iota(jnp.int32, (dates, dates), 1)
    same_date = column == (row ^ (ids_ref[1] * rows))
    for p in range(slots):
        span = slice(p * dates, (p + 1) * dates)
        alive = (live_ref[ids_ref[2]] > p // (BLOCK_ROWS // DG)).astype(F32)
        rows_qkv = qkv_ref[span, :]
        others = beside_ref[p, :, beside_ref.shape[2] - 2 * channels :]
        upstream = [up_ref[0, p], others[:, :channels], up_ref[1, p], others[:, channels:]]
        upstream = jnp.concatenate(upstream, axis=0) * alive.astype(BF16)
        valid = valid_ref[p : p + 1, :].astype(F32)
        allowed = jnp.sum(jnp.where(same_date, valid, 0.0), axis=1, keepdims=True) > 0
        grads = [[], [], []]
        contexts = []
        for h in range(heads):
            q, k, v = (
                rows_qkv[:, i * channels + h * HEAD_DIM : i * channels + (h + 1) * HEAD_DIM]
                for i in range(3)
            )
            up = upstream[:, h * HEAD_DIM : (h + 1) * HEAD_DIM]
            scores = jnp.where(allowed, dot_nt(k, q) * inv_scale, -1e30)
            exps = jnp.exp(scores - jnp.max(scores, axis=0, keepdims=True))
            probs = exps * (1.0 / jnp.sum(exps, axis=0, keepdims=True))
            low = probs.astype(BF16)
            contexts.append(dot_tn(low, v) * alive)
            grads[2].append(dot(low, up))
            gprobs = dot_nt(v, up)
            gscores = probs * (gprobs - jnp.sum(probs * gprobs, axis=0, keepdims=True)) * inv_scale
            glow = gscores.astype(BF16)
            grads[0].append(dot_tn(glow, k))
            grads[1].append(dot(glow, q))
        gqkv_ref[span, :] = jnp.concatenate(grads[0] + grads[1] + grads[2], axis=1).astype(BF16)
        context = jnp.concatenate(contexts, axis=1).astype(BF16)
        for s, out in enumerate((own_ref, close_ref, across_ref.at[0], across_ref.at[1])):
            out[p] = context[s * rows : (s + 1) * rows]


def back_kernel(gqkv_ref, unit_ref, weights, stay_ref, pass_ref, cross_ref, sums_ref):
    slots, rows, width = stay_ref.shape
    dates = gqkv_ref.shape[0] // slots
    tail = 2 * slots * rows
    step = 256
    for n in range(width // step):
        lanes = slice(n * step, (n + 1) * step)
        partial = dot_nt(gqkv_ref[...], weights[lanes, :])
        low = partial.astype(BF16)
        for p in range(slots):
            for s in range(dates // rows):
                block = low[p * dates + s * rows : p * dates + (s + 1) * rows]
                if s % 2:
                    at = (s // 2 * slots + p) * rows
                    cross_ref[at : at + rows, lanes] = block
                else:
                    (pass_ref if s else stay_ref)[p, :, lanes] = block
        gain_sum = jnp.sum(partial * unit_ref[:, lanes].astype(F32), axis=0, keepdims=True)
        sums = jnp.concatenate([gain_sum, jnp.sum(partial, axis=0, keepdims=True)], axis=0)
        sums_ref[:, lanes] = sums
        high = sums.astype(BF16)
        rest = (sums - high.astype(F32)).astype(BF16)
        fill = jnp.zeros((cross_ref.shape[0] - tail - 4, step), BF16)
        cross_ref[tail:, lanes] = jnp.concatenate([high, rest, fill], axis=0)


def merge_kernel(pass_ref, close_ref, sums_ref, out_ref, total_ref):
    slots, rows, width = out_ref.shape
    for p in range(slots):
        at = (slots + p) * rows
        out_ref[p] = (pass_ref[p].astype(F32) + close_ref[at : at + rows].astype(F32)).astype(BF16)
    sums = close_ref[2 * slots * rows :].astype(F32)
    total_ref[...] = sums_ref[...] + sums[0:2] + sums[2:4]


def both_kernel(close_ref, far_ref, both_ref):
    both_ref[0] = close_ref[...]
    both_ref[1] = far_ref[1]


def add_kernel(*refs):
    total = refs[0][...]
    for ref in refs[1:-1]:
        total = total + ref[...]
    refs[-1][...] = total


def home_kernel(ids_ref, stay_ref, close_ref, own_ref, beside_ref, across_ref, grad_ref, attended_ref, held):
    slots, rows, width = grad_ref.shape
    group = ids_ref[1]
    held[group] = own_ref[...]
    held[group ^ 1] = beside_ref[0]
    held[group ^ 2] = across_ref[0]
    held[group ^ 3] = beside_ref[1]
    for p in range(slots):
        close = close_ref[p * rows : (p + 1) * rows].astype(F32)
        grad_ref[p] = stay_ref[p].astype(F32) + close
        attended_ref[p] = jnp.concatenate([held[g, p] for g in range(held.shape[0])], axis=1)


def finish_kernel(ids_ref, live_ref, unit_ref, inv_ref, gain_ref, grad_ref, far_ref, *refs):
    out_ref, norm_ref = refs[-2:]
    slots = unit_ref.shape[0]
    gain = gain_ref[...]
    for p in range(slots):
        alive = (live_ref[ids_ref[2]] > p // (BLOCK_ROWS // DG)).astype(F32)
        unit = unit_ref[p]
        scaled = (grad_ref[p] + far_ref[p].astype(F32)) * gain
        out = inv_ref[p][:, 0:1] * (
            scaled
            - jnp.mean(scaled, axis=-1, keepdims=True)
            - unit * jnp.mean(scaled * unit, axis=-1, keepdims=True)
        )
        out_ref[p] = (out * alive).astype(BF16)
    total = refs[0][...]
    for ref in refs[1:-2]:
        total = total + ref[...]
    norm_ref[...] = total


def swapped(array, axis, bits):
    return lax.ppermute(array, axis, [(i, i ^ bits) for i in range(lax.axis_size(axis))])


def after(array, *others):
    return lax.optimization_barrier((array, *others))[0]


def near(array):
    return pltpu.with_memory_space_constraint(array, pltpu.VMEM)


def call(kernel, name, out_shape, in_specs, args, megabytes, scratch=(), microseconds=0.01, aliases=()):
    return pl.pallas_call(
        kernel,
        out_shape=out_shape,
        in_specs=in_specs,
        out_specs=jax.tree.map(lambda _: VMEM, out_shape),
        scratch_shapes=list(scratch),
        input_output_aliases=dict(aliases),
        compiler_params=pltpu.CompilerParams(vmem_limit_bytes=megabytes * 1024 * 1024),
        cost_estimate=pl.CostEstimate(
            flops=int(microseconds * 10**9), bytes_accessed=1000, transcendentals=0
        ),
        name=name,
    )(*args)


def pick(w_qkv, ids, share, part, other):
    wide = -(-part // 128) * 128
    return call(
        functools.partial(pick_kernel, part, other),
        "pick",
        (pltpu.VMEM((share, 3 * part), BF16),)
        if other
        else (pltpu.VMEM((share // 2, 3 * part), BF16),) * 2,
        [SMEM, HBM],
        (ids, pltpu.with_memory_space_constraint(w_qkv, pltpu.HBM)),
        4,
        scratch=(pltpu.VMEM((3, share, wide), BF16), pltpu.SemaphoreType.DMA((3,))),
    )


def local(tokens, cotangent, valid, visible, live, pos_table, norm_gain, norm_bias, w_qkv):
    slots, rows, width = tokens.shape
    groups = lax.axis_size("date")
    owners = lax.axis_size("tile")
    depth, triple = w_qkv.shape
    channels = triple // 3
    part = channels // groups
    dates = rows * groups
    ids = jnp.stack([lax.axis_index(name) for name in ("rep", "date", "tile")]).astype(jnp.int32)
    gain2, bias2 = norm_gain.reshape(1, width), norm_bias.reshape(1, width)

    chain = owners == 4 and lax.axis_size("rep") == 2 and depth % 64 == 0
    ring = [(0, 1), (1, 3), (3, 2), (2, 0)]
    share = depth // 2
    if chain:
        low, high = pick(w_qkv, ids, share, part, False)
        chains = []
        for held in (low, high):
            first = lax.ppermute(held, "tile", ring)
            second = lax.ppermute(first, "tile", ring)
            first_other = swapped(first, "rep", 1)
            if chains:
                (rest,) = pick(w_qkv, after(ids, first), share, part, True)
                first_other = after(first_other, rest)
            second = after(second, first_other)
            third = lax.ppermute(second, "tile", ring)
            second_other = swapped(second, "rep", 1)
            third = after(third, second_other)
            third_other = swapped(third, "rep", 1)
            chains.append((first, first_other, second, second_other, third, third_other))
        first, later = chains[0][0], chains[1][2]
    else:
        first = later = ids

    across = call(
        functools.partial(pack_across_kernel, part),
        "pack_across",
        pltpu.VMEM((slots, rows, width + 2 * part), BF16),
        [SMEM, VMEM, VMEM],
        (after(ids, first), tokens, cotangent),
        6,
    )
    across = swapped(across, "date", 2)
    pair = pltpu.VMEM((2, slots, rows, part), BF16)
    beside, ups = call(
        functools.partial(pack_beside_kernel, part),
        "pack_beside",
        (pltpu.VMEM((slots, rows, 2 * width + 2 * part), BF16), pair),
        [SMEM, VMEM, VMEM, VMEM],
        (after(ids, later), tokens, cotangent, near(across)),
        6,
    )
    beside = swapped(beside, "date", 1)

    normed, unit, own_unit, own_inv = call(
        norm_kernel,
        "norm",
        (
            pltpu.VMEM((slots * dates, width), BF16),
            pltpu.VMEM((slots * dates, width), BF16),
            pltpu.VMEM((slots, rows, width), F32),
            pltpu.VMEM((slots, rows, 128), F32),
        ),
        [SMEM] + [VMEM] * 6,
        (visible, pos_table, gain2, bias2, tokens, near(across), near(beside)),
        12,
        microseconds=2,
    )
    whole = pltpu.VMEM((width, 3 * part), BF16)
    if chain:
        own = [near(piece) for piece in (low, high, rest)]
        pieces = [near(piece) for piece in chains[0]]
        weights = call(
            functools.partial(place_kernel, depth),
            "place",
            whole,
            [SMEM] + [VMEM] * (len(own) + len(pieces)),
            (ids, *own, *pieces),
            4,
            microseconds=8,
        )
        pieces = [near(piece) for piece in chains[1]]
    else:
        group = lax.axis_index("date")
        mine = [
            lax.dynamic_slice_in_dim(w_qkv, i * channels + group * part, part, 1) for i in range(3)
        ]
        weights = lax.all_gather(jnp.concatenate(mine, axis=1), "tile", axis=0, tiled=True)
        pieces = []

    piece = pltpu.VMEM((slots, rows, part), BF16)
    context, close_context, far_context, gqkv, weights = call(
        functools.partial(attend_kernel, len(pieces), depth),
        "attend",
        (
            piece,
            piece,
            pair,
            pltpu.VMEM((slots * dates, 3 * part), BF16),
            whole,
        ),
        [SMEM] * 2 + [VMEM] * (5 + len(pieces)),
        (ids, live, near(weights), near(normed), valid, near(ups), near(beside), *pieces),
        20,
        aliases=((2, 4),),
        scratch=(pltpu.VMEM((slots * dates, 3 * part), BF16),),
    )
    far_context = swapped(far_context, "date", 2)

    block = pltpu.VMEM((slots, rows, width), BF16)
    pairs = pltpu.VMEM((2, width), F32)
    stay, passing, cross, sums = call(
        back_kernel,
        "back",
        (block, block, pltpu.VMEM((2 * slots * rows + 16, width), BF16), pairs),
        [VMEM] * 3,
        (near(gqkv), near(unit), near(weights)),
        12,
    )

    close = swapped(cross, "date", 1)
    both = call(
        both_kernel,
        "both",
        pair,
        [VMEM] * 2,
        (near(close_context), near(far_context)),
        2,
        microseconds=10,
    )
    close = after(close, both)
    chip, total = call(
        merge_kernel,
        "merge",
        (block, pairs),
        [VMEM] * 3,
        (near(passing), near(close), near(sums)),
        6,
    )
    far = swapped(chip, "date", 2)
    if owners == 4:
        total = call(
            add_kernel,
            "add",
            pairs,
            [VMEM] * owners,
            [near(total)] + [near(swapped(total, "tile", s)) for s in range(1, owners)],
            2,
        )
    else:
        total = lax.psum(total, "tile")
    far_total = swapped(total, "date", 2)
    both = swapped(both, "date", 1)
    home, attended = call(
        home_kernel,
        "home",
        (pltpu.VMEM((slots, rows, width), F32), jax.ShapeDtypeStruct((slots, rows, channels), BF16)),
        [SMEM] + [VMEM] * 5,
        (ids, near(stay), near(close), near(context), near(both), near(far_context)),
        6,
        scratch=(pltpu.VMEM((groups, slots, rows, part), BF16),),
    )
    grad_tokens, grad_norm = call(
        finish_kernel,
        "finish",
        (
            jax.ShapeDtypeStruct((slots, rows, width), BF16),
            jax.ShapeDtypeStruct((2, width), F32),
        ),
        [SMEM] * 2 + [VMEM] * 7,
        (ids, live, near(own_unit), near(own_inv), gain2, near(home), near(far), total, far_total),
        6,
    )
    return attended, grad_tokens, grad_norm


def solution(mesh):
    in_specs = (
        P(("rep", "tile"), "date", None),
        P(("rep", "tile"), "date", None),
        P(("rep", "tile"), None),
        P(("rep", "tile")),
        P("rep"),
        P(),
        P(),
        P(),
        P("tile", None),
    )
    out_specs = (P(("rep", "tile"), "date", None), P(("rep", "tile"), "date", None), P("rep", None))
    return jax.shard_map(local, mesh=mesh, in_specs=in_specs, out_specs=out_specs, check_vma=False)
```

```python
import functools

import jax
import jax.numpy as jnp
from jax import lax
from jax.experimental import pallas as pl
from jax.experimental.pallas import tpu as pltpu
from jax.sharding import PartitionSpec as P

HEAD_DIM = 80
DG = 32
BLOCK_ROWS = 32
F32 = jnp.float32
BF16 = jnp.bfloat16

VMEM = pl.BlockSpec(memory_space=pltpu.VMEM)
SMEM = pl.BlockSpec(memory_space=pltpu.SMEM)
HBM = pl.BlockSpec(memory_space=pltpu.HBM)


def dot(a, b):
    return jnp.dot(a, b, preferred_element_type=F32)


def dot_nt(a, b):
    return lax.dot_general(a, b, (((1,), (1,)), ((), ())), preferred_element_type=F32)


def dot_tn(a, b):
    return lax.dot_general(a, b, (((0,), (0,)), ((), ())), preferred_element_type=F32)


def window_of(group, part):
    wide = -(-part // 128) * 128
    odd = lax.rem(group, 2)
    start = (group // 2) * (2 * part) + odd * (2 * part - wide)
    return start, wide, odd == 1


def pick_kernel(part, other, ids_ref, w_ref, *refs):
    out_refs, windows, sems = refs[:-2], refs[-2], refs[-1]
    height = windows.shape[1]
    channels = w_ref.shape[1] // 3
    half = 1 - ids_ref[0] if other else ids_ref[0]
    first = pl.multiple_of(half * height, 16)
    start, wide, odd = window_of(ids_ref[1], part)
    moves = [
        pltpu.make_async_copy(
            w_ref.at[pl.ds(first, height), pl.ds(pl.multiple_of(i * channels + start, 128), wide)],
            windows.at[i],
            sems.at[i],
        )
        for i in range(3)
    ]
    for move in moves:
        move.start()
    for move in moves:
        move.wait()
    pieces = []
    for i in range(3):
        window = windows[i]
        pieces.append(jnp.where(odd, window[:, wide - part :], window[:, :part]))
    picked = jnp.concatenate(pieces, axis=1)
    at = 0
    for out_ref in out_refs:
        out_ref[...] = picked[at : at + out_ref.shape[0]]
        at += out_ref.shape[0]


def chip_pair(ids_ref, part):
    pair = ids_ref[1] // 2
    return pl.multiple_of(pair * (2 * part), 128), pl.multiple_of((1 - pair) * (2 * part), 128)


def pack_across_kernel(part, ids_ref, tokens_ref, cotangent_ref, out_ref):
    width = tokens_ref.shape[2]
    theirs = chip_pair(ids_ref, part)[1]
    out_ref[:, :, :width] = tokens_ref[...]
    out_ref[:, :, width:] = cotangent_ref[:, :, pl.ds(theirs, 2 * part)]


def pack_beside_kernel(part, ids_ref, tokens_ref, cotangent_ref, across_ref, out_ref, up_ref):
    width = tokens_ref.shape[2]
    ours = chip_pair(ids_ref, part)[0]
    odd = lax.rem(ids_ref[1], 2) == 1
    out_ref[:, :, :width] = tokens_ref[...]
    out_ref[:, :, width : 2 * width] = across_ref[:, :, :width]
    theirs = []
    for i, block in enumerate((cotangent_ref[:, :, pl.ds(ours, 2 * part)], across_ref[:, :, width:])):
        low, high = block[:, :, :part], block[:, :, part:]
        up_ref[i] = jnp.where(odd, high, low)
        theirs.append(jnp.where(odd, low, high))
    out_ref[:, :, 2 * width :] = jnp.concatenate(theirs, axis=2)


def norm_kernel(visible_ref, pos_ref, gain_ref, bias_ref, tokens_ref, across_ref, beside_ref, *refs):
    normed_ref, unit_ref, own_unit_ref, own_inv_ref = refs
    slots, rows, width = tokens_ref.shape
    gain = gain_ref[...]
    bias = bias_ref[...]
    for p in range(slots):
        iota = lax.broadcasted_iota(jnp.int32, (8, pos_ref.shape[0]), 1)
        onehot = (iota == visible_ref[p]).astype(F32).astype(BF16)
        position = dot(onehot, pos_ref[...])[0:1]
        groups = (
            tokens_ref[p],
            beside_ref[p, :, :width],
            across_ref[p, :, :width],
            beside_ref[p, :, width : 2 * width],
        )
        for s, tokens in enumerate(groups):
            embedded = (tokens.astype(F32) + position).astype(BF16).astype(F32)
            centred = embedded - jnp.mean(embedded, axis=-1, keepdims=True)
            inv_std = lax.rsqrt(jnp.mean(centred * centred, axis=-1, keepdims=True) + 1e-06)
            unit = centred * inv_std
            at = (p * len(groups) + s) * rows
            normed_ref[at : at + rows] = (unit * gain + bias).astype(BF16)
            unit_ref[at : at + rows] = unit.astype(BF16)
            if s == 0:
                own_unit_ref[p] = unit
                own_inv_ref[p] = jnp.broadcast_to(inv_std, own_inv_ref.shape[1:])


def put_pieces(ids_ref, depth, offset, steps, piece_refs, weights):
    owners = 4
    rep, owner = ids_ref[0], ids_ref[2]
    share = depth // 2
    spot = owner ^ (owner >> 1)
    for i, ref in enumerate(piece_refs):
        back = lax.rem(spot + owners - steps[i // 2], owners)
        half = 1 - rep if i % 2 else rep
        first = (back ^ (back >> 1)) * depth + half * share + offset
        weights[pl.ds(pl.multiple_of(first, 16), ref.shape[0]), :] = ref[...]


def place_kernel(depth, ids_ref, low_ref, high_ref, rest_ref, *refs):
    weights = refs[-1]
    rep, own = ids_ref[0], ids_ref[2] * depth
    share = depth // 2
    low = pl.multiple_of(own + rep * share, 16)
    weights[pl.ds(low, low_ref.shape[0]), :] = low_ref[...]
    high = pl.multiple_of(own + rep * share + low_ref.shape[0], 16)
    weights[pl.ds(high, high_ref.shape[0]), :] = high_ref[...]
    rest = pl.multiple_of(own + (1 - rep) * share, 16)
    weights[pl.ds(rest, rest_ref.shape[0]), :] = rest_ref[...]
    put_pieces(ids_ref, depth, 0, (1, 2, 3), refs[:6], weights)
    put_pieces(ids_ref, depth, depth // 4, (1, 2), refs[6:-1], weights)


def attend_kernel(
    count, depth, ids_ref, live_ref, _, normed_ref, valid_ref, up_ref, beside_ref, *refs
):
    piece_refs = refs[:count]
    own_ref, close_ref, across_ref, gqkv_ref, weights, qkv_ref = refs[count:]
    _, slots, rows, channels = up_ref.shape
    dates = valid_ref.shape[1]
    heads = channels // HEAD_DIM
    inv_scale = 1.0 / HEAD_DIM**0.5
    if count:
        put_pieces(ids_ref, depth, depth // 4, (3,), piece_refs, weights)
    qkv_ref[...] = dot(normed_ref[...], weights[...]).astype(BF16)
    row = lax.broadcasted_iota(jnp.int32, (dates, dates), 0)
    column = lax.broadcasted_iota(jnp.int32, (dates, dates), 1)
    same_date = column == (row ^ (ids_ref[1] * rows))
    for p in range(slots):
        span = slice(p * dates, (p + 1) * dates)
        alive = (live_ref[ids_ref[2]] > p // (BLOCK_ROWS // DG)).astype(F32)
        rows_qkv = qkv_ref[span, :]
        others = beside_ref[p, :, beside_ref.shape[2] - 2 * channels :]
        upstream = [up_ref[0, p], others[:, :channels], up_ref[1, p], others[:, channels:]]
        upstream = jnp.concatenate(upstream, axis=0) * alive.astype(BF16)
        valid = valid_ref[p : p + 1, :].astype(F32)
        allowed = jnp.sum(jnp.where(same_date, valid, 0.0), axis=1, keepdims=True) > 0
        grads = [[], [], []]
        contexts = []
        for h in range(heads):
            q, k, v = (
                rows_qkv[:, i * channels + h * HEAD_DIM : i * channels + (h + 1) * HEAD_DIM]
                for i in range(3)
            )
            up = upstream[:, h * HEAD_DIM : (h + 1) * HEAD_DIM]
            scores = jnp.where(allowed, dot_nt(k, q) * inv_scale, -1e30)
            exps = jnp.exp(scores - jnp.max(scores, axis=0, keepdims=True))
            probs = exps * (1.0 / jnp.sum(exps, axis=0, keepdims=True))
            low = probs.astype(BF16)
            contexts.append(dot_tn(low, v) * alive)
            grads[2].append(dot(low, up))
            gprobs = dot_nt(v, up)
            gscores = probs * (gprobs - jnp.sum(probs * gprobs, axis=0, keepdims=True)) * inv_scale
            glow = gscores.astype(BF16)
            grads[0].append(dot_tn(glow, k))
            grads[1].append(dot(glow, q))
        gqkv_ref[span, :] = jnp.concatenate(grads[0] + grads[1] + grads[2], axis=1).astype(BF16)
        context = jnp.concatenate(contexts, axis=1).astype(BF16)
        for s, out in enumerate((own_ref, close_ref, across_ref.at[0], across_ref.at[1])):
            out[p] = context[s * rows : (s + 1) * rows]


def back_kernel(gqkv_ref, unit_ref, weights, stay_ref, pass_ref, cross_ref, sums_ref):
    slots, rows, width = stay_ref.shape
    dates = gqkv_ref.shape[0] // slots
    tail = 2 * slots * rows
    step = 256
    for n in range(width // step):
        lanes = slice(n * step, (n + 1) * step)
        partial = dot_nt(gqkv_ref[...], weights[lanes, :])
        low = partial.astype(BF16)
        for p in range(slots):
            for s in range(dates // rows):
                block = low[p * dates + s * rows : p * dates + (s + 1) * rows]
                if s % 2:
                    at = (s // 2 * slots + p) * rows
                    cross_ref[at : at + rows, lanes] = block
                else:
                    (pass_ref if s else stay_ref)[p, :, lanes] = block
        gain_sum = jnp.sum(partial * unit_ref[:, lanes].astype(F32), axis=0, keepdims=True)
        sums = jnp.concatenate([gain_sum, jnp.sum(partial, axis=0, keepdims=True)], axis=0)
        sums_ref[:, lanes] = sums
        high = sums.astype(BF16)
        rest = (sums - high.astype(F32)).astype(BF16)
        fill = jnp.zeros((cross_ref.shape[0] - tail - 4, step), BF16)
        cross_ref[tail:, lanes] = jnp.concatenate([high, rest, fill], axis=0)


def merge_kernel(pass_ref, close_ref, sums_ref, out_ref, total_ref):
    slots, rows, width = out_ref.shape
    for p in range(slots):
        at = (slots + p) * rows
        out_ref[p] = (pass_ref[p].astype(F32) + close_ref[at : at + rows].astype(F32)).astype(BF16)
    sums = close_ref[2 * slots * rows :].astype(F32)
    total_ref[...] = sums_ref[...] + sums[0:2] + sums[2:4]


def both_kernel(close_ref, far_ref, both_ref):
    both_ref[0] = close_ref[...]
    both_ref[1] = far_ref[1]


def add_kernel(*refs):
    total = refs[0][...]
    for ref in refs[1:-1]:
        total = total + ref[...]
    refs[-1][...] = total


def home_kernel(ids_ref, stay_ref, close_ref, own_ref, beside_ref, across_ref, grad_ref, attended_ref, held):
    slots, rows, width = grad_ref.shape
    group = ids_ref[1]
    held[group] = own_ref[...]
    held[group ^ 1] = beside_ref[0]
    held[group ^ 2] = across_ref[0]
    held[group ^ 3] = beside_ref[1]
    for p in range(slots):
        close = close_ref[p * rows : (p + 1) * rows].astype(F32)
        grad_ref[p] = stay_ref[p].astype(F32) + close
        attended_ref[p] = jnp.concatenate([held[g, p] for g in range(held.shape[0])], axis=1)


def finish_kernel(ids_ref, live_ref, unit_ref, inv_ref, gain_ref, grad_ref, far_ref, *refs):
    out_ref, norm_ref = refs[-2:]
    slots = unit_ref.shape[0]
    gain = gain_ref[...]
    for p in range(slots):
        alive = (live_ref[ids_ref[2]] > p // (BLOCK_ROWS // DG)).astype(F32)
        unit = unit_ref[p]
        scaled = (grad_ref[p] + far_ref[p].astype(F32)) * gain
        out = inv_ref[p][:, 0:1] * (
            scaled
            - jnp.mean(scaled, axis=-1, keepdims=True)
            - unit * jnp.mean(scaled * unit, axis=-1, keepdims=True)
        )
        out_ref[p] = (out * alive).astype(BF16)
    total = refs[0][...]
    for ref in refs[1:-2]:
        total = total + ref[...]
    norm_ref[...] = total


def swapped(array, axis, bits):
    return lax.ppermute(array, axis, [(i, i ^ bits) for i in range(lax.axis_size(axis))])


def after(array, *others):
    return lax.optimization_barrier((array, *others))[0]


def near(array):
    return pltpu.with_memory_space_constraint(array, pltpu.VMEM)


def call(kernel, name, out_shape, in_specs, args, megabytes, scratch=(), microseconds=0.01, aliases=()):
    return pl.pallas_call(
        kernel,
        out_shape=out_shape,
        in_specs=in_specs,
        out_specs=jax.tree.map(lambda _: VMEM, out_shape),
        scratch_shapes=list(scratch),
        input_output_aliases=dict(aliases),
        compiler_params=pltpu.CompilerParams(vmem_limit_bytes=megabytes * 1024 * 1024),
        cost_estimate=pl.CostEstimate(
            flops=int(microseconds * 10**9), bytes_accessed=1000, transcendentals=0
        ),
        name=name,
    )(*args)


def pick(w_qkv, ids, share, part, other):
    wide = -(-part // 128) * 128
    return call(
        functools.partial(pick_kernel, part, other),
        "pick",
        (pltpu.VMEM((share, 3 * part), BF16),)
        if other
        else (pltpu.VMEM((share // 2, 3 * part), BF16),) * 2,
        [SMEM, HBM],
        (ids, pltpu.with_memory_space_constraint(w_qkv, pltpu.HBM)),
        4,
        scratch=(pltpu.VMEM((3, share, wide), BF16), pltpu.SemaphoreType.DMA((3,))),
    )


def local(tokens, cotangent, valid, visible, live, pos_table, norm_gain, norm_bias, w_qkv):
    slots, rows, width = tokens.shape
    groups = lax.axis_size("date")
    owners = lax.axis_size("tile")
    depth, triple = w_qkv.shape
    channels = triple // 3
    part = channels // groups
    dates = rows * groups
    ids = jnp.stack([lax.axis_index(name) for name in ("rep", "date", "tile")]).astype(jnp.int32)
    gain2, bias2 = norm_gain.reshape(1, width), norm_bias.reshape(1, width)

    chain = owners == 4 and lax.axis_size("rep") == 2 and depth % 64 == 0
    ring = [(0, 1), (1, 3), (3, 2), (2, 0)]
    share = depth // 2
    if chain:
        low, high = pick(w_qkv, ids, share, part, False)
        chains = []
        for held in (low, high):
            first = lax.ppermute(held, "tile", ring)
            if chains:
                (rest,) = pick(w_qkv, after(ids, held), share, part, True)
                first = after(first, rest)
            second = lax.ppermute(first, "tile", ring)
            first_other = swapped(first, "rep", 1)
            second = after(second, first_other)
            third = lax.ppermute(second, "tile", ring)
            second_other = swapped(second, "rep", 1)
            if not chains:
                third = after(third, second_other)
            third_other = swapped(third, "rep", 1)
            chains.append((first, first_other, second, second_other, third, third_other))
        first, later = chains[1][0], chains[1][2]
    else:
        first = later = ids

    across = call(
        functools.partial(pack_across_kernel, part),
        "pack_across",
        pltpu.VMEM((slots, rows, width + 2 * part), BF16),
        [SMEM, VMEM, VMEM],
        (after(ids, first), tokens, cotangent),
        6,
    )
    across = swapped(across, "date", 2)
    pair = pltpu.VMEM((2, slots, rows, part), BF16)
    beside, ups = call(
        functools.partial(pack_beside_kernel, part),
        "pack_beside",
        (pltpu.VMEM((slots, rows, 2 * width + 2 * part), BF16), pair),
        [SMEM, VMEM, VMEM, VMEM],
        (after(ids, later), tokens, cotangent, near(across)),
        6,
    )
    beside = swapped(beside, "date", 1)

    normed, unit, own_unit, own_inv = call(
        norm_kernel,
        "norm",
        (
            pltpu.VMEM((slots * dates, width), BF16),
            pltpu.VMEM((slots * dates, width), BF16),
            pltpu.VMEM((slots, rows, width), F32),
            pltpu.VMEM((slots, rows, 128), F32),
        ),
        [SMEM] + [VMEM] * 6,
        (visible, pos_table, gain2, bias2, tokens, near(across), near(beside)),
        12,
        microseconds=2,
    )
    whole = pltpu.VMEM((width, 3 * part), BF16)
    if chain:
        own = [near(piece) for piece in (low, high, rest)]
        pieces = [near(piece) for piece in chains[0] + chains[1][:4]]
        weights = call(
            functools.partial(place_kernel, depth),
            "place",
            whole,
            [SMEM] + [VMEM] * (len(own) + len(pieces)),
            (ids, *own, *pieces),
            4,
            microseconds=8,
        )
        pieces = [near(piece) for piece in chains[1][4:]]
    else:
        group = lax.axis_index("date")
        mine = [
            lax.dynamic_slice_in_dim(w_qkv, i * channels + group * part, part, 1) for i in range(3)
        ]
        weights = lax.all_gather(jnp.concatenate(mine, axis=1), "tile", axis=0, tiled=True)
        pieces = []

    piece = pltpu.VMEM((slots, rows, part), BF16)
    context, close_context, far_context, gqkv, weights = call(
        functools.partial(attend_kernel, len(pieces), depth),
        "attend",
        (
            piece,
            piece,
            pair,
            pltpu.VMEM((slots * dates, 3 * part), BF16),
            whole,
        ),
        [SMEM] * 2 + [VMEM] * (5 + len(pieces)),
        (ids, live, near(weights), near(normed), valid, near(ups), near(beside), *pieces),
        20,
        aliases=((2, 4),),
        scratch=(pltpu.VMEM((slots * dates, 3 * part), BF16),),
    )
    far_context = swapped(far_context, "date", 2)

    block = pltpu.VMEM((slots, rows, width), BF16)
    pairs = pltpu.VMEM((2, width), F32)
    stay, passing, cross, sums = call(
        back_kernel,
        "back",
        (block, block, pltpu.VMEM((2 * slots * rows + 16, width), BF16), pairs),
        [VMEM] * 3,
        (near(gqkv), near(unit), near(weights)),
        12,
    )

    close = swapped(cross, "date", 1)
    both = call(
        both_kernel,
        "both",
        pair,
        [VMEM] * 2,
        (near(close_context), near(far_context)),
        2,
        microseconds=10,
    )
    close = after(close, both)
    chip, total = call(
        merge_kernel,
        "merge",
        (block, pairs),
        [VMEM] * 3,
        (near(passing), near(close), near(sums)),
        6,
    )
    far = swapped(chip, "date", 2)
    both = swapped(both, "date", 1)
    home, attended = call(
        home_kernel,
        "home",
        (pltpu.VMEM((slots, rows, width), F32), jax.ShapeDtypeStruct((slots, rows, channels), BF16)),
        [SMEM] + [VMEM] * 5,
        (ids, near(stay), near(close), near(context), near(both), near(far_context)),
        6,
        scratch=(pltpu.VMEM((groups, slots, rows, part), BF16),),
    )
    if owners == 4:
        tiles = [swapped(total, "tile", s) for s in range(1, owners)]
        tiles[0] = after(tiles[0], home)
        total = call(
            add_kernel,
            "add",
            pairs,
            [VMEM] * owners,
            [near(total)] + [near(tile) for tile in tiles],
            2,
        )
    else:
        total = lax.psum(total, "tile")
    far_total = swapped(total, "date", 2)
    grad_tokens, grad_norm = call(
        finish_kernel,
        "finish",
        (
            jax.ShapeDtypeStruct((slots, rows, width), BF16),
            jax.ShapeDtypeStruct((2, width), F32),
        ),
        [SMEM] * 2 + [VMEM] * 7,
        (ids, live, near(own_unit), near(own_inv), gain2, near(home), near(far), total, far_total),
        6,
    )
    return attended, grad_tokens, grad_norm


def solution(mesh):
    in_specs = (
        P(("rep", "tile"), "date", None),
        P(("rep", "tile"), "date", None),
        P(("rep", "tile"), None),
        P(("rep", "tile")),
        P("rep"),
        P(),
        P(),
        P(),
        P("tile", None),
    )
    out_specs = (P(("rep", "tile"), "date", None), P(("rep", "tile"), "date", None), P("rep", None))
    return jax.shard_map(local, mesh=mesh, in_specs=in_specs, out_specs=out_specs, check_vma=False)
```

```python
import functools

import jax
import jax.numpy as jnp
from jax import lax
from jax.experimental import pallas as pl
from jax.experimental.pallas import tpu as pltpu
from jax.sharding import PartitionSpec as P

HEAD_DIM = 80
DG = 32
BLOCK_ROWS = 32
F32 = jnp.float32
BF16 = jnp.bfloat16

VMEM = pl.BlockSpec(memory_space=pltpu.VMEM)
SMEM = pl.BlockSpec(memory_space=pltpu.SMEM)
HBM = pl.BlockSpec(memory_space=pltpu.HBM)


def dot(a, b):
    return jnp.dot(a, b, preferred_element_type=F32)


def dot_nt(a, b):
    return lax.dot_general(a, b, (((1,), (1,)), ((), ())), preferred_element_type=F32)


def dot_tn(a, b):
    return lax.dot_general(a, b, (((0,), (0,)), ((), ())), preferred_element_type=F32)


def window_of(group, part):
    wide = -(-part // 128) * 128
    odd = lax.rem(group, 2)
    start = (group // 2) * (2 * part) + odd * (2 * part - wide)
    return start, wide, odd == 1


def pick_kernel(part, other, ids_ref, w_ref, *refs):
    out_refs, windows, sems = refs[:-2], refs[-2], refs[-1]
    height = windows.shape[1]
    channels = w_ref.shape[1] // 3
    half = 1 - ids_ref[0] if other else ids_ref[0]
    first = pl.multiple_of(half * height, 16)
    start, wide, odd = window_of(ids_ref[1], part)
    moves = [
        pltpu.make_async_copy(
            w_ref.at[pl.ds(first, height), pl.ds(pl.multiple_of(i * channels + start, 128), wide)],
            windows.at[i],
            sems.at[i],
        )
        for i in range(3)
    ]
    for move in moves:
        move.start()
    for move in moves:
        move.wait()
    pieces = []
    for i in range(3):
        window = windows[i]
        pieces.append(jnp.where(odd, window[:, wide - part :], window[:, :part]))
    picked = jnp.concatenate(pieces, axis=1)
    at = 0
    for out_ref in out_refs:
        out_ref[...] = picked[at : at + out_ref.shape[0]]
        at += out_ref.shape[0]


def chip_pair(ids_ref, part):
    pair = ids_ref[1] // 2
    return pl.multiple_of(pair * (2 * part), 128), pl.multiple_of((1 - pair) * (2 * part), 128)


def pack_across_kernel(part, ids_ref, tokens_ref, cotangent_ref, out_ref):
    width = tokens_ref.shape[2]
    theirs = chip_pair(ids_ref, part)[1]
    out_ref[:, :, :width] = tokens_ref[...]
    out_ref[:, :, width:] = cotangent_ref[:, :, pl.ds(theirs, 2 * part)]


def pack_beside_kernel(part, ids_ref, tokens_ref, cotangent_ref, across_ref, out_ref, up_ref):
    width = tokens_ref.shape[2]
    ours = chip_pair(ids_ref, part)[0]
    odd = lax.rem(ids_ref[1], 2) == 1
    out_ref[:, :, :width] = tokens_ref[...]
    out_ref[:, :, width : 2 * width] = across_ref[:, :, :width]
    theirs = []
    for i, block in enumerate((cotangent_ref[:, :, pl.ds(ours, 2 * part)], across_ref[:, :, width:])):
        low, high = block[:, :, :part], block[:, :, part:]
        up_ref[i] = jnp.where(odd, high, low)
        theirs.append(jnp.where(odd, low, high))
    out_ref[:, :, 2 * width :] = jnp.concatenate(theirs, axis=2)


def norm_kernel(visible_ref, pos_ref, gain_ref, bias_ref, tokens_ref, across_ref, beside_ref, *refs):
    normed_ref, unit_ref, own_unit_ref, own_inv_ref = refs
    slots, rows, width = tokens_ref.shape
    gain = gain_ref[...]
    bias = bias_ref[...]
    for p in range(slots):
        iota = lax.broadcasted_iota(jnp.int32, (8, pos_ref.shape[0]), 1)
        onehot = (iota == visible_ref[p]).astype(F32).astype(BF16)
        position = dot(onehot, pos_ref[...])[0:1]
        groups = (
            tokens_ref[p],
            beside_ref[p, :, :width],
            across_ref[p, :, :width],
            beside_ref[p, :, width : 2 * width],
        )
        for s, tokens in enumerate(groups):
            embedded = (tokens.astype(F32) + position).astype(BF16).astype(F32)
            centred = embedded - jnp.mean(embedded, axis=-1, keepdims=True)
            inv_std = lax.rsqrt(jnp.mean(centred * centred, axis=-1, keepdims=True) + 1e-06)
            unit = centred * inv_std
            at = (p * len(groups) + s) * rows
            normed_ref[at : at + rows] = (unit * gain + bias).astype(BF16)
            unit_ref[at : at + rows] = unit.astype(BF16)
            if s == 0:
                own_unit_ref[p] = unit
                own_inv_ref[p] = jnp.broadcast_to(inv_std, own_inv_ref.shape[1:])


def put_pieces(ids_ref, depth, offset, steps, piece_refs, weights):
    owners = 4
    rep, owner = ids_ref[0], ids_ref[2]
    share = depth // 2
    spot = owner ^ (owner >> 1)
    for i, ref in enumerate(piece_refs):
        back = lax.rem(spot + owners - steps[i // 2], owners)
        half = 1 - rep if i % 2 else rep
        first = (back ^ (back >> 1)) * depth + half * share + offset
        weights[pl.ds(pl.multiple_of(first, 16), ref.shape[0]), :] = ref[...]


def place_kernel(depth, ids_ref, low_ref, high_ref, rest_ref, *refs):
    weights = refs[-1]
    rep, own = ids_ref[0], ids_ref[2] * depth
    share = depth // 2
    low = pl.multiple_of(own + rep * share, 16)
    weights[pl.ds(low, low_ref.shape[0]), :] = low_ref[...]
    high = pl.multiple_of(own + rep * share + low_ref.shape[0], 16)
    weights[pl.ds(high, high_ref.shape[0]), :] = high_ref[...]
    rest = pl.multiple_of(own + (1 - rep) * share, 16)
    weights[pl.ds(rest, rest_ref.shape[0]), :] = rest_ref[...]
    put_pieces(ids_ref, depth, 0, (1, 2, 3), refs[:6], weights)
    put_pieces(ids_ref, depth, depth // 4, (1, 2), refs[6:-1], weights)


def attend_kernel(
    count, depth, ids_ref, live_ref, _, normed_ref, valid_ref, up_ref, beside_ref, *refs
):
    piece_refs = refs[:count]
    own_ref, close_ref, across_ref, gqkv_ref, weights, qkv_ref = refs[count:]
    _, slots, rows, channels = up_ref.shape
    dates = valid_ref.shape[1]
    heads = channels // HEAD_DIM
    inv_scale = 1.0 / HEAD_DIM**0.5
    if count:
        put_pieces(ids_ref, depth, depth // 4, (3,), piece_refs, weights)
    qkv_ref[...] = dot(normed_ref[...], weights[...]).astype(BF16)
    row = lax.broadcasted_iota(jnp.int32, (dates, dates), 0)
    column = lax.broadcasted_iota(jnp.int32, (dates, dates), 1)
    same_date = column == (row ^ (ids_ref[1] * rows))
    for p in range(slots):
        span = slice(p * dates, (p + 1) * dates)
        alive = (live_ref[ids_ref[2]] > p // (BLOCK_ROWS // DG)).astype(F32)
        rows_qkv = qkv_ref[span, :]
        others = beside_ref[p, :, beside_ref.shape[2] - 2 * channels :]
        upstream = [up_ref[0, p], others[:, :channels], up_ref[1, p], others[:, channels:]]
        upstream = jnp.concatenate(upstream, axis=0) * alive.astype(BF16)
        valid = valid_ref[p : p + 1, :].astype(F32)
        allowed = jnp.sum(jnp.where(same_date, valid, 0.0), axis=1, keepdims=True) > 0
        grads = [[], [], []]
        contexts = []
        for h in range(heads):
            q, k, v = (
                rows_qkv[:, i * channels + h * HEAD_DIM : i * channels + (h + 1) * HEAD_DIM]
                for i in range(3)
            )
            up = upstream[:, h * HEAD_DIM : (h + 1) * HEAD_DIM]
            scores = jnp.where(allowed, dot_nt(k, q) * inv_scale, -1e30)
            exps = jnp.exp(scores - jnp.max(scores, axis=0, keepdims=True))
            probs = exps * (1.0 / jnp.sum(exps, axis=0, keepdims=True))
            low = probs.astype(BF16)
            contexts.append(dot_tn(low, v) * alive)
            grads[2].append(dot(low, up))
            gprobs = dot_nt(v, up)
            gscores = probs * (gprobs - jnp.sum(probs * gprobs, axis=0, keepdims=True)) * inv_scale
            glow = gscores.astype(BF16)
            grads[0].append(dot_tn(glow, k))
            grads[1].append(dot(glow, q))
        gqkv_ref[span, :] = jnp.concatenate(grads[0] + grads[1] + grads[2], axis=1).astype(BF16)
        context = jnp.concatenate(contexts, axis=1).astype(BF16)
        for s, out in enumerate((own_ref, close_ref, across_ref.at[0], across_ref.at[1])):
            out[p] = context[s * rows : (s + 1) * rows]


def back_kernel(gqkv_ref, unit_ref, weights, stay_ref, pass_ref, cross_ref, sums_ref):
    slots, rows, width = stay_ref.shape
    dates = gqkv_ref.shape[0] // slots
    step = 256
    for n in range(width // step):
        lanes = slice(n * step, (n + 1) * step)
        partial = dot_nt(gqkv_ref[...], weights[lanes, :])
        low = partial.astype(BF16)
        for p in range(slots):
            for s in range(dates // rows):
                block = low[p * dates + s * rows : p * dates + (s + 1) * rows]
                if s % 2:
                    at = (s // 2 * slots + p) * rows
                    cross_ref[at : at + rows, lanes] = block
                else:
                    (pass_ref if s else stay_ref)[p, :, lanes] = block
        gain_sum = jnp.sum(partial * unit_ref[:, lanes].astype(F32), axis=0, keepdims=True)
        sums = jnp.concatenate([gain_sum, jnp.sum(partial, axis=0, keepdims=True)], axis=0)
        sums_ref[:, lanes] = sums


def merge_kernel(pass_ref, close_ref, out_ref):
    slots, rows, width = out_ref.shape
    for p in range(slots):
        at = (slots + p) * rows
        out_ref[p] = (pass_ref[p].astype(F32) + close_ref[at : at + rows].astype(F32)).astype(BF16)


def both_kernel(close_ref, far_ref, both_ref):
    both_ref[0] = close_ref[...]
    both_ref[1] = far_ref[1]


def add_kernel(*refs):
    total = refs[0][...]
    for ref in refs[1:-1]:
        total = total + ref[...]
    refs[-1][...] = total


def home_kernel(ids_ref, stay_ref, close_ref, own_ref, beside_ref, across_ref, grad_ref, attended_ref, held):
    slots, rows, width = grad_ref.shape
    group = ids_ref[1]
    held[group] = own_ref[...]
    held[group ^ 1] = beside_ref[0]
    held[group ^ 2] = across_ref[0]
    held[group ^ 3] = beside_ref[1]
    for p in range(slots):
        close = close_ref[p * rows : (p + 1) * rows].astype(F32)
        grad_ref[p] = stay_ref[p].astype(F32) + close
        attended_ref[p] = jnp.concatenate([held[g, p] for g in range(held.shape[0])], axis=1)


def finish_kernel(ids_ref, live_ref, unit_ref, inv_ref, gain_ref, grad_ref, far_ref, *refs):
    out_ref, norm_ref = refs[-2:]
    slots = unit_ref.shape[0]
    gain = gain_ref[...]
    for p in range(slots):
        alive = (live_ref[ids_ref[2]] > p // (BLOCK_ROWS // DG)).astype(F32)
        unit = unit_ref[p]
        scaled = (grad_ref[p] + far_ref[p].astype(F32)) * gain
        out = inv_ref[p][:, 0:1] * (
            scaled
            - jnp.mean(scaled, axis=-1, keepdims=True)
            - unit * jnp.mean(scaled * unit, axis=-1, keepdims=True)
        )
        out_ref[p] = (out * alive).astype(BF16)
    total = refs[0][...]
    for ref in refs[1:-2]:
        total = total + ref[...]
    norm_ref[...] = total


def swapped(array, axis, bits):
    return lax.ppermute(array, axis, [(i, i ^ bits) for i in range(lax.axis_size(axis))])


def after(array, *others):
    return lax.optimization_barrier((array, *others))[0]


def near(array):
    return pltpu.with_memory_space_constraint(array, pltpu.VMEM)


def call(kernel, name, out_shape, in_specs, args, megabytes, scratch=(), microseconds=0.01, aliases=()):
    return pl.pallas_call(
        kernel,
        out_shape=out_shape,
        in_specs=in_specs,
        out_specs=jax.tree.map(lambda _: VMEM, out_shape),
        scratch_shapes=list(scratch),
        input_output_aliases=dict(aliases),
        compiler_params=pltpu.CompilerParams(vmem_limit_bytes=megabytes * 1024 * 1024),
        cost_estimate=pl.CostEstimate(
            flops=int(microseconds * 10**9), bytes_accessed=1000, transcendentals=0
        ),
        name=name,
    )(*args)


def pick(w_qkv, ids, share, part, other):
    wide = -(-part // 128) * 128
    return call(
        functools.partial(pick_kernel, part, other),
        "pick",
        (pltpu.VMEM((share, 3 * part), BF16),)
        if other
        else (pltpu.VMEM((share // 2, 3 * part), BF16),) * 2,
        [SMEM, HBM],
        (ids, pltpu.with_memory_space_constraint(w_qkv, pltpu.HBM)),
        4,
        scratch=(pltpu.VMEM((3, share, wide), BF16), pltpu.SemaphoreType.DMA((3,))),
    )


def local(tokens, cotangent, valid, visible, live, pos_table, norm_gain, norm_bias, w_qkv):
    slots, rows, width = tokens.shape
    groups = lax.axis_size("date")
    owners = lax.axis_size("tile")
    depth, triple = w_qkv.shape
    channels = triple // 3
    part = channels // groups
    dates = rows * groups
    ids = jnp.stack([lax.axis_index(name) for name in ("rep", "date", "tile")]).astype(jnp.int32)
    gain2, bias2 = norm_gain.reshape(1, width), norm_bias.reshape(1, width)

    chain = owners == 4 and lax.axis_size("rep") == 2 and depth % 64 == 0
    ring = [(0, 1), (1, 3), (3, 2), (2, 0)]
    share = depth // 2
    if chain:
        low, high = pick(w_qkv, ids, share, part, False)
        chains = []
        for held in (low, high):
            first = lax.ppermute(held, "tile", ring)
            if chains:
                (rest,) = pick(w_qkv, after(ids, held), share, part, True)
                first = after(first, rest)
            second = lax.ppermute(first, "tile", ring)
            first_other = swapped(first, "rep", 1)
            second = after(second, first_other)
            third = lax.ppermute(second, "tile", ring)
            second_other = swapped(second, "rep", 1)
            if not chains:
                third = after(third, second_other)
            third_other = swapped(third, "rep", 1)
            chains.append((first, first_other, second, second_other, third, third_other))
        first, later = chains[1][0], chains[1][2]
    else:
        first = later = ids

    across = call(
        functools.partial(pack_across_kernel, part),
        "pack_across",
        pltpu.VMEM((slots, rows, width + 2 * part), BF16),
        [SMEM, VMEM, VMEM],
        (after(ids, first), tokens, cotangent),
        6,
    )
    across = swapped(across, "date", 2)
    pair = pltpu.VMEM((2, slots, rows, part), BF16)
    beside, ups = call(
        functools.partial(pack_beside_kernel, part),
        "pack_beside",
        (pltpu.VMEM((slots, rows, 2 * width + 2 * part), BF16), pair),
        [SMEM, VMEM, VMEM, VMEM],
        (after(ids, later), tokens, cotangent, near(across)),
        6,
    )
    beside = swapped(beside, "date", 1)

    normed, unit, own_unit, own_inv = call(
        norm_kernel,
        "norm",
        (
            pltpu.VMEM((slots * dates, width), BF16),
            pltpu.VMEM((slots * dates, width), BF16),
            pltpu.VMEM((slots, rows, width), F32),
            pltpu.VMEM((slots, rows, 128), F32),
        ),
        [SMEM] + [VMEM] * 6,
        (visible, pos_table, gain2, bias2, tokens, near(across), near(beside)),
        12,
        microseconds=2,
    )
    whole = pltpu.VMEM((width, 3 * part), BF16)
    if chain:
        own = [near(piece) for piece in (low, high, rest)]
        pieces = [near(piece) for piece in chains[0] + chains[1][:4]]
        weights = call(
            functools.partial(place_kernel, depth),
            "place",
            whole,
            [SMEM] + [VMEM] * (len(own) + len(pieces)),
            (ids, *own, *pieces),
            4,
            microseconds=8,
        )
        pieces = [near(piece) for piece in chains[1][4:]]
    else:
        group = lax.axis_index("date")
        mine = [
            lax.dynamic_slice_in_dim(w_qkv, i * channels + group * part, part, 1) for i in range(3)
        ]
        weights = lax.all_gather(jnp.concatenate(mine, axis=1), "tile", axis=0, tiled=True)
        pieces = []

    piece = pltpu.VMEM((slots, rows, part), BF16)
    context, close_context, far_context, gqkv, weights = call(
        functools.partial(attend_kernel, len(pieces), depth),
        "attend",
        (
            piece,
            piece,
            pair,
            pltpu.VMEM((slots * dates, 3 * part), BF16),
            whole,
        ),
        [SMEM] * 2 + [VMEM] * (5 + len(pieces)),
        (ids, live, near(weights), near(normed), valid, near(ups), near(beside), *pieces),
        20,
        aliases=((2, 4),),
        scratch=(pltpu.VMEM((slots * dates, 3 * part), BF16),),
    )
    far_context = swapped(far_context, "date", 2)

    block = pltpu.VMEM((slots, rows, width), BF16)
    pairs = pltpu.VMEM((2, width), F32)
    stay, passing, cross, sums = call(
        back_kernel,
        "back",
        (block, block, pltpu.VMEM((2 * slots * rows, width), BF16), pairs),
        [VMEM] * 3,
        (near(gqkv), near(unit), near(weights)),
        12,
    )

    close = swapped(cross, "date", 1)
    tiles = [sums]
    if owners == 4:
        tiles += [swapped(sums, "tile", s) for s in range(1, owners)]
    both = call(
        both_kernel,
        "both",
        pair,
        [VMEM] * 2,
        (near(close_context), near(far_context)),
        2,
        microseconds=6.5,
    )
    close = after(close, both, *tiles[1:])
    chip = call(merge_kernel, "merge", block, [VMEM] * 2, (near(passing), near(close)), 6)
    far = swapped(chip, "date", 2)
    both = swapped(both, "date", 1)
    home, attended = call(
        home_kernel,
        "home",
        (pltpu.VMEM((slots, rows, width), F32), jax.ShapeDtypeStruct((slots, rows, channels), BF16)),
        [SMEM] + [VMEM] * 5,
        (ids, near(stay), near(close), near(context), near(both), near(far_context)),
        6,
        scratch=(pltpu.VMEM((groups, slots, rows, part), BF16),),
    )
    if owners == 4:
        tiles = [near(tile) for tile in tiles]
        total = call(add_kernel, "add", pairs, [VMEM] * owners, tiles, 2)
    else:
        total = lax.psum(sums, "tile")
    totals = [total] + [swapped(total, "date", s) for s in range(1, groups)]
    grad_tokens, grad_norm = call(
        finish_kernel,
        "finish",
        (
            jax.ShapeDtypeStruct((slots, rows, width), BF16),
            jax.ShapeDtypeStruct((2, width), F32),
        ),
        [SMEM] * 2 + [VMEM] * (5 + groups),
        (ids, live, near(own_unit), near(own_inv), gain2, near(home), near(far), *totals),
        6,
    )
    return attended, grad_tokens, grad_norm


def solution(mesh):
    in_specs = (
        P(("rep", "tile"), "date", None),
        P(("rep", "tile"), "date", None),
        P(("rep", "tile"), None),
        P(("rep", "tile")),
        P("rep"),
        P(),
        P(),
        P(),
        P("tile", None),
    )
    out_specs = (P(("rep", "tile"), "date", None), P(("rep", "tile"), "date", None), P("rep", None))
    return jax.shard_map(local, mesh=mesh, in_specs=in_specs, out_specs=out_specs, check_vma=False)
```

```python
import functools

import jax
import jax.numpy as jnp
from jax import lax
from jax.experimental import pallas as pl
from jax.experimental.pallas import tpu as pltpu
from jax.sharding import PartitionSpec as P

HEAD_DIM = 80
DG = 32
BLOCK_ROWS = 32
F32 = jnp.float32
BF16 = jnp.bfloat16

VMEM = pl.BlockSpec(memory_space=pltpu.VMEM)
SMEM = pl.BlockSpec(memory_space=pltpu.SMEM)
HBM = pl.BlockSpec(memory_space=pltpu.HBM)


def dot(a, b):
    return jnp.dot(a, b, preferred_element_type=F32)


def dot_nt(a, b):
    return lax.dot_general(a, b, (((1,), (1,)), ((), ())), preferred_element_type=F32)


def dot_tn(a, b):
    return lax.dot_general(a, b, (((0,), (0,)), ((), ())), preferred_element_type=F32)


def window_of(group, part):
    wide = -(-part // 128) * 128
    odd = lax.rem(group, 2)
    start = (group // 2) * (2 * part) + odd * (2 * part - wide)
    return start, wide, odd == 1


def pick_kernel(part, other, ids_ref, w_ref, *refs):
    out_refs, windows, sems = refs[:-2], refs[-2], refs[-1]
    height = windows.shape[1]
    channels = w_ref.shape[1] // 3
    half = 1 - ids_ref[0] if other else ids_ref[0]
    first = pl.multiple_of(half * height, 16)
    start, wide, odd = window_of(ids_ref[1], part)
    moves = [
        pltpu.make_async_copy(
            w_ref.at[pl.ds(first, height), pl.ds(pl.multiple_of(i * channels + start, 128), wide)],
            windows.at[i],
            sems.at[i],
        )
        for i in range(3)
    ]
    for move in moves:
        move.start()
    for move in moves:
        move.wait()
    pieces = []
    for i in range(3):
        window = windows[i]
        pieces.append(jnp.where(odd, window[:, wide - part :], window[:, :part]))
    picked = jnp.concatenate(pieces, axis=1)
    at = 0
    for out_ref in out_refs:
        out_ref[...] = picked[at : at + out_ref.shape[0]]
        at += out_ref.shape[0]


def chip_pair(ids_ref, part):
    pair = ids_ref[1] // 2
    return pl.multiple_of(pair * (2 * part), 128), pl.multiple_of((1 - pair) * (2 * part), 128)


def pack_across_kernel(part, ids_ref, tokens_ref, cotangent_ref, out_ref):
    width = tokens_ref.shape[2]
    theirs = chip_pair(ids_ref, part)[1]
    out_ref[:, :, :width] = tokens_ref[...]
    out_ref[:, :, width:] = cotangent_ref[:, :, pl.ds(theirs, 2 * part)]


def pack_beside_kernel(part, ids_ref, tokens_ref, cotangent_ref, across_ref, out_ref, up_ref):
    width = tokens_ref.shape[2]
    ours = chip_pair(ids_ref, part)[0]
    odd = lax.rem(ids_ref[1], 2) == 1
    out_ref[:, :, :width] = tokens_ref[...]
    out_ref[:, :, width : 2 * width] = across_ref[:, :, :width]
    theirs = []
    for i, block in enumerate((cotangent_ref[:, :, pl.ds(ours, 2 * part)], across_ref[:, :, width:])):
        low, high = block[:, :, :part], block[:, :, part:]
        up_ref[i] = jnp.where(odd, high, low)
        theirs.append(jnp.where(odd, low, high))
    out_ref[:, :, 2 * width :] = jnp.concatenate(theirs, axis=2)


def norm_kernel(visible_ref, pos_ref, gain_ref, bias_ref, tokens_ref, across_ref, beside_ref, *refs):
    normed_ref, unit_ref, own_unit_ref, own_inv_ref = refs
    slots, rows, width = tokens_ref.shape
    gain = gain_ref[...]
    bias = bias_ref[...]
    for p in range(slots):
        iota = lax.broadcasted_iota(jnp.int32, (8, pos_ref.shape[0]), 1)
        onehot = (iota == visible_ref[p]).astype(F32).astype(BF16)
        position = dot(onehot, pos_ref[...])[0:1]
        groups = (
            tokens_ref[p],
            beside_ref[p, :, :width],
            across_ref[p, :, :width],
            beside_ref[p, :, width : 2 * width],
        )
        for s, tokens in enumerate(groups):
            embedded = (tokens.astype(F32) + position).astype(BF16).astype(F32)
            centred = embedded - jnp.mean(embedded, axis=-1, keepdims=True)
            inv_std = lax.rsqrt(jnp.mean(centred * centred, axis=-1, keepdims=True) + 1e-06)
            unit = centred * inv_std
            at = (p * len(groups) + s) * rows
            normed_ref[at : at + rows] = (unit * gain + bias).astype(BF16)
            unit_ref[at : at + rows] = unit.astype(BF16)
            if s == 0:
                own_unit_ref[p] = unit
                own_inv_ref[p] = jnp.broadcast_to(inv_std, own_inv_ref.shape[1:])


def put_pieces(ids_ref, depth, offset, steps, piece_refs, weights):
    owners = 4
    rep, owner = ids_ref[0], ids_ref[2]
    share = depth // 2
    spot = owner ^ (owner >> 1)
    for i, ref in enumerate(piece_refs):
        back = lax.rem(spot + owners - steps[i // 2], owners)
        half = 1 - rep if i % 2 else rep
        first = (back ^ (back >> 1)) * depth + half * share + offset
        weights[pl.ds(pl.multiple_of(first, 16), ref.shape[0]), :] = ref[...]


def place_kernel(depth, ids_ref, low_ref, high_ref, rest_ref, *refs):
    weights = refs[-1]
    rep, own = ids_ref[0], ids_ref[2] * depth
    share = depth // 2
    low = pl.multiple_of(own + rep * share, 16)
    weights[pl.ds(low, low_ref.shape[0]), :] = low_ref[...]
    high = pl.multiple_of(own + rep * share + low_ref.shape[0], 16)
    weights[pl.ds(high, high_ref.shape[0]), :] = high_ref[...]
    rest = pl.multiple_of(own + (1 - rep) * share, 16)
    weights[pl.ds(rest, rest_ref.shape[0]), :] = rest_ref[...]
    put_pieces(ids_ref, depth, 0, (1, 2, 3), refs[:6], weights)
    put_pieces(ids_ref, depth, depth // 4, (1, 2), refs[6:-1], weights)


def attend_kernel(
    count, depth, ids_ref, live_ref, _, normed_ref, valid_ref, up_ref, beside_ref, *refs
):
    piece_refs = refs[:count]
    own_ref, close_ref, across_ref, gqkv_ref, weights, qkv_ref = refs[count:]
    _, slots, rows, channels = up_ref.shape
    dates = valid_ref.shape[1]
    heads = channels // HEAD_DIM
    inv_scale = 1.0 / HEAD_DIM**0.5
    if count:
        put_pieces(ids_ref, depth, depth // 4, (3,), piece_refs, weights)
    qkv_ref[...] = dot(normed_ref[...], weights[...]).astype(BF16)
    row = lax.broadcasted_iota(jnp.int32, (dates, dates), 0)
    column = lax.broadcasted_iota(jnp.int32, (dates, dates), 1)
    same_date = column == (row ^ (ids_ref[1] * rows))
    for p in range(slots):
        span = slice(p * dates, (p + 1) * dates)
        alive = (live_ref[ids_ref[2]] > p // (BLOCK_ROWS // DG)).astype(F32)
        rows_qkv = qkv_ref[span, :]
        others = beside_ref[p, :, beside_ref.shape[2] - 2 * channels :]
        upstream = [up_ref[0, p], others[:, :channels], up_ref[1, p], others[:, channels:]]
        upstream = jnp.concatenate(upstream, axis=0) * alive.astype(BF16)
        valid = valid_ref[p : p + 1, :].astype(F32)
        allowed = jnp.sum(jnp.where(same_date, valid, 0.0), axis=1, keepdims=True) > 0
        grads = [[], [], []]
        contexts = []
        for h in range(heads):
            q, k, v = (
                rows_qkv[:, i * channels + h * HEAD_DIM : i * channels + (h + 1) * HEAD_DIM]
                for i in range(3)
            )
            up = upstream[:, h * HEAD_DIM : (h + 1) * HEAD_DIM]
            scores = jnp.where(allowed, dot_nt(k, q) * inv_scale, -1e30)
            exps = jnp.exp(scores - jnp.max(scores, axis=0, keepdims=True))
            probs = exps * (1.0 / jnp.sum(exps, axis=0, keepdims=True))
            low = probs.astype(BF16)
            contexts.append(dot_tn(low, v) * alive)
            grads[2].append(dot(low, up))
            gprobs = dot_nt(v, up)
            gscores = probs * (gprobs - jnp.sum(probs * gprobs, axis=0, keepdims=True)) * inv_scale
            glow = gscores.astype(BF16)
            grads[0].append(dot_tn(glow, k))
            grads[1].append(dot(glow, q))
        gqkv_ref[span, :] = jnp.concatenate(grads[0] + grads[1] + grads[2], axis=1).astype(BF16)
        context = jnp.concatenate(contexts, axis=1).astype(BF16)
        for s, out in enumerate((own_ref, close_ref, across_ref.at[0], across_ref.at[1])):
            out[p] = context[s * rows : (s + 1) * rows]


def back_kernel(gqkv_ref, unit_ref, weights, stay_ref, pass_ref, cross_ref, sums_ref):
    slots, rows, width = stay_ref.shape
    dates = gqkv_ref.shape[0] // slots
    tail = 2 * slots * rows
    step = 256
    for n in range(width // step):
        lanes = slice(n * step, (n + 1) * step)
        partial = dot_nt(gqkv_ref[...], weights[lanes, :])
        low = partial.astype(BF16)
        for p in range(slots):
            for s in range(dates // rows):
                block = low[p * dates + s * rows : p * dates + (s + 1) * rows]
                if s % 2:
                    at = (s // 2 * slots + p) * rows
                    cross_ref[at : at + rows, lanes] = block
                else:
                    (pass_ref if s else stay_ref)[p, :, lanes] = block
        gain_sum = jnp.sum(partial * unit_ref[:, lanes].astype(F32), axis=0, keepdims=True)
        sums = jnp.concatenate([gain_sum, jnp.sum(partial, axis=0, keepdims=True)], axis=0)
        sums_ref[:, lanes] = sums
        high = sums.astype(BF16)
        rest = (sums - high.astype(F32)).astype(BF16)
        fill = jnp.zeros((cross_ref.shape[0] - tail - 4, step), BF16)
        cross_ref[tail:, lanes] = jnp.concatenate([high, rest, fill], axis=0)


def merge_kernel(pass_ref, close_ref, sums_ref, out_ref, total_ref):
    slots, rows, width = out_ref.shape
    for p in range(slots):
        at = (slots + p) * rows
        out_ref[p] = (pass_ref[p].astype(F32) + close_ref[at : at + rows].astype(F32)).astype(BF16)
    sums = close_ref[2 * slots * rows :].astype(F32)
    total_ref[...] = sums_ref[...] + sums[0:2] + sums[2:4]


def both_kernel(close_ref, far_ref, both_ref):
    both_ref[0] = close_ref[...]
    both_ref[1] = far_ref[1]


def add_kernel(*refs):
    total = refs[0][...]
    for ref in refs[1:-1]:
        total = total + ref[...]
    refs[-1][...] = total


def home_kernel(ids_ref, stay_ref, close_ref, own_ref, beside_ref, across_ref, grad_ref, attended_ref, held):
    slots, rows, width = grad_ref.shape
    group = ids_ref[1]
    held[group] = own_ref[...]
    held[group ^ 1] = beside_ref[0]
    held[group ^ 2] = across_ref[0]
    held[group ^ 3] = beside_ref[1]
    for p in range(slots):
        close = close_ref[p * rows : (p + 1) * rows].astype(F32)
        grad_ref[p] = stay_ref[p].astype(F32) + close
        attended_ref[p] = jnp.concatenate([held[g, p] for g in range(held.shape[0])], axis=1)


def finish_kernel(ids_ref, live_ref, unit_ref, inv_ref, gain_ref, grad_ref, far_ref, *refs):
    out_ref, norm_ref = refs[-2:]
    slots = unit_ref.shape[0]
    gain = gain_ref[...]
    for p in range(slots):
        alive = (live_ref[ids_ref[2]] > p // (BLOCK_ROWS // DG)).astype(F32)
        unit = unit_ref[p]
        scaled = (grad_ref[p] + far_ref[p].astype(F32)) * gain
        out = inv_ref[p][:, 0:1] * (
            scaled
            - jnp.mean(scaled, axis=-1, keepdims=True)
            - unit * jnp.mean(scaled * unit, axis=-1, keepdims=True)
        )
        out_ref[p] = (out * alive).astype(BF16)
    total = refs[0][...]
    for ref in refs[1:-2]:
        total = total + ref[...]
    norm_ref[...] = total


def swapped(array, axis, bits):
    return lax.ppermute(array, axis, [(i, i ^ bits) for i in range(lax.axis_size(axis))])


def after(array, *others):
    return lax.optimization_barrier((array, *others))[0]


def near(array):
    return pltpu.with_memory_space_constraint(array, pltpu.VMEM)


def call(kernel, name, out_shape, in_specs, args, megabytes, scratch=(), microseconds=0.01, aliases=()):
    return pl.pallas_call(
        kernel,
        out_shape=out_shape,
        in_specs=in_specs,
        out_specs=jax.tree.map(lambda _: VMEM, out_shape),
        scratch_shapes=list(scratch),
        input_output_aliases=dict(aliases),
        compiler_params=pltpu.CompilerParams(vmem_limit_bytes=megabytes * 1024 * 1024),
        cost_estimate=pl.CostEstimate(
            flops=int(microseconds * 10**9), bytes_accessed=1000, transcendentals=0
        ),
        name=name,
    )(*args)


def pick(w_qkv, ids, share, part, other):
    wide = -(-part // 128) * 128
    return call(
        functools.partial(pick_kernel, part, other),
        "pick",
        (pltpu.VMEM((share, 3 * part), BF16),)
        if other
        else (pltpu.VMEM((share // 2, 3 * part), BF16),) * 2,
        [SMEM, HBM],
        (ids, pltpu.with_memory_space_constraint(w_qkv, pltpu.HBM)),
        4,
        scratch=(pltpu.VMEM((3, share, wide), BF16), pltpu.SemaphoreType.DMA((3,))),
    )


def local(tokens, cotangent, valid, visible, live, pos_table, norm_gain, norm_bias, w_qkv):
    slots, rows, width = tokens.shape
    groups = lax.axis_size("date")
    owners = lax.axis_size("tile")
    depth, triple = w_qkv.shape
    channels = triple // 3
    part = channels // groups
    dates = rows * groups
    ids = jnp.stack([lax.axis_index(name) for name in ("rep", "date", "tile")]).astype(jnp.int32)
    gain2, bias2 = norm_gain.reshape(1, width), norm_bias.reshape(1, width)

    chain = owners == 4 and lax.axis_size("rep") == 2 and depth % 64 == 0
    ring = [(0, 1), (1, 3), (3, 2), (2, 0)]
    share = depth // 2
    if chain:
        low, high = pick(w_qkv, ids, share, part, False)
        chains = []
        for held in (low, high):
            first = lax.ppermute(held, "tile", ring)
            if chains:
                (rest,) = pick(w_qkv, after(ids, held), share, part, True)
                first = after(first, rest)
            second = lax.ppermute(first, "tile", ring)
            first_other = swapped(first, "rep", 1)
            second = after(second, first_other)
            third = lax.ppermute(second, "tile", ring)
            second_other = swapped(second, "rep", 1)
            if not chains:
                third = after(third, second_other)
            third_other = swapped(third, "rep", 1)
            chains.append((first, first_other, second, second_other, third, third_other))
        first, later = chains[1][0], chains[1][2]
    else:
        first = later = ids

    across = call(
        functools.partial(pack_across_kernel, part),
        "pack_across",
        pltpu.VMEM((slots, rows, width + 2 * part), BF16),
        [SMEM, VMEM, VMEM],
        (after(ids, first), tokens, cotangent),
        6,
    )
    across = swapped(across, "date", 2)
    pair = pltpu.VMEM((2, slots, rows, part), BF16)
    beside, ups = call(
        functools.partial(pack_beside_kernel, part),
        "pack_beside",
        (pltpu.VMEM((slots, rows, 2 * width + 2 * part), BF16), pair),
        [SMEM, VMEM, VMEM, VMEM],
        (after(ids, later), tokens, cotangent, near(across)),
        6,
    )
    beside = swapped(beside, "date", 1)

    normed, unit, own_unit, own_inv = call(
        norm_kernel,
        "norm",
        (
            pltpu.VMEM((slots * dates, width), BF16),
            pltpu.VMEM((slots * dates, width), BF16),
            pltpu.VMEM((slots, rows, width), F32),
            pltpu.VMEM((slots, rows, 128), F32),
        ),
        [SMEM] + [VMEM] * 6,
        (visible, pos_table, gain2, bias2, tokens, near(across), near(beside)),
        12,
        microseconds=2,
    )
    whole = pltpu.VMEM((width, 3 * part), BF16)
    if chain:
        own = [near(piece) for piece in (low, high, rest)]
        pieces = [near(piece) for piece in chains[0] + chains[1][:4]]
        weights = call(
            functools.partial(place_kernel, depth),
            "place",
            whole,
            [SMEM] + [VMEM] * (len(own) + len(pieces)),
            (ids, *own, *pieces),
            4,
            microseconds=8,
        )
        pieces = [near(piece) for piece in chains[1][4:]]
    else:
        group = lax.axis_index("date")
        mine = [
            lax.dynamic_slice_in_dim(w_qkv, i * channels + group * part, part, 1) for i in range(3)
        ]
        weights = lax.all_gather(jnp.concatenate(mine, axis=1), "tile", axis=0, tiled=True)
        pieces = []

    piece = pltpu.VMEM((slots, rows, part), BF16)
    context, close_context, far_context, gqkv, weights = call(
        functools.partial(attend_kernel, len(pieces), depth),
        "attend",
        (
            piece,
            piece,
            pair,
            pltpu.VMEM((slots * dates, 3 * part), BF16),
            whole,
        ),
        [SMEM] * 2 + [VMEM] * (5 + len(pieces)),
        (ids, live, near(weights), near(normed), valid, near(ups), near(beside), *pieces),
        20,
        aliases=((2, 4),),
        scratch=(pltpu.VMEM((slots * dates, 3 * part), BF16),),
    )
    far_context = swapped(far_context, "date", 2)

    block = pltpu.VMEM((slots, rows, width), BF16)
    pairs = pltpu.VMEM((2, width), F32)
    stay, passing, cross, sums = call(
        back_kernel,
        "back",
        (block, block, pltpu.VMEM((2 * slots * rows + 16, width), BF16), pairs),
        [VMEM] * 3,
        (near(gqkv), near(unit), near(weights)),
        12,
    )

    close = swapped(cross, "date", 1)
    chip, total = call(
        merge_kernel,
        "merge",
        (block, pairs),
        [VMEM] * 3,
        (near(passing), near(close), near(sums)),
        6,
    )
    far = swapped(chip, "date", 2)
    if owners == 4:
        total = call(
            add_kernel,
            "add",
            pairs,
            [VMEM] * owners,
            [near(total)] + [near(swapped(total, "tile", s)) for s in range(1, owners)],
            2,
        )
    else:
        total = lax.psum(total, "tile")
    far_total = swapped(total, "date", 2)
    far_context = after(far_context, total)
    both = call(both_kernel, "both", pair, [VMEM] * 2, (near(close_context), near(far_context)), 2)
    both = swapped(both, "date", 1)
    home, attended = call(
        home_kernel,
        "home",
        (pltpu.VMEM((slots, rows, width), F32), jax.ShapeDtypeStruct((slots, rows, channels), BF16)),
        [SMEM] + [VMEM] * 5,
        (ids, near(stay), near(close), near(context), near(both), near(far_context)),
        6,
        scratch=(pltpu.VMEM((groups, slots, rows, part), BF16),),
    )
    grad_tokens, grad_norm = call(
        finish_kernel,
        "finish",
        (
            jax.ShapeDtypeStruct((slots, rows, width), BF16),
            jax.ShapeDtypeStruct((2, width), F32),
        ),
        [SMEM] * 2 + [VMEM] * 7,
        (ids, live, near(own_unit), near(own_inv), gain2, near(home), near(far), total, far_total),
        6,
    )
    return attended, grad_tokens, grad_norm


def solution(mesh):
    in_specs = (
        P(("rep", "tile"), "date", None),
        P(("rep", "tile"), "date", None),
        P(("rep", "tile"), None),
        P(("rep", "tile")),
        P("rep"),
        P(),
        P(),
        P(),
        P("tile", None),
    )
    out_specs = (P(("rep", "tile"), "date", None), P(("rep", "tile"), "date", None), P("rep", None))
    return jax.shard_map(local, mesh=mesh, in_specs=in_specs, out_specs=out_specs, check_vma=False)
```

```python
import functools

import jax
import jax.numpy as jnp
from jax import lax
from jax.experimental import pallas as pl
from jax.experimental.pallas import tpu as pltpu
from jax.sharding import PartitionSpec as P

HEAD_DIM = 80
DG = 32
BLOCK_ROWS = 32
F32 = jnp.float32
BF16 = jnp.bfloat16

VMEM = pl.BlockSpec(memory_space=pltpu.VMEM)
SMEM = pl.BlockSpec(memory_space=pltpu.SMEM)
HBM = pl.BlockSpec(memory_space=pltpu.HBM)


def dot(a, b):
    return jnp.dot(a, b, preferred_element_type=F32)


def dot_nt(a, b):
    return lax.dot_general(a, b, (((1,), (1,)), ((), ())), preferred_element_type=F32)


def dot_tn(a, b):
    return lax.dot_general(a, b, (((0,), (0,)), ((), ())), preferred_element_type=F32)


def window_of(group, part):
    wide = -(-part // 128) * 128
    odd = lax.rem(group, 2)
    start = (group // 2) * (2 * part) + odd * (2 * part - wide)
    return start, wide, odd == 1


def pick_kernel(part, other, ids_ref, w_ref, *refs):
    out_refs, windows, sems = refs[:-2], refs[-2], refs[-1]
    height = windows.shape[1]
    channels = w_ref.shape[1] // 3
    half = 1 - ids_ref[0] if other else ids_ref[0]
    first = pl.multiple_of(half * height, 16)
    start, wide, odd = window_of(ids_ref[1], part)
    moves = [
        pltpu.make_async_copy(
            w_ref.at[pl.ds(first, height), pl.ds(pl.multiple_of(i * channels + start, 128), wide)],
            windows.at[i],
            sems.at[i],
        )
        for i in range(3)
    ]
    for move in moves:
        move.start()
    for move in moves:
        move.wait()
    pieces = []
    for i in range(3):
        window = windows[i]
        pieces.append(jnp.where(odd, window[:, wide - part :], window[:, :part]))
    picked = jnp.concatenate(pieces, axis=1)
    at = 0
    for out_ref in out_refs:
        out_ref[...] = picked[at : at + out_ref.shape[0]]
        at += out_ref.shape[0]


def chip_pair(ids_ref, part):
    pair = ids_ref[1] // 2
    return pl.multiple_of(pair * (2 * part), 128), pl.multiple_of((1 - pair) * (2 * part), 128)


def pack_across_kernel(part, ids_ref, tokens_ref, cotangent_ref, out_ref):
    width = tokens_ref.shape[2]
    theirs = chip_pair(ids_ref, part)[1]
    out_ref[:, :, :width] = tokens_ref[...]
    out_ref[:, :, width:] = cotangent_ref[:, :, pl.ds(theirs, 2 * part)]


def pack_beside_kernel(part, ids_ref, tokens_ref, cotangent_ref, across_ref, out_ref, up_ref):
    width = tokens_ref.shape[2]
    ours = chip_pair(ids_ref, part)[0]
    odd = lax.rem(ids_ref[1], 2) == 1
    out_ref[:, :, :width] = tokens_ref[...]
    out_ref[:, :, width : 2 * width] = across_ref[:, :, :width]
    theirs = []
    for i, block in enumerate((cotangent_ref[:, :, pl.ds(ours, 2 * part)], across_ref[:, :, width:])):
        low, high = block[:, :, :part], block[:, :, part:]
        up_ref[i] = jnp.where(odd, high, low)
        theirs.append(jnp.where(odd, low, high))
    out_ref[:, :, 2 * width :] = jnp.concatenate(theirs, axis=2)


def norm_kernel(visible_ref, pos_ref, gain_ref, bias_ref, tokens_ref, across_ref, beside_ref, *refs):
    normed_ref, unit_ref, own_unit_ref, own_inv_ref = refs
    slots, rows, width = tokens_ref.shape
    gain = gain_ref[...]
    bias = bias_ref[...]
    for p in range(slots):
        iota = lax.broadcasted_iota(jnp.int32, (8, pos_ref.shape[0]), 1)
        onehot = (iota == visible_ref[p]).astype(F32).astype(BF16)
        position = dot(onehot, pos_ref[...])[0:1]
        groups = (
            tokens_ref[p],
            beside_ref[p, :, :width],
            across_ref[p, :, :width],
            beside_ref[p, :, width : 2 * width],
        )
        for s, tokens in enumerate(groups):
            embedded = (tokens.astype(F32) + position).astype(BF16).astype(F32)
            centred = embedded - jnp.mean(embedded, axis=-1, keepdims=True)
            inv_std = lax.rsqrt(jnp.mean(centred * centred, axis=-1, keepdims=True) + 1e-06)
            unit = centred * inv_std
            at = (p * len(groups) + s) * rows
            normed_ref[at : at + rows] = (unit * gain + bias).astype(BF16)
            unit_ref[at : at + rows] = unit.astype(BF16)
            if s == 0:
                own_unit_ref[p] = unit
                own_inv_ref[p] = jnp.broadcast_to(inv_std, own_inv_ref.shape[1:])


def put_pieces(ids_ref, depth, offset, steps, piece_refs, weights):
    owners = 4
    rep, owner = ids_ref[0], ids_ref[2]
    share = depth // 2
    spot = owner ^ (owner >> 1)
    for i, ref in enumerate(piece_refs):
        back = lax.rem(spot + owners - steps[i // 2], owners)
        half = 1 - rep if i % 2 else rep
        first = (back ^ (back >> 1)) * depth + half * share + offset
        weights[pl.ds(pl.multiple_of(first, 16), ref.shape[0]), :] = ref[...]


def place_kernel(depth, ids_ref, low_ref, high_ref, rest_ref, *refs):
    weights = refs[-1]
    rep, own = ids_ref[0], ids_ref[2] * depth
    share = depth // 2
    low = pl.multiple_of(own + rep * share, 16)
    weights[pl.ds(low, low_ref.shape[0]), :] = low_ref[...]
    high = pl.multiple_of(own + rep * share + low_ref.shape[0], 16)
    weights[pl.ds(high, high_ref.shape[0]), :] = high_ref[...]
    rest = pl.multiple_of(own + (1 - rep) * share, 16)
    weights[pl.ds(rest, rest_ref.shape[0]), :] = rest_ref[...]
    put_pieces(ids_ref, depth, 0, (1, 2, 3), refs[:6], weights)
    put_pieces(ids_ref, depth, depth // 4, (1, 2), refs[6:-1], weights)


def attend_kernel(
    count, depth, ids_ref, live_ref, _, normed_ref, valid_ref, up_ref, beside_ref, *refs
):
    piece_refs = refs[:count]
    own_ref, close_ref, across_ref, gqkv_ref, weights, qkv_ref = refs[count:]
    _, slots, rows, channels = up_ref.shape
    dates = valid_ref.shape[1]
    heads = channels // HEAD_DIM
    inv_scale = 1.0 / HEAD_DIM**0.5
    if count:
        put_pieces(ids_ref, depth, depth // 4, (3,), piece_refs, weights)
    qkv_ref[...] = dot(normed_ref[...], weights[...]).astype(BF16)
    row = lax.broadcasted_iota(jnp.int32, (dates, dates), 0)
    column = lax.broadcasted_iota(jnp.int32, (dates, dates), 1)
    same_date = column == (row ^ (ids_ref[1] * rows))
    for p in range(slots):
        span = slice(p * dates, (p + 1) * dates)
        alive = (live_ref[ids_ref[2]] > p // (BLOCK_ROWS // DG)).astype(F32)
        rows_qkv = qkv_ref[span, :]
        others = beside_ref[p, :, beside_ref.shape[2] - 2 * channels :]
        upstream = [up_ref[0, p], others[:, :channels], up_ref[1, p], others[:, channels:]]
        upstream = jnp.concatenate(upstream, axis=0) * alive.astype(BF16)
        valid = valid_ref[p : p + 1, :].astype(F32)
        allowed = jnp.sum(jnp.where(same_date, valid, 0.0), axis=1, keepdims=True) > 0
        grads = [[], [], []]
        contexts = []
        for h in range(heads):
            q, k, v = (
                rows_qkv[:, i * channels + h * HEAD_DIM : i * channels + (h + 1) * HEAD_DIM]
                for i in range(3)
            )
            up = upstream[:, h * HEAD_DIM : (h + 1) * HEAD_DIM]
            scores = jnp.where(allowed, dot_nt(k, q) * inv_scale, -1e30)
            exps = jnp.exp(scores - jnp.max(scores, axis=0, keepdims=True))
            probs = exps * (1.0 / jnp.sum(exps, axis=0, keepdims=True))
            low = probs.astype(BF16)
            contexts.append(dot_tn(low, v) * alive)
            grads[2].append(dot(low, up))
            gprobs = dot_nt(v, up)
            gscores = probs * (gprobs - jnp.sum(probs * gprobs, axis=0, keepdims=True)) * inv_scale
            glow = gscores.astype(BF16)
            grads[0].append(dot_tn(glow, k))
            grads[1].append(dot(glow, q))
        gqkv_ref[span, :] = jnp.concatenate(grads[0] + grads[1] + grads[2], axis=1).astype(BF16)
        context = jnp.concatenate(contexts, axis=1).astype(BF16)
        for s, out in enumerate((own_ref, close_ref, across_ref.at[0], across_ref.at[1])):
            out[p] = context[s * rows : (s + 1) * rows]


def back_kernel(gqkv_ref, unit_ref, weights, stay_ref, pass_ref, cross_ref, sums_ref):
    slots, rows, width = stay_ref.shape
    dates = gqkv_ref.shape[0] // slots
    tail = 2 * slots * rows
    step = 256
    for n in range(width // step):
        lanes = slice(n * step, (n + 1) * step)
        partial = dot_nt(gqkv_ref[...], weights[lanes, :])
        low = partial.astype(BF16)
        for p in range(slots):
            for s in range(dates // rows):
                block = low[p * dates + s * rows : p * dates + (s + 1) * rows]
                if s % 2:
                    at = (s // 2 * slots + p) * rows
                    cross_ref[at : at + rows, lanes] = block
                else:
                    (pass_ref if s else stay_ref)[p, :, lanes] = block
        gain_sum = jnp.sum(partial * unit_ref[:, lanes].astype(F32), axis=0, keepdims=True)
        sums = jnp.concatenate([gain_sum, jnp.sum(partial, axis=0, keepdims=True)], axis=0)
        sums_ref[:, lanes] = sums
        high = sums.astype(BF16)
        rest = (sums - high.astype(F32)).astype(BF16)
        fill = jnp.zeros((cross_ref.shape[0] - tail - 4, step), BF16)
        cross_ref[tail:, lanes] = jnp.concatenate([high, rest, fill], axis=0)


def merge_kernel(pass_ref, close_ref, sums_ref, out_ref, total_ref):
    slots, rows, width = out_ref.shape
    for p in range(slots):
        at = (slots + p) * rows
        out_ref[p] = (pass_ref[p].astype(F32) + close_ref[at : at + rows].astype(F32)).astype(BF16)
    sums = close_ref[2 * slots * rows :].astype(F32)
    total_ref[...] = sums_ref[...] + sums[0:2] + sums[2:4]


def both_kernel(close_ref, far_ref, both_ref):
    both_ref[0] = close_ref[...]
    both_ref[1] = far_ref[1]


def add_kernel(*refs):
    total = refs[0][...]
    for ref in refs[1:-1]:
        total = total + ref[...]
    refs[-1][...] = total


def home_kernel(ids_ref, stay_ref, close_ref, own_ref, beside_ref, across_ref, grad_ref, attended_ref, held):
    slots, rows, width = grad_ref.shape
    group = ids_ref[1]
    held[group] = own_ref[...]
    held[group ^ 1] = beside_ref[0]
    held[group ^ 2] = across_ref[0]
    held[group ^ 3] = beside_ref[1]
    for p in range(slots):
        close = close_ref[p * rows : (p + 1) * rows].astype(F32)
        grad_ref[p] = stay_ref[p].astype(F32) + close
        attended_ref[p] = jnp.concatenate([held[g, p] for g in range(held.shape[0])], axis=1)


def finish_kernel(ids_ref, live_ref, unit_ref, inv_ref, gain_ref, grad_ref, far_ref, *refs):
    out_ref, norm_ref = refs[-2:]
    slots = unit_ref.shape[0]
    gain = gain_ref[...]
    for p in range(slots):
        alive = (live_ref[ids_ref[2]] > p // (BLOCK_ROWS // DG)).astype(F32)
        unit = unit_ref[p]
        scaled = (grad_ref[p] + far_ref[p].astype(F32)) * gain
        out = inv_ref[p][:, 0:1] * (
            scaled
            - jnp.mean(scaled, axis=-1, keepdims=True)
            - unit * jnp.mean(scaled * unit, axis=-1, keepdims=True)
        )
        out_ref[p] = (out * alive).astype(BF16)
    total = refs[0][...]
    for ref in refs[1:-2]:
        total = total + ref[...]
    norm_ref[...] = total


def swapped(array, axis, bits):
    return lax.ppermute(array, axis, [(i, i ^ bits) for i in range(lax.axis_size(axis))])


def after(array, *others):
    return lax.optimization_barrier((array, *others))[0]


def near(array):
    return pltpu.with_memory_space_constraint(array, pltpu.VMEM)


def call(kernel, name, out_shape, in_specs, args, megabytes, scratch=(), microseconds=0.01, aliases=()):
    return pl.pallas_call(
        kernel,
        out_shape=out_shape,
        in_specs=in_specs,
        out_specs=jax.tree.map(lambda _: VMEM, out_shape),
        scratch_shapes=list(scratch),
        input_output_aliases=dict(aliases),
        compiler_params=pltpu.CompilerParams(vmem_limit_bytes=megabytes * 1024 * 1024),
        cost_estimate=pl.CostEstimate(
            flops=int(microseconds * 10**9), bytes_accessed=1000, transcendentals=0
        ),
        name=name,
    )(*args)


def pick(w_qkv, ids, share, part, other):
    wide = -(-part // 128) * 128
    return call(
        functools.partial(pick_kernel, part, other),
        "pick",
        (pltpu.VMEM((share, 3 * part), BF16),)
        if other
        else (pltpu.VMEM((share // 2, 3 * part), BF16),) * 2,
        [SMEM, HBM],
        (ids, pltpu.with_memory_space_constraint(w_qkv, pltpu.HBM)),
        4,
        scratch=(pltpu.VMEM((3, share, wide), BF16), pltpu.SemaphoreType.DMA((3,))),
    )


def local(tokens, cotangent, valid, visible, live, pos_table, norm_gain, norm_bias, w_qkv):
    slots, rows, width = tokens.shape
    groups = lax.axis_size("date")
    owners = lax.axis_size("tile")
    depth, triple = w_qkv.shape
    channels = triple // 3
    part = channels // groups
    dates = rows * groups
    ids = jnp.stack([lax.axis_index(name) for name in ("rep", "date", "tile")]).astype(jnp.int32)
    gain2, bias2 = norm_gain.reshape(1, width), norm_bias.reshape(1, width)

    chain = owners == 4 and lax.axis_size("rep") == 2 and depth % 64 == 0
    ring = [(0, 1), (1, 3), (3, 2), (2, 0)]
    share = depth // 2
    if chain:
        low, high = pick(w_qkv, ids, share, part, False)
        chains = []
        for held in (low, high):
            first = lax.ppermute(held, "tile", ring)
            if chains:
                (rest,) = pick(w_qkv, after(ids, held), share, part, True)
                first = after(first, rest)
            second = lax.ppermute(first, "tile", ring)
            first_other = swapped(first, "rep", 1)
            second = after(second, first_other)
            third = lax.ppermute(second, "tile", ring)
            second_other = swapped(second, "rep", 1)
            third_other = swapped(third, "rep", 1)
            chains.append((first, first_other, second, second_other, third, third_other))
        first, later = chains[1][0], (chains[1][2], chains[0][3])
    else:
        first, later = ids, ()

    across = call(
        functools.partial(pack_across_kernel, part),
        "pack_across",
        pltpu.VMEM((slots, rows, width + 2 * part), BF16),
        [SMEM, VMEM, VMEM],
        (after(ids, first), tokens, cotangent),
        6,
    )
    across = swapped(across, "date", 2)
    pair = pltpu.VMEM((2, slots, rows, part), BF16)
    beside, ups = call(
        functools.partial(pack_beside_kernel, part),
        "pack_beside",
        (pltpu.VMEM((slots, rows, 2 * width + 2 * part), BF16), pair),
        [SMEM, VMEM, VMEM, VMEM],
        (after(ids, *later), tokens, cotangent, near(across)),
        6,
    )
    beside = swapped(beside, "date", 1)

    normed, unit, own_unit, own_inv = call(
        norm_kernel,
        "norm",
        (
            pltpu.VMEM((slots * dates, width), BF16),
            pltpu.VMEM((slots * dates, width), BF16),
            pltpu.VMEM((slots, rows, width), F32),
            pltpu.VMEM((slots, rows, 128), F32),
        ),
        [SMEM] + [VMEM] * 6,
        (visible, pos_table, gain2, bias2, tokens, near(across), near(beside)),
        12,
        microseconds=2,
    )
    whole = pltpu.VMEM((width, 3 * part), BF16)
    if chain:
        own = [near(piece) for piece in (low, high, rest)]
        pieces = [near(piece) for piece in chains[0] + chains[1][:4]]
        weights = call(
            functools.partial(place_kernel, depth),
            "place",
            whole,
            [SMEM] + [VMEM] * (len(own) + len(pieces)),
            (ids, *own, *pieces),
            4,
            microseconds=8,
        )
        pieces = [near(piece) for piece in chains[1][4:]]
    else:
        group = lax.axis_index("date")
        mine = [
            lax.dynamic_slice_in_dim(w_qkv, i * channels + group * part, part, 1) for i in range(3)
        ]
        weights = lax.all_gather(jnp.concatenate(mine, axis=1), "tile", axis=0, tiled=True)
        pieces = []

    piece = pltpu.VMEM((slots, rows, part), BF16)
    context, close_context, far_context, gqkv, weights = call(
        functools.partial(attend_kernel, len(pieces), depth),
        "attend",
        (
            piece,
            piece,
            pair,
            pltpu.VMEM((slots * dates, 3 * part), BF16),
            whole,
        ),
        [SMEM] * 2 + [VMEM] * (5 + len(pieces)),
        (ids, live, near(weights), near(normed), valid, near(ups), near(beside), *pieces),
        20,
        aliases=((2, 4),),
        scratch=(pltpu.VMEM((slots * dates, 3 * part), BF16),),
    )
    far_context = swapped(far_context, "date", 2)

    block = pltpu.VMEM((slots, rows, width), BF16)
    pairs = pltpu.VMEM((2, width), F32)
    stay, passing, cross, sums = call(
        back_kernel,
        "back",
        (block, block, pltpu.VMEM((2 * slots * rows + 16, width), BF16), pairs),
        [VMEM] * 3,
        (near(gqkv), near(unit), near(weights)),
        12,
    )

    close = swapped(cross, "date", 1)
    chip, total = call(
        merge_kernel,
        "merge",
        (block, pairs),
        [VMEM] * 3,
        (near(passing), near(close), near(sums)),
        6,
    )
    far = swapped(chip, "date", 2)
    if owners == 4:
        total = call(
            add_kernel,
            "add",
            pairs,
            [VMEM] * owners,
            [near(total)] + [near(swapped(total, "tile", s)) for s in range(1, owners)],
            2,
        )
    else:
        total = lax.psum(total, "tile")
    far_total = swapped(total, "date", 2)
    far_context = after(far_context, total)
    both = call(both_kernel, "both", pair, [VMEM] * 2, (near(close_context), near(far_context)), 2)
    both = swapped(both, "date", 1)
    home, attended = call(
        home_kernel,
        "home",
        (pltpu.VMEM((slots, rows, width), F32), jax.ShapeDtypeStruct((slots, rows, channels), BF16)),
        [SMEM] + [VMEM] * 5,
        (ids, near(stay), near(close), near(context), near(both), near(far_context)),
        6,
        scratch=(pltpu.VMEM((groups, slots, rows, part), BF16),),
    )
    grad_tokens, grad_norm = call(
        finish_kernel,
        "finish",
        (
            jax.ShapeDtypeStruct((slots, rows, width), BF16),
            jax.ShapeDtypeStruct((2, width), F32),
        ),
        [SMEM] * 2 + [VMEM] * 7,
        (ids, live, near(own_unit), near(own_inv), gain2, near(home), near(far), total, far_total),
        6,
    )
    return attended, grad_tokens, grad_norm


def solution(mesh):
    in_specs = (
        P(("rep", "tile"), "date", None),
        P(("rep", "tile"), "date", None),
        P(("rep", "tile"), None),
        P(("rep", "tile")),
        P("rep"),
        P(),
        P(),
        P(),
        P("tile", None),
    )
    out_specs = (P(("rep", "tile"), "date", None), P(("rep", "tile"), "date", None), P("rep", None))
    return jax.shard_map(local, mesh=mesh, in_specs=in_specs, out_specs=out_specs, check_vma=False)
```

```python
import functools

import jax
import jax.numpy as jnp
from jax import lax
from jax.experimental import pallas as pl
from jax.experimental.pallas import tpu as pltpu
from jax.sharding import PartitionSpec as P

HEAD_DIM = 80
DG = 32
BLOCK_ROWS = 32
F32 = jnp.float32
BF16 = jnp.bfloat16

VMEM = pl.BlockSpec(memory_space=pltpu.VMEM)
SMEM = pl.BlockSpec(memory_space=pltpu.SMEM)
HBM = pl.BlockSpec(memory_space=pltpu.HBM)


def dot(a, b):
    return jnp.dot(a, b, preferred_element_type=F32)


def dot_nt(a, b):
    return lax.dot_general(a, b, (((1,), (1,)), ((), ())), preferred_element_type=F32)


def dot_tn(a, b):
    return lax.dot_general(a, b, (((0,), (0,)), ((), ())), preferred_element_type=F32)


def window_of(group, part):
    wide = -(-part // 128) * 128
    odd = lax.rem(group, 2)
    start = (group // 2) * (2 * part) + odd * (2 * part - wide)
    return start, wide, odd == 1


def pick_kernel(part, other, ids_ref, w_ref, *refs):
    out_refs, windows, sems = refs[:-2], refs[-2], refs[-1]
    height = windows.shape[1]
    channels = w_ref.shape[1] // 3
    half = 1 - ids_ref[0] if other else ids_ref[0]
    first = pl.multiple_of(half * height, 16)
    start, wide, odd = window_of(ids_ref[1], part)
    moves = [
        pltpu.make_async_copy(
            w_ref.at[pl.ds(first, height), pl.ds(pl.multiple_of(i * channels + start, 128), wide)],
            windows.at[i],
            sems.at[i],
        )
        for i in range(3)
    ]
    for move in moves:
        move.start()
    for move in moves:
        move.wait()
    pieces = []
    for i in range(3):
        window = windows[i]
        pieces.append(jnp.where(odd, window[:, wide - part :], window[:, :part]))
    picked = jnp.concatenate(pieces, axis=1)
    at = 0
    for out_ref in out_refs:
        out_ref[...] = picked[at : at + out_ref.shape[0]]
        at += out_ref.shape[0]


def chip_pair(ids_ref, part):
    pair = ids_ref[1] // 2
    return pl.multiple_of(pair * (2 * part), 128), pl.multiple_of((1 - pair) * (2 * part), 128)


def pack_across_kernel(part, ids_ref, tokens_ref, cotangent_ref, out_ref):
    width = tokens_ref.shape[2]
    theirs = chip_pair(ids_ref, part)[1]
    out_ref[:, :, :width] = tokens_ref[...]
    out_ref[:, :, width:] = cotangent_ref[:, :, pl.ds(theirs, 2 * part)]


def pack_beside_kernel(part, ids_ref, tokens_ref, cotangent_ref, across_ref, out_ref, up_ref):
    width = tokens_ref.shape[2]
    ours = chip_pair(ids_ref, part)[0]
    odd = lax.rem(ids_ref[1], 2) == 1
    out_ref[:, :, :width] = tokens_ref[...]
    out_ref[:, :, width : 2 * width] = across_ref[:, :, :width]
    theirs = []
    for i, block in enumerate((cotangent_ref[:, :, pl.ds(ours, 2 * part)], across_ref[:, :, width:])):
        low, high = block[:, :, :part], block[:, :, part:]
        up_ref[i] = jnp.where(odd, high, low)
        theirs.append(jnp.where(odd, low, high))
    out_ref[:, :, 2 * width :] = jnp.concatenate(theirs, axis=2)


def norm_kernel(visible_ref, pos_ref, gain_ref, bias_ref, tokens_ref, across_ref, beside_ref, *refs):
    normed_ref, unit_ref, own_unit_ref, own_inv_ref = refs
    slots, rows, width = tokens_ref.shape
    gain = gain_ref[...]
    bias = bias_ref[...]
    for p in range(slots):
        iota = lax.broadcasted_iota(jnp.int32, (8, pos_ref.shape[0]), 1)
        onehot = (iota == visible_ref[p]).astype(F32).astype(BF16)
        position = dot(onehot, pos_ref[...])[0:1]
        groups = (
            tokens_ref[p],
            beside_ref[p, :, :width],
            across_ref[p, :, :width],
            beside_ref[p, :, width : 2 * width],
        )
        for s, tokens in enumerate(groups):
            embedded = (tokens.astype(F32) + position).astype(BF16).astype(F32)
            centred = embedded - jnp.mean(embedded, axis=-1, keepdims=True)
            inv_std = lax.rsqrt(jnp.mean(centred * centred, axis=-1, keepdims=True) + 1e-06)
            unit = centred * inv_std
            at = (p * len(groups) + s) * rows
            normed_ref[at : at + rows] = (unit * gain + bias).astype(BF16)
            unit_ref[at : at + rows] = unit.astype(BF16)
            if s == 0:
                own_unit_ref[p] = unit
                own_inv_ref[p] = jnp.broadcast_to(inv_std, own_inv_ref.shape[1:])


def put_pieces(ids_ref, depth, offset, steps, piece_refs, weights):
    owners = 4
    rep, owner = ids_ref[0], ids_ref[2]
    share = depth // 2
    spot = owner ^ (owner >> 1)
    for i, ref in enumerate(piece_refs):
        back = lax.rem(spot + owners - steps[i // 2], owners)
        half = 1 - rep if i % 2 else rep
        first = (back ^ (back >> 1)) * depth + half * share + offset
        weights[pl.ds(pl.multiple_of(first, 16), ref.shape[0]), :] = ref[...]


def place_kernel(depth, ids_ref, low_ref, high_ref, rest_ref, *refs):
    weights = refs[-1]
    rep, own = ids_ref[0], ids_ref[2] * depth
    share = depth // 2
    low = pl.multiple_of(own + rep * share, 16)
    weights[pl.ds(low, low_ref.shape[0]), :] = low_ref[...]
    high = pl.multiple_of(own + rep * share + low_ref.shape[0], 16)
    weights[pl.ds(high, high_ref.shape[0]), :] = high_ref[...]
    rest = pl.multiple_of(own + (1 - rep) * share, 16)
    weights[pl.ds(rest, rest_ref.shape[0]), :] = rest_ref[...]
    put_pieces(ids_ref, depth, 0, (1, 2, 3), refs[:6], weights)
    put_pieces(ids_ref, depth, depth // 4, (1, 2), refs[6:-1], weights)


def attend_kernel(
    count, depth, ids_ref, live_ref, _, normed_ref, valid_ref, up_ref, beside_ref, *refs
):
    piece_refs = refs[:count]
    own_ref, close_ref, across_ref, gqkv_ref, weights, qkv_ref = refs[count:]
    _, slots, rows, channels = up_ref.shape
    dates = valid_ref.shape[1]
    heads = channels // HEAD_DIM
    inv_scale = 1.0 / HEAD_DIM**0.5
    if count:
        put_pieces(ids_ref, depth, depth // 4, (3,), piece_refs, weights)
    qkv_ref[...] = dot(normed_ref[...], weights[...]).astype(BF16)
    row = lax.broadcasted_iota(jnp.int32, (dates, dates), 0)
    column = lax.broadcasted_iota(jnp.int32, (dates, dates), 1)
    same_date = column == (row ^ (ids_ref[1] * rows))
    for p in range(slots):
        span = slice(p * dates, (p + 1) * dates)
        alive = (live_ref[ids_ref[2]] > p // (BLOCK_ROWS // DG)).astype(F32)
        rows_qkv = qkv_ref[span, :]
        others = beside_ref[p, :, beside_ref.shape[2] - 2 * channels :]
        upstream = [up_ref[0, p], others[:, :channels], up_ref[1, p], others[:, channels:]]
        upstream = jnp.concatenate(upstream, axis=0) * alive.astype(BF16)
        valid = valid_ref[p : p + 1, :].astype(F32)
        allowed = jnp.sum(jnp.where(same_date, valid, 0.0), axis=1, keepdims=True) > 0
        grads = [[], [], []]
        contexts = []
        for h in range(heads):
            q, k, v = (
                rows_qkv[:, i * channels + h * HEAD_DIM : i * channels + (h + 1) * HEAD_DIM]
                for i in range(3)
            )
            up = upstream[:, h * HEAD_DIM : (h + 1) * HEAD_DIM]
            scores = jnp.where(allowed, dot_nt(k, q) * inv_scale, -1e30)
            exps = jnp.exp(scores - jnp.max(scores, axis=0, keepdims=True))
            probs = exps * (1.0 / jnp.sum(exps, axis=0, keepdims=True))
            low = probs.astype(BF16)
            contexts.append(dot_tn(low, v) * alive)
            grads[2].append(dot(low, up))
            gprobs = dot_nt(v, up)
            gscores = probs * (gprobs - jnp.sum(probs * gprobs, axis=0, keepdims=True)) * inv_scale
            glow = gscores.astype(BF16)
            grads[0].append(dot_tn(glow, k))
            grads[1].append(dot(glow, q))
        gqkv_ref[span, :] = jnp.concatenate(grads[0] + grads[1] + grads[2], axis=1).astype(BF16)
        context = jnp.concatenate(contexts, axis=1).astype(BF16)
        for s, out in enumerate((own_ref, close_ref, across_ref.at[0], across_ref.at[1])):
            out[p] = context[s * rows : (s + 1) * rows]


def back_kernel(gqkv_ref, unit_ref, weights, stay_ref, pass_ref, cross_ref, sums_ref):
    slots, rows, width = stay_ref.shape
    dates = gqkv_ref.shape[0] // slots
    tail = 2 * slots * rows
    step = 256
    for n in range(width // step):
        lanes = slice(n * step, (n + 1) * step)
        partial = dot_nt(gqkv_ref[...], weights[lanes, :])
        low = partial.astype(BF16)
        for p in range(slots):
            for s in range(dates // rows):
                block = low[p * dates + s * rows : p * dates + (s + 1) * rows]
                if s % 2:
                    at = (s // 2 * slots + p) * rows
                    cross_ref[at : at + rows, lanes] = block
                else:
                    (pass_ref if s else stay_ref)[p, :, lanes] = block
        gain_sum = jnp.sum(partial * unit_ref[:, lanes].astype(F32), axis=0, keepdims=True)
        sums = jnp.concatenate([gain_sum, jnp.sum(partial, axis=0, keepdims=True)], axis=0)
        sums_ref[:, lanes] = sums
        high = sums.astype(BF16)
        rest = (sums - high.astype(F32)).astype(BF16)
        fill = jnp.zeros((cross_ref.shape[0] - tail - 4, step), BF16)
        cross_ref[tail:, lanes] = jnp.concatenate([high, rest, fill], axis=0)


def merge_kernel(pass_ref, close_ref, sums_ref, out_ref, total_ref):
    slots, rows, width = out_ref.shape
    for p in range(slots):
        at = (slots + p) * rows
        out_ref[p] = (pass_ref[p].astype(F32) + close_ref[at : at + rows].astype(F32)).astype(BF16)
    sums = close_ref[2 * slots * rows :].astype(F32)
    total_ref[...] = sums_ref[...] + sums[0:2] + sums[2:4]


def both_kernel(close_ref, far_ref, both_ref):
    both_ref[0] = close_ref[...]
    both_ref[1] = far_ref[1]


def add_kernel(*refs):
    total = refs[0][...]
    for ref in refs[1:-1]:
        total = total + ref[...]
    refs[-1][...] = total


def home_kernel(ids_ref, stay_ref, close_ref, own_ref, beside_ref, across_ref, grad_ref, attended_ref, held):
    slots, rows, width = grad_ref.shape
    group = ids_ref[1]
    held[group] = own_ref[...]
    held[group ^ 1] = beside_ref[0]
    held[group ^ 2] = across_ref[0]
    held[group ^ 3] = beside_ref[1]
    for p in range(slots):
        close = close_ref[p * rows : (p + 1) * rows].astype(F32)
        grad_ref[p] = stay_ref[p].astype(F32) + close
        attended_ref[p] = jnp.concatenate([held[g, p] for g in range(held.shape[0])], axis=1)


def finish_kernel(ids_ref, live_ref, unit_ref, inv_ref, gain_ref, grad_ref, far_ref, *refs):
    out_ref, norm_ref = refs[-2:]
    slots = unit_ref.shape[0]
    gain = gain_ref[...]
    for p in range(slots):
        alive = (live_ref[ids_ref[2]] > p // (BLOCK_ROWS // DG)).astype(F32)
        unit = unit_ref[p]
        scaled = (grad_ref[p] + far_ref[p].astype(F32)) * gain
        out = inv_ref[p][:, 0:1] * (
            scaled
            - jnp.mean(scaled, axis=-1, keepdims=True)
            - unit * jnp.mean(scaled * unit, axis=-1, keepdims=True)
        )
        out_ref[p] = (out * alive).astype(BF16)
    total = refs[0][...]
    for ref in refs[1:-2]:
        total = total + ref[...]
    norm_ref[...] = total


def swapped(array, axis, bits):
    return lax.ppermute(array, axis, [(i, i ^ bits) for i in range(lax.axis_size(axis))])


def after(array, *others):
    return lax.optimization_barrier((array, *others))[0]


def near(array):
    return pltpu.with_memory_space_constraint(array, pltpu.VMEM)


def call(kernel, name, out_shape, in_specs, args, megabytes, scratch=(), microseconds=0.01, aliases=()):
    return pl.pallas_call(
        kernel,
        out_shape=out_shape,
        in_specs=in_specs,
        out_specs=jax.tree.map(lambda _: VMEM, out_shape),
        scratch_shapes=list(scratch),
        input_output_aliases=dict(aliases),
        compiler_params=pltpu.CompilerParams(vmem_limit_bytes=megabytes * 1024 * 1024),
        cost_estimate=pl.CostEstimate(
            flops=int(microseconds * 10**9), bytes_accessed=1000, transcendentals=0
        ),
        name=name,
    )(*args)


def pick(w_qkv, ids, share, part, other):
    wide = -(-part // 128) * 128
    return call(
        functools.partial(pick_kernel, part, other),
        "pick",
        (pltpu.VMEM((share, 3 * part), BF16),)
        if other
        else (pltpu.VMEM((share // 2, 3 * part), BF16),) * 2,
        [SMEM, HBM],
        (ids, pltpu.with_memory_space_constraint(w_qkv, pltpu.HBM)),
        4,
        scratch=(pltpu.VMEM((3, share, wide), BF16), pltpu.SemaphoreType.DMA((3,))),
    )


def local(tokens, cotangent, valid, visible, live, pos_table, norm_gain, norm_bias, w_qkv):
    slots, rows, width = tokens.shape
    groups = lax.axis_size("date")
    owners = lax.axis_size("tile")
    depth, triple = w_qkv.shape
    channels = triple // 3
    part = channels // groups
    dates = rows * groups
    ids = jnp.stack([lax.axis_index(name) for name in ("rep", "date", "tile")]).astype(jnp.int32)
    gain2, bias2 = norm_gain.reshape(1, width), norm_bias.reshape(1, width)

    chain = owners == 4 and lax.axis_size("rep") == 2 and depth % 64 == 0
    ring = [(0, 1), (1, 3), (3, 2), (2, 0)]
    share = depth // 2
    if chain:
        low, high = pick(w_qkv, ids, share, part, False)
        chains = []
        for held in (low, high):
            first = lax.ppermute(held, "tile", ring)
            if chains:
                (rest,) = pick(w_qkv, after(ids, held), share, part, True)
                first = after(first, rest)
            second = lax.ppermute(first, "tile", ring)
            first_other = swapped(first, "rep", 1)
            third = lax.ppermute(second, "tile", ring)
            second_other = swapped(after(second, first_other), "rep", 1)
            third_other = swapped(third, "rep", 1)
            chains.append((first, first_other, second, second_other, third, third_other))
        first, later = chains[1][0], (chains[1][2], chains[0][3])
    else:
        first, later = ids, ()

    across = call(
        functools.partial(pack_across_kernel, part),
        "pack_across",
        pltpu.VMEM((slots, rows, width + 2 * part), BF16),
        [SMEM, VMEM, VMEM],
        (after(ids, first), tokens, cotangent),
        6,
    )
    across = swapped(across, "date", 2)
    pair = pltpu.VMEM((2, slots, rows, part), BF16)
    beside, ups = call(
        functools.partial(pack_beside_kernel, part),
        "pack_beside",
        (pltpu.VMEM((slots, rows, 2 * width + 2 * part), BF16), pair),
        [SMEM, VMEM, VMEM, VMEM],
        (after(ids, *later), tokens, cotangent, near(across)),
        6,
    )
    beside = swapped(beside, "date", 1)

    normed, unit, own_unit, own_inv = call(
        norm_kernel,
        "norm",
        (
            pltpu.VMEM((slots * dates, width), BF16),
            pltpu.VMEM((slots * dates, width), BF16),
            pltpu.VMEM((slots, rows, width), F32),
            pltpu.VMEM((slots, rows, 128), F32),
        ),
        [SMEM] + [VMEM] * 6,
        (visible, pos_table, gain2, bias2, tokens, near(across), near(beside)),
        12,
        microseconds=2,
    )
    whole = pltpu.VMEM((width, 3 * part), BF16)
    if chain:
        own = [near(piece) for piece in (low, high, rest)]
        pieces = [near(piece) for piece in chains[0] + chains[1][:4]]
        weights = call(
            functools.partial(place_kernel, depth),
            "place",
            whole,
            [SMEM] + [VMEM] * (len(own) + len(pieces)),
            (ids, *own, *pieces),
            4,
            microseconds=8,
        )
        pieces = [near(piece) for piece in chains[1][4:]]
    else:
        group = lax.axis_index("date")
        mine = [
            lax.dynamic_slice_in_dim(w_qkv, i * channels + group * part, part, 1) for i in range(3)
        ]
        weights = lax.all_gather(jnp.concatenate(mine, axis=1), "tile", axis=0, tiled=True)
        pieces = []

    piece = pltpu.VMEM((slots, rows, part), BF16)
    context, close_context, far_context, gqkv, weights = call(
        functools.partial(attend_kernel, len(pieces), depth),
        "attend",
        (
            piece,
            piece,
            pair,
            pltpu.VMEM((slots * dates, 3 * part), BF16),
            whole,
        ),
        [SMEM] * 2 + [VMEM] * (5 + len(pieces)),
        (ids, live, near(weights), near(normed), valid, near(ups), near(beside), *pieces),
        20,
        aliases=((2, 4),),
        scratch=(pltpu.VMEM((slots * dates, 3 * part), BF16),),
    )
    far_context = swapped(far_context, "date", 2)

    block = pltpu.VMEM((slots, rows, width), BF16)
    pairs = pltpu.VMEM((2, width), F32)
    stay, passing, cross, sums = call(
        back_kernel,
        "back",
        (block, block, pltpu.VMEM((2 * slots * rows + 16, width), BF16), pairs),
        [VMEM] * 3,
        (near(gqkv), near(unit), near(weights)),
        12,
    )

    close = swapped(cross, "date", 1)
    chip, total = call(
        merge_kernel,
        "merge",
        (block, pairs),
        [VMEM] * 3,
        (near(passing), near(close), near(sums)),
        6,
    )
    far = swapped(chip, "date", 2)
    if owners == 4:
        total = call(
            add_kernel,
            "add",
            pairs,
            [VMEM] * owners,
            [near(total)] + [near(swapped(total, "tile", s)) for s in range(1, owners)],
            2,
        )
    else:
        total = lax.psum(total, "tile")
    far_total = swapped(total, "date", 2)
    far_context = after(far_context, total)
    both = call(both_kernel, "both", pair, [VMEM] * 2, (near(close_context), near(far_context)), 2)
    both = swapped(both, "date", 1)
    home, attended = call(
        home_kernel,
        "home",
        (pltpu.VMEM((slots, rows, width), F32), jax.ShapeDtypeStruct((slots, rows, channels), BF16)),
        [SMEM] + [VMEM] * 5,
        (ids, near(stay), near(close), near(context), near(both), near(far_context)),
        6,
        scratch=(pltpu.VMEM((groups, slots, rows, part), BF16),),
    )
    grad_tokens, grad_norm = call(
        finish_kernel,
        "finish",
        (
            jax.ShapeDtypeStruct((slots, rows, width), BF16),
            jax.ShapeDtypeStruct((2, width), F32),
        ),
        [SMEM] * 2 + [VMEM] * 7,
        (ids, live, near(own_unit), near(own_inv), gain2, near(home), near(far), total, far_total),
        6,
    )
    return attended, grad_tokens, grad_norm


def solution(mesh):
    in_specs = (
        P(("rep", "tile"), "date", None),
        P(("rep", "tile"), "date", None),
        P(("rep", "tile"), None),
        P(("rep", "tile")),
        P("rep"),
        P(),
        P(),
        P(),
        P("tile", None),
    )
    out_specs = (P(("rep", "tile"), "date", None), P(("rep", "tile"), "date", None), P("rep", None))
    return jax.shard_map(local, mesh=mesh, in_specs=in_specs, out_specs=out_specs, check_vma=False)
```

```python
import functools

import jax
import jax.numpy as jnp
from jax import lax
from jax.experimental import pallas as pl
from jax.experimental.pallas import tpu as pltpu
from jax.sharding import PartitionSpec as P

HEAD_DIM = 80
DG = 32
BLOCK_ROWS = 32
F32 = jnp.float32
BF16 = jnp.bfloat16

VMEM = pl.BlockSpec(memory_space=pltpu.VMEM)
SMEM = pl.BlockSpec(memory_space=pltpu.SMEM)
HBM = pl.BlockSpec(memory_space=pltpu.HBM)


def dot(a, b):
    return jnp.dot(a, b, preferred_element_type=F32)


def dot_nt(a, b):
    return lax.dot_general(a, b, (((1,), (1,)), ((), ())), preferred_element_type=F32)


def dot_tn(a, b):
    return lax.dot_general(a, b, (((0,), (0,)), ((), ())), preferred_element_type=F32)


def window_of(group, part):
    wide = -(-part // 128) * 128
    odd = lax.rem(group, 2)
    start = (group // 2) * (2 * part) + odd * (2 * part - wide)
    return start, wide, odd == 1


def pick_kernel(part, other, ids_ref, w_ref, *refs):
    out_refs, windows, sems = refs[:-2], refs[-2], refs[-1]
    height = windows.shape[1]
    channels = w_ref.shape[1] // 3
    half = 1 - ids_ref[0] if other else ids_ref[0]
    first = pl.multiple_of(half * height, 16)
    start, wide, odd = window_of(ids_ref[1], part)
    moves = [
        pltpu.make_async_copy(
            w_ref.at[pl.ds(first, height), pl.ds(pl.multiple_of(i * channels + start, 128), wide)],
            windows.at[i],
            sems.at[i],
        )
        for i in range(3)
    ]
    for move in moves:
        move.start()
    for move in moves:
        move.wait()
    pieces = []
    for i in range(3):
        window = windows[i]
        pieces.append(jnp.where(odd, window[:, wide - part :], window[:, :part]))
    picked = jnp.concatenate(pieces, axis=1)
    at = 0
    for out_ref in out_refs:
        out_ref[...] = picked[at : at + out_ref.shape[0]]
        at += out_ref.shape[0]


def chip_pair(ids_ref, part):
    pair = ids_ref[1] // 2
    return pl.multiple_of(pair * (2 * part), 128), pl.multiple_of((1 - pair) * (2 * part), 128)


def pack_across_kernel(part, ids_ref, tokens_ref, cotangent_ref, out_ref):
    width = tokens_ref.shape[2]
    theirs = chip_pair(ids_ref, part)[1]
    out_ref[:, :, :width] = tokens_ref[...]
    out_ref[:, :, width:] = cotangent_ref[:, :, pl.ds(theirs, 2 * part)]


def pack_beside_kernel(part, ids_ref, tokens_ref, cotangent_ref, across_ref, out_ref, up_ref):
    width = tokens_ref.shape[2]
    ours = chip_pair(ids_ref, part)[0]
    odd = lax.rem(ids_ref[1], 2) == 1
    out_ref[:, :, :width] = tokens_ref[...]
    out_ref[:, :, width : 2 * width] = across_ref[:, :, :width]
    theirs = []
    for i, block in enumerate((cotangent_ref[:, :, pl.ds(ours, 2 * part)], across_ref[:, :, width:])):
        low, high = block[:, :, :part], block[:, :, part:]
        up_ref[i] = jnp.where(odd, high, low)
        theirs.append(jnp.where(odd, low, high))
    out_ref[:, :, 2 * width :] = jnp.concatenate(theirs, axis=2)


def norm_kernel(visible_ref, pos_ref, gain_ref, bias_ref, tokens_ref, across_ref, beside_ref, *refs):
    normed_ref, unit_ref, own_unit_ref, own_inv_ref = refs
    slots, rows, width = tokens_ref.shape
    gain = gain_ref[...]
    bias = bias_ref[...]
    for p in range(slots):
        iota = lax.broadcasted_iota(jnp.int32, (8, pos_ref.shape[0]), 1)
        onehot = (iota == visible_ref[p]).astype(F32).astype(BF16)
        position = dot(onehot, pos_ref[...])[0:1]
        groups = (
            tokens_ref[p],
            beside_ref[p, :, :width],
            across_ref[p, :, :width],
            beside_ref[p, :, width : 2 * width],
        )
        for s, tokens in enumerate(groups):
            embedded = (tokens.astype(F32) + position).astype(BF16).astype(F32)
            centred = embedded - jnp.mean(embedded, axis=-1, keepdims=True)
            inv_std = lax.rsqrt(jnp.mean(centred * centred, axis=-1, keepdims=True) + 1e-06)
            unit = centred * inv_std
            at = (p * len(groups) + s) * rows
            normed_ref[at : at + rows] = (unit * gain + bias).astype(BF16)
            unit_ref[at : at + rows] = unit.astype(BF16)
            if s == 0:
                own_unit_ref[p] = unit
                own_inv_ref[p] = jnp.broadcast_to(inv_std, own_inv_ref.shape[1:])


def put_pieces(ids_ref, depth, offset, steps, piece_refs, weights):
    owners = 4
    rep, owner = ids_ref[0], ids_ref[2]
    share = depth // 2
    spot = owner ^ (owner >> 1)
    for i, ref in enumerate(piece_refs):
        back = lax.rem(spot + owners - steps[i // 2], owners)
        half = 1 - rep if i % 2 else rep
        first = (back ^ (back >> 1)) * depth + half * share + offset
        weights[pl.ds(pl.multiple_of(first, 16), ref.shape[0]), :] = ref[...]


def place_kernel(depth, ids_ref, low_ref, high_ref, rest_ref, *refs):
    weights = refs[-1]
    rep, own = ids_ref[0], ids_ref[2] * depth
    share = depth // 2
    low = pl.multiple_of(own + rep * share, 16)
    weights[pl.ds(low, low_ref.shape[0]), :] = low_ref[...]
    high = pl.multiple_of(own + rep * share + low_ref.shape[0], 16)
    weights[pl.ds(high, high_ref.shape[0]), :] = high_ref[...]
    rest = pl.multiple_of(own + (1 - rep) * share, 16)
    weights[pl.ds(rest, rest_ref.shape[0]), :] = rest_ref[...]
    put_pieces(ids_ref, depth, 0, (1, 2, 3), refs[:6], weights)
    put_pieces(ids_ref, depth, depth // 4, (1, 2), refs[6:-1], weights)


def attend_kernel(
    count, depth, ids_ref, live_ref, _, normed_ref, valid_ref, up_ref, beside_ref, *refs
):
    piece_refs = refs[:count]
    own_ref, close_ref, across_ref, gqkv_ref, weights, qkv_ref = refs[count:]
    _, slots, rows, channels = up_ref.shape
    dates = valid_ref.shape[1]
    heads = channels // HEAD_DIM
    inv_scale = 1.0 / HEAD_DIM**0.5
    if count:
        put_pieces(ids_ref, depth, depth // 4, (3,), piece_refs, weights)
    qkv_ref[...] = dot(normed_ref[...], weights[...]).astype(BF16)
    row = lax.broadcasted_iota(jnp.int32, (dates, dates), 0)
    column = lax.broadcasted_iota(jnp.int32, (dates, dates), 1)
    same_date = column == (row ^ (ids_ref[1] * rows))
    for p in range(slots):
        span = slice(p * dates, (p + 1) * dates)
        alive = (live_ref[ids_ref[2]] > p // (BLOCK_ROWS // DG)).astype(F32)
        rows_qkv = qkv_ref[span, :]
        others = beside_ref[p, :, beside_ref.shape[2] - 2 * channels :]
        upstream = [up_ref[0, p], others[:, :channels], up_ref[1, p], others[:, channels:]]
        upstream = jnp.concatenate(upstream, axis=0) * alive.astype(BF16)
        valid = valid_ref[p : p + 1, :].astype(F32)
        allowed = jnp.sum(jnp.where(same_date, valid, 0.0), axis=1, keepdims=True) > 0
        grads = [[], [], []]
        contexts = []
        for h in range(heads):
            q, k, v = (
                rows_qkv[:, i * channels + h * HEAD_DIM : i * channels + (h + 1) * HEAD_DIM]
                for i in range(3)
            )
            up = upstream[:, h * HEAD_DIM : (h + 1) * HEAD_DIM]
            scores = jnp.where(allowed, dot_nt(k, q) * inv_scale, -1e30)
            exps = jnp.exp(scores - jnp.max(scores, axis=0, keepdims=True))
            probs = exps * (1.0 / jnp.sum(exps, axis=0, keepdims=True))
            low = probs.astype(BF16)
            contexts.append(dot_tn(low, v) * alive)
            grads[2].append(dot(low, up))
            gprobs = dot_nt(v, up)
            gscores = probs * (gprobs - jnp.sum(probs * gprobs, axis=0, keepdims=True)) * inv_scale
            glow = gscores.astype(BF16)
            grads[0].append(dot_tn(glow, k))
            grads[1].append(dot(glow, q))
        gqkv_ref[span, :] = jnp.concatenate(grads[0] + grads[1] + grads[2], axis=1).astype(BF16)
        context = jnp.concatenate(contexts, axis=1).astype(BF16)
        for s, out in enumerate((own_ref, close_ref, across_ref.at[0], across_ref.at[1])):
            out[p] = context[s * rows : (s + 1) * rows]


def back_kernel(gqkv_ref, unit_ref, weights, stay_ref, pass_ref, cross_ref, sums_ref):
    slots, rows, width = stay_ref.shape
    dates = gqkv_ref.shape[0] // slots
    tail = 2 * slots * rows
    step = 256
    for n in range(width // step):
        lanes = slice(n * step, (n + 1) * step)
        partial = dot_nt(gqkv_ref[...], weights[lanes, :])
        low = partial.astype(BF16)
        for p in range(slots):
            for s in range(dates // rows):
                block = low[p * dates + s * rows : p * dates + (s + 1) * rows]
                if s % 2:
                    at = (s // 2 * slots + p) * rows
                    cross_ref[at : at + rows, lanes] = block
                else:
                    (pass_ref if s else stay_ref)[p, :, lanes] = block
        gain_sum = jnp.sum(partial * unit_ref[:, lanes].astype(F32), axis=0, keepdims=True)
        sums = jnp.concatenate([gain_sum, jnp.sum(partial, axis=0, keepdims=True)], axis=0)
        sums_ref[:, lanes] = sums
        high = sums.astype(BF16)
        rest = (sums - high.astype(F32)).astype(BF16)
        fill = jnp.zeros((cross_ref.shape[0] - tail - 4, step), BF16)
        cross_ref[tail:, lanes] = jnp.concatenate([high, rest, fill], axis=0)


def merge_kernel(pass_ref, close_ref, sums_ref, out_ref, total_ref):
    slots, rows, width = out_ref.shape
    for p in range(slots):
        at = (slots + p) * rows
        out_ref[p] = (pass_ref[p].astype(F32) + close_ref[at : at + rows].astype(F32)).astype(BF16)
    sums = close_ref[2 * slots * rows :].astype(F32)
    total_ref[...] = sums_ref[...] + sums[0:2] + sums[2:4]


def both_kernel(close_ref, far_ref, both_ref):
    both_ref[0] = close_ref[...]
    both_ref[1] = far_ref[1]


def add_kernel(*refs):
    total = refs[0][...]
    for ref in refs[1:-1]:
        total = total + ref[...]
    refs[-1][...] = total


def home_kernel(ids_ref, stay_ref, close_ref, own_ref, beside_ref, across_ref, grad_ref, attended_ref, held):
    slots, rows, width = grad_ref.shape
    group = ids_ref[1]
    held[group] = own_ref[...]
    held[group ^ 1] = beside_ref[0]
    held[group ^ 2] = across_ref[0]
    held[group ^ 3] = beside_ref[1]
    for p in range(slots):
        close = close_ref[p * rows : (p + 1) * rows].astype(F32)
        grad_ref[p] = stay_ref[p].astype(F32) + close
        attended_ref[p] = jnp.concatenate([held[g, p] for g in range(held.shape[0])], axis=1)


def finish_kernel(ids_ref, live_ref, unit_ref, inv_ref, gain_ref, grad_ref, far_ref, *refs):
    out_ref, norm_ref = refs[-2:]
    slots = unit_ref.shape[0]
    gain = gain_ref[...]
    for p in range(slots):
        alive = (live_ref[ids_ref[2]] > p // (BLOCK_ROWS // DG)).astype(F32)
        unit = unit_ref[p]
        scaled = (grad_ref[p] + far_ref[p].astype(F32)) * gain
        out = inv_ref[p][:, 0:1] * (
            scaled
            - jnp.mean(scaled, axis=-1, keepdims=True)
            - unit * jnp.mean(scaled * unit, axis=-1, keepdims=True)
        )
        out_ref[p] = (out * alive).astype(BF16)
    total = refs[0][...]
    for ref in refs[1:-2]:
        total = total + ref[...]
    norm_ref[...] = total


def swapped(array, axis, bits):
    return lax.ppermute(array, axis, [(i, i ^ bits) for i in range(lax.axis_size(axis))])


def after(array, *others):
    return lax.optimization_barrier((array, *others))[0]


def near(array):
    return pltpu.with_memory_space_constraint(array, pltpu.VMEM)


def call(kernel, name, out_shape, in_specs, args, megabytes, scratch=(), microseconds=0.01, aliases=()):
    return pl.pallas_call(
        kernel,
        out_shape=out_shape,
        in_specs=in_specs,
        out_specs=jax.tree.map(lambda _: VMEM, out_shape),
        scratch_shapes=list(scratch),
        input_output_aliases=dict(aliases),
        compiler_params=pltpu.CompilerParams(vmem_limit_bytes=megabytes * 1024 * 1024),
        cost_estimate=pl.CostEstimate(
            flops=int(microseconds * 10**9), bytes_accessed=1000, transcendentals=0
        ),
        name=name,
    )(*args)


def pick(w_qkv, ids, share, part, other):
    wide = -(-part // 128) * 128
    return call(
        functools.partial(pick_kernel, part, other),
        "pick",
        (pltpu.VMEM((share, 3 * part), BF16),)
        if other
        else (pltpu.VMEM((share // 2, 3 * part), BF16),) * 2,
        [SMEM, HBM],
        (ids, pltpu.with_memory_space_constraint(w_qkv, pltpu.HBM)),
        4,
        scratch=(pltpu.VMEM((3, share, wide), BF16), pltpu.SemaphoreType.DMA((3,))),
    )


def local(tokens, cotangent, valid, visible, live, pos_table, norm_gain, norm_bias, w_qkv):
    slots, rows, width = tokens.shape
    groups = lax.axis_size("date")
    owners = lax.axis_size("tile")
    depth, triple = w_qkv.shape
    channels = triple // 3
    part = channels // groups
    dates = rows * groups
    ids = jnp.stack([lax.axis_index(name) for name in ("rep", "date", "tile")]).astype(jnp.int32)
    gain2, bias2 = norm_gain.reshape(1, width), norm_bias.reshape(1, width)

    chain = owners == 4 and lax.axis_size("rep") == 2 and depth % 64 == 0
    ring = [(0, 1), (1, 3), (3, 2), (2, 0)]
    share = depth // 2
    if chain:
        low, high = pick(w_qkv, ids, share, part, False)
        chains = []
        for held in (low, high):
            first = lax.ppermute(held, "tile", ring)
            if chains:
                (rest,) = pick(w_qkv, after(ids, held), share, part, True)
                first = after(first, rest)
            second = lax.ppermute(first, "tile", ring)
            first_other = swapped(first, "rep", 1)
            third = lax.ppermute(second, "tile", ring)
            second_other = swapped(second, "rep", 1)
            third_other = swapped(third, "rep", 1)
            chains.append((first, first_other, second, second_other, third, third_other))
        first, later = chains[1][0], (chains[1][2], chains[0][3], chains[0][1], chains[1][1])
    else:
        first, later = ids, ()

    across = call(
        functools.partial(pack_across_kernel, part),
        "pack_across",
        pltpu.VMEM((slots, rows, width + 2 * part), BF16),
        [SMEM, VMEM, VMEM],
        (after(ids, first), tokens, cotangent),
        6,
    )
    across = swapped(across, "date", 2)
    pair = pltpu.VMEM((2, slots, rows, part), BF16)
    beside, ups = call(
        functools.partial(pack_beside_kernel, part),
        "pack_beside",
        (pltpu.VMEM((slots, rows, 2 * width + 2 * part), BF16), pair),
        [SMEM, VMEM, VMEM, VMEM],
        (after(ids, *later), tokens, cotangent, near(across)),
        6,
    )
    beside = swapped(beside, "date", 1)

    normed, unit, own_unit, own_inv = call(
        norm_kernel,
        "norm",
        (
            pltpu.VMEM((slots * dates, width), BF16),
            pltpu.VMEM((slots * dates, width), BF16),
            pltpu.VMEM((slots, rows, width), F32),
            pltpu.VMEM((slots, rows, 128), F32),
        ),
        [SMEM] + [VMEM] * 6,
        (visible, pos_table, gain2, bias2, tokens, near(across), near(beside)),
        12,
        microseconds=2,
    )
    whole = pltpu.VMEM((width, 3 * part), BF16)
    if chain:
        own = [near(piece) for piece in (low, high, rest)]
        pieces = [near(piece) for piece in chains[0] + chains[1][:4]]
        weights = call(
            functools.partial(place_kernel, depth),
            "place",
            whole,
            [SMEM] + [VMEM] * (len(own) + len(pieces)),
            (ids, *own, *pieces),
            4,
            microseconds=8,
        )
        pieces = [near(piece) for piece in chains[1][4:]]
    else:
        group = lax.axis_index("date")
        mine = [
            lax.dynamic_slice_in_dim(w_qkv, i * channels + group * part, part, 1) for i in range(3)
        ]
        weights = lax.all_gather(jnp.concatenate(mine, axis=1), "tile", axis=0, tiled=True)
        pieces = []

    piece = pltpu.VMEM((slots, rows, part), BF16)
    context, close_context, far_context, gqkv, weights = call(
        functools.partial(attend_kernel, len(pieces), depth),
        "attend",
        (
            piece,
            piece,
            pair,
            pltpu.VMEM((slots * dates, 3 * part), BF16),
            whole,
        ),
        [SMEM] * 2 + [VMEM] * (5 + len(pieces)),
        (ids, live, near(weights), near(normed), valid, near(ups), near(beside), *pieces),
        20,
        aliases=((2, 4),),
        scratch=(pltpu.VMEM((slots * dates, 3 * part), BF16),),
    )
    far_context = swapped(far_context, "date", 2)

    block = pltpu.VMEM((slots, rows, width), BF16)
    pairs = pltpu.VMEM((2, width), F32)
    stay, passing, cross, sums = call(
        back_kernel,
        "back",
        (block, block, pltpu.VMEM((2 * slots * rows + 16, width), BF16), pairs),
        [VMEM] * 3,
        (near(gqkv), near(unit), near(weights)),
        12,
    )

    close = swapped(cross, "date", 1)
    chip, total = call(
        merge_kernel,
        "merge",
        (block, pairs),
        [VMEM] * 3,
        (near(passing), near(close), near(sums)),
        6,
    )
    far = swapped(chip, "date", 2)
    if owners == 4:
        total = call(
            add_kernel,
            "add",
            pairs,
            [VMEM] * owners,
            [near(total)] + [near(swapped(total, "tile", s)) for s in range(1, owners)],
            2,
        )
    else:
        total = lax.psum(total, "tile")
    far_total = swapped(total, "date", 2)
    far_context = after(far_context, total)
    both = call(both_kernel, "both", pair, [VMEM] * 2, (near(close_context), near(far_context)), 2)
    both = swapped(both, "date", 1)
    home, attended = call(
        home_kernel,
        "home",
        (pltpu.VMEM((slots, rows, width), F32), jax.ShapeDtypeStruct((slots, rows, channels), BF16)),
        [SMEM] + [VMEM] * 5,
        (ids, near(stay), near(close), near(context), near(both), near(far_context)),
        6,
        scratch=(pltpu.VMEM((groups, slots, rows, part), BF16),),
    )
    grad_tokens, grad_norm = call(
        finish_kernel,
        "finish",
        (
            jax.ShapeDtypeStruct((slots, rows, width), BF16),
            jax.ShapeDtypeStruct((2, width), F32),
        ),
        [SMEM] * 2 + [VMEM] * 7,
        (ids, live, near(own_unit), near(own_inv), gain2, near(home), near(far), total, far_total),
        6,
    )
    return attended, grad_tokens, grad_norm


def solution(mesh):
    in_specs = (
        P(("rep", "tile"), "date", None),
        P(("rep", "tile"), "date", None),
        P(("rep", "tile"), None),
        P(("rep", "tile")),
        P("rep"),
        P(),
        P(),
        P(),
        P("tile", None),
    )
    out_specs = (P(("rep", "tile"), "date", None), P(("rep", "tile"), "date", None), P("rep", None))
    return jax.shard_map(local, mesh=mesh, in_specs=in_specs, out_specs=out_specs, check_vma=False)
```
